256 devices in a mesh: nodes: 64 (over y, z, core), heads: 4 (over x).
Axes of the slice: x: 4, y: 4, z: 8, core: 2. Of those that a mesh axis runs over, the one named last changes fastest.
Arguments:
- node_feats: bfloat16 [16384, 512], P('nodes'), may hold values from -16 to 16
- node_types: int32 [16384], P('nodes'), may hold values from 0 to 4
- queries: bfloat16 [16384, 512], P('nodes', 'heads'), may hold values from -6 to 6
- key_rows: bfloat16 [16384, 512], P('nodes', 'heads'), may hold values from -6 to 6
- value_rows: bfloat16 [16384, 512], P('nodes', 'heads'), may hold values from -6 to 6
- halo_keys: bfloat16 [32768, 512], P('nodes', 'heads'), may hold values from -6 to 6
- halo_values: bfloat16 [32768, 512], P('nodes', 'heads'), may hold values from -6 to 6
- halo_rows: int32 [32768], P('nodes'), may hold values from 0 to 256, as said below
- edge_tiles: int32 [2560, 3], P('nodes'), may hold values from 0 to 14, as said below
- grad_output: bfloat16 [16384, 512], P('nodes', 'heads'), may hold values from -6 to 6
- proj_weight: bfloat16 [3, 5, 512, 512], P(None, None, None, 'heads'), may hold values from -0.25 to 0.25
- rel_weight: bfloat16 [2, 15, 8, 64, 64], P(None, None, 'heads'), may hold values from -0.75 to 0.75
- rel_prior: float32 [15, 8], P(None, 'heads'), may hold values from 0.5 to 2
Outputs:
- grad_feats: bfloat16 [16384, 512], P('nodes', 'heads')
- grad_proj: float32 [512, 3, 5, 512], P('nodes', None, None, 'heads')
- grad_rel: float32 [2, 15, 8, 64, 64], P(None, None, 'heads')
- grad_prior: float32 [15, 8], P(None, 'heads')
The draws below stay inside these ranges and needn't reach their ends.
Inputs may be any that keep to these rules, and one draw needn't show every extreme that they name: `halo_rows`: slab s's halo is 64 blocks of 8 slots, block j holding distinct rows of slab j first and 256 in its empty slots; block s of slab s is empty; one slab t is copied in full: every slab other than t holds 8 distinct rows of t in block t; every other block of another slab holds between 1 and 8 rows. `edge_tiles`: an entry is live when its destination tile is below 4, and is empty with destination 256 // 64, source 0 and relation 0. A source tile below 4 lies among the slab's own rows, the others among its halo slots. Every destination tile has a live entry whose source lies among the own rows. Some slab has every entry live.
All inputs are finite; a program needn't handle non-finite values.
Results may differ from the reference program's by a relative error of at most 0.012.
The reference program's roundings to bfloat16 on the way count: a program that leaves them out, or rounds other values in their place, can miss the bound.
Values may be sent and summed in bfloat16 or wider, within the bound.
No kernel may reach another device: no remote copies, remote signals or barrier semaphores. Data moves between devices by JAX's collectives and lax.ppermute only.
A program may use at most 64 MiB of HBM per device.

```python
import math
import jax
import jax.numpy as jnp
from jax import lax

D = 512
HEADS = 8
HEAD_DIM = 64
TYPES = 5
RELS = 15
TILE = 64
ROWS = 256
CAP = 8
HALO = 512
TILES_DEV = 40
NODES = 16384
N_NODES = 64


def draw_halo_rows(key, part):
    key = jax.random.fold_in(key, 11)
    first, second, third = jax.random.split(key, 3)
    counts = jax.random.randint(first, (N_NODES, N_NODES), 1, CAP + 1)
    target = jax.random.randint(second, (), 0, N_NODES)
    sender = jnp.arange(N_NODES)[:, None]
    owners = jnp.arange(N_NODES)[None, :]
    counts = jnp.where(owners == target, CAP, counts)
    counts = jnp.where(sender == owners, 0, counts)
    scores = jax.random.randint(third, (N_NODES, N_NODES, ROWS), 0, 65536) * ROWS + jnp.arange(ROWS)
    ranked = jnp.argsort(scores, axis=-1)[..., :CAP]
    slot_index = jnp.arange(CAP)
    row_ids = jnp.where(slot_index[None, None, :] < counts[..., None], ranked, ROWS)
    return row_ids.reshape(-1).astype(jnp.int32)


def draw_edge_tiles(key, part):
    key = jax.random.fold_in(key, 23)
    keys_list = jax.random.split(key, 7)
    dest_tiles = ROWS // TILE
    source_tiles = dest_tiles + HALO // TILE
    spread = 1024
    picks = jax.random.randint(keys_list[0], (N_NODES,), 0, spread)
    live_count = dest_tiles + picks * (picks + spread) * (TILES_DEV - dest_tiles) // (2 * spread * spread)
    busiest = jax.random.randint(keys_list[1], (), 0, N_NODES)
    live_count = jnp.where(jnp.arange(N_NODES) == busiest, TILES_DEV, live_count)
    entry = jnp.arange(TILES_DEV)[None, :]
    target = jnp.where(entry < dest_tiles, entry, jax.random.randint(keys_list[2], (N_NODES, TILES_DEV), 0, dest_tiles))
    source = jnp.where(entry < dest_tiles, jax.random.randint(keys_list[3], (N_NODES, TILES_DEV), 0, dest_tiles), jax.random.randint(keys_list[4], (N_NODES, TILES_DEV), 0, source_tiles))
    relation = jax.random.randint(keys_list[5], (N_NODES, TILES_DEV), 0, RELS)
    live_mask = entry < live_count[:, None]
    target = jnp.where(live_mask, target, dest_tiles)
    source = jnp.where(live_mask, source, 0)
    relation = jnp.where(live_mask, relation, 0)
    orders = jax.vmap(lambda sub: jax.random.permutation(sub, TILES_DEV))(jax.random.split(keys_list[6], N_NODES))
    stacked = jnp.stack([target, source, relation], axis=-1)
    shuffled = jnp.take_along_axis(stacked, orders[:, :, None], axis=1)
    return shuffled.reshape(N_NODES * TILES_DEV, 3).astype(jnp.int32)


def place_ends(array, own_key, smallest, high):
    index_at = [jax.random.randint(jax.random.fold_in(own_key, axis), (), 0, length) for axis, length in enumerate(array.shape)]
    longest = array.shape.index(max(array.shape))
    next_to = index_at[:longest] + [(index_at[longest] + 1) % array.shape[longest]] + index_at[longest + 1:]
    return array.at[tuple(index_at)].set(smallest).at[tuple(next_to)].set(high)


def spiked(array, own_key, source, target, blocks, factor):
    owner, partner = [(jnp.arange(array.shape[position]) // (array.shape[position] // blocks)).reshape([-1 if axis == position else 1 for axis in range(array.ndim)]) for position in (source, target)]
    chosen = jax.random.permutation(own_key, blocks)[partner]
    strong = (owner == chosen) | (owner == (partner + blocks // 2) % blocks)
    return jnp.where(strong, factor * array, array)


def steps_of(own_key, shape, shards, least, largest):
    def one(position, blocks):
        draws = jax.random.uniform(jax.random.fold_in(jax.random.fold_in(own_key, 6), position), (blocks,), jnp.float32, least / len(shards), largest / len(shards))
        return jnp.repeat(jnp.exp(draws), shape[position] // blocks).reshape((-1,) + (1,) * (len(shape) - position - 1))

    loudness = one(*shards[0])
    for cut in shards[1:]:
        loudness = loudness * one(*cut)
    return loudness


def normal_values(rng, dims, scale, reach, shards=(), held_as=jnp.bfloat16):
    drawn = jax.random.normal(rng, dims, jnp.float32) * scale
    if len(shards) > 0:
        drawn = steps_of(rng, dims, shards, -0.22, 0.18) * drawn
    return jnp.clip(drawn, min=-reach, max=reach).astype(held_as)


def heavy_noise(stream_key, dims, width, most, cuts, heavy, held_as=jnp.bfloat16):
    values = width * jax.random.normal(stream_key, dims, jnp.float32)
    if cuts:
        values = values * steps_of(stream_key, dims, cuts, -0.22, 0.18)
    return jnp.clip(spiked(values, jax.random.fold_in(stream_key, 3), *heavy), -most, most).astype(held_as)


def setup_inputs(seed: int = 0) -> dict:
    splits = jax.random.split(jax.random.key(seed), 14)
    return {
        "node_feats": heavy_noise(splits[0], (NODES, D), 1.0, 16.0, ((0, 64),), (0, 1, 64, 4.0)),
        "node_types": place_ends(jax.random.randint(splits[1], (NODES,), 0, TYPES), jax.random.fold_in(splits[1], 1), 0, TYPES - 1).astype(jnp.int32),
        "queries": normal_values(splits[2], (NODES, D), 1.0, 6.0, ((0, 64), (1, 4))),
        "key_rows": normal_values(splits[3], (NODES, D), 1.0, 6.0, ((0, 64), (1, 4))),
        "value_rows": normal_values(splits[4], (NODES, D), 1.0, 6.0, ((0, 64), (1, 4))),
        "halo_keys": normal_values(splits[5], (N_NODES * HALO, D), 1.0, 6.0, ((0, 64), (1, 4))),
        "halo_values": normal_values(splits[6], (N_NODES * HALO, D), 1.0, 6.0, ((0, 64), (1, 4))),
        "halo_rows": draw_halo_rows(jax.random.fold_in(splits[13], 71), 0),
        "edge_tiles": draw_edge_tiles(jax.random.fold_in(splits[13], 71), 0),
        "grad_output": normal_values(splits[9], (NODES, D), 1.0, 6.0, ((0, 64), (1, 4))),
        "proj_weight": normal_values(splits[10], (3, TYPES, D, D), D ** -0.5, 0.25, ((3, 4),)),
        "rel_weight": normal_values(splits[11], (2, RELS, HEADS, HEAD_DIM, HEAD_DIM), HEAD_DIM ** -0.5, 0.75, ((2, 4),)),
        "rel_prior": jnp.clip(jnp.exp(math.log(2.0) - 1.3862944 * jax.random.uniform(splits[12], (RELS, HEADS), jnp.float32) ** steps_of(splits[12], (RELS, HEADS), ((1, 4),), -0.2, 0.2)), 0.5, 2.0),
    }


def attend(queries, key_rows, value_rows, valid, grad_output, edge_tiles, rel_weight, rel_prior):
    head_count = queries.shape[1]
    head_dim = queries.shape[2]
    dest_tiles = queries.shape[0] // TILE
    source_tiles = key_rows.shape[0] // TILE
    inv_root = head_dim ** -0.5
    query_tiles = queries.reshape(dest_tiles, TILE, head_count, head_dim).astype(jnp.float32)
    key_tiles = key_rows.reshape(source_tiles, TILE, head_count, head_dim).astype(jnp.float32)
    value_tiles = value_rows.reshape(source_tiles, TILE, head_count, head_dim).astype(jnp.float32)
    grad_tiles = grad_output.reshape(dest_tiles, TILE, head_count, head_dim).astype(jnp.float32)
    target = edge_tiles[:, 0]
    source = edge_tiles[:, 1]
    relation = edge_tiles[:, 2]
    live_mask = (target < dest_tiles).astype(jnp.float32)
    clipped = jnp.minimum(target, dest_tiles - 1)
    query_edge = query_tiles[clipped]
    key_edge = key_tiles[source]
    value_edge = value_tiles[source]
    grad_edge = grad_tiles[clipped]
    columns = valid.reshape(source_tiles, TILE)[source] * live_mask[:, None]
    score_weight = rel_weight[0][relation].astype(jnp.float32)
    message_weight = rel_weight[1][relation].astype(jnp.float32)
    prior_edge = rel_prior[relation]
    key_mixed = jnp.einsum('etha,ehab->ethb', key_edge, score_weight).astype(jnp.bfloat16).astype(jnp.float32)
    message = jnp.einsum('etha,ehab->ethb', value_edge, message_weight).astype(jnp.bfloat16).astype(jnp.float32)
    logits = jnp.einsum('etha,esha->ehts', query_edge, key_mixed) * inv_root
    exp_scores = jnp.exp(logits * prior_edge[:, :, None, None]) * columns[:, None, None, :]
    owner_map = (target[:, None] == jnp.arange(dest_tiles)[None, :]).astype(jnp.float32)
    denominator = jnp.einsum('ed,eht->dht', owner_map, jnp.sum(exp_scores, axis=-1), precision=lax.Precision.HIGHEST)
    softmax = exp_scores / denominator[clipped][..., None]
    prob_bf = softmax.astype(jnp.bfloat16).astype(jnp.float32)
    partial_value = jnp.einsum('ehts,eshb->ethb', prob_bf, message)
    output = jnp.einsum('ed,ethb->dthb', owner_map, partial_value, precision=lax.Precision.HIGHEST)
    deltas = jnp.sum(grad_tiles * output, axis=-1)
    delta_edge = jnp.transpose(deltas[clipped], (0, 2, 1))
    prob_grad = jnp.einsum('ethb,eshb->ehts', grad_edge, message)
    score_grad = softmax * (prob_grad - delta_edge[..., None])
    logit_grad = (score_grad * (prior_edge * inv_root)[:, :, None, None]).astype(jnp.bfloat16).astype(jnp.float32)
    query_edge_grad = jnp.einsum('ehts,esha->etha', logit_grad, key_mixed)
    key_mixed_grad = jnp.einsum('ehts,etha->esha', logit_grad, query_edge).astype(jnp.bfloat16).astype(jnp.float32)
    message_grad = jnp.einsum('ehts,ethb->eshb', prob_bf, grad_edge).astype(jnp.bfloat16).astype(jnp.float32)
    key_edge_grad = jnp.einsum('eshb,ehab->esha', key_mixed_grad, score_weight)
    value_edge_grad = jnp.einsum('eshb,ehab->esha', message_grad, message_weight)
    score_weight_grad = jnp.einsum('esha,eshb->ehab', key_edge, key_mixed_grad)
    message_weight_grad = jnp.einsum('esha,eshb->ehab', value_edge, message_grad)
    prior_edge_grad = jnp.sum(score_grad * logits, axis=(2, 3))
    source_map = (source[:, None] == jnp.arange(source_tiles)[None, :]).astype(jnp.float32) * live_mask[:, None]
    query_grad = jnp.einsum('ed,etha->dtha', owner_map, query_edge_grad, precision=lax.Precision.HIGHEST)
    key_grad = jnp.einsum('ej,esha->jsha', source_map, key_edge_grad, precision=lax.Precision.HIGHEST)
    value_grad = jnp.einsum('ej,esha->jsha', source_map, value_edge_grad, precision=lax.Precision.HIGHEST)
    chooser = (relation[:, None] == jnp.arange(RELS)[None, :]).astype(jnp.float32)
    relation_grad = jnp.stack([
        jnp.einsum('er,ehab->rhab', chooser, score_weight_grad, precision=lax.Precision.HIGHEST),
        jnp.einsum('er,ehab->rhab', chooser, message_weight_grad, precision=lax.Precision.HIGHEST)])
    prior_grad = jnp.einsum('er,eh->rh', chooser, prior_edge_grad, precision=lax.Precision.HIGHEST)
    return (query_grad.reshape(dest_tiles * TILE, head_count, head_dim),
            key_grad.reshape(source_tiles * TILE, head_count, head_dim),
            value_grad.reshape(source_tiles * TILE, head_count, head_dim),
            relation_grad, prior_grad)


def reference(node_feats, node_types, queries, key_rows, value_rows, halo_keys, halo_values, halo_rows, edge_tiles, grad_output, proj_weight, rel_weight, rel_prior):
    head_dim = D // HEADS
    slab_count = N_NODES

    def by_heads(matrix, count):
        return matrix.reshape(slab_count, count, HEADS, head_dim)

    def per_slab(items):
        query_slab, key_slab, value_slab, halo_key_slab, halo_value_slab, halo_slab, tile_slab, grad_slab = items
        valid = jnp.concatenate([jnp.ones((ROWS,), jnp.float32), (halo_slab < ROWS).astype(jnp.float32)])
        return attend(query_slab, jnp.concatenate([key_slab, halo_key_slab]),
                      jnp.concatenate([value_slab, halo_value_slab]), valid, grad_slab,
                      tile_slab, rel_weight, rel_prior)

    query_grad, key_grad, value_grad, relation_grad, prior_grad = lax.map(per_slab, (
        by_heads(queries, ROWS), by_heads(key_rows, ROWS), by_heads(value_rows, ROWS),
        by_heads(halo_keys, HALO), by_heads(halo_values, HALO),
        halo_rows.reshape(slab_count, HALO), edge_tiles.reshape(slab_count, TILES_DEV, 3),
        by_heads(grad_output, ROWS)))
    query_bf = query_grad.reshape(NODES, D).astype(jnp.bfloat16)
    key_own = key_grad[:, :ROWS].reshape(NODES, D).astype(jnp.bfloat16)
    value_own = value_grad[:, :ROWS].reshape(NODES, D).astype(jnp.bfloat16)
    key_halo = key_grad[:, ROWS:].reshape(slab_count * HALO, D).astype(jnp.bfloat16)
    value_halo = value_grad[:, ROWS:].reshape(slab_count * HALO, D).astype(jnp.bfloat16)
    slot_index = jnp.arange(slab_count * HALO).astype(jnp.int32)
    owners = (slot_index % HALO) // CAP
    places = jnp.where(halo_rows < ROWS, owners * ROWS + halo_rows, NODES).astype(jnp.int32)
    key_back = jnp.zeros((NODES, D), jnp.float32).at[places].add(key_halo.astype(jnp.float32), mode="drop")
    value_back = jnp.zeros((NODES, D), jnp.float32).at[places].add(value_halo.astype(jnp.float32), mode="drop")
    gradients = (query_bf.astype(jnp.float32), key_own.astype(jnp.float32) + key_back,
                 value_own.astype(jnp.float32) + value_back)
    feats_wide = node_feats.astype(jnp.float32)
    grad_feats = jnp.zeros((NODES, D), jnp.float32)
    blocks = []
    for proj_index in range(3):
        row_blocks = []
        for type_index in range(TYPES):
            masked = gradients[proj_index] * (node_types == type_index).astype(jnp.float32)[:, None]
            weight_wide = proj_weight[proj_index, type_index].astype(jnp.float32)
            grad_feats = grad_feats + jnp.dot(masked, weight_wide.T, precision=lax.Precision.HIGHEST)
            row_blocks.append(jnp.dot(feats_wide.T, masked, precision=lax.Precision.HIGHEST))
        blocks.append(jnp.stack(row_blocks))
    grad_proj = jnp.transpose(jnp.stack(blocks), (2, 0, 1, 3))
    return grad_feats.astype(jnp.bfloat16), grad_proj, jnp.sum(relation_grad, axis=0), jnp.sum(prior_grad, axis=0)
```

```python
import jax
import jax.numpy as jnp
from jax import lax
from jax.experimental import pallas as pl
from jax.experimental.pallas import tpu as pltpu
from jax.sharding import Mesh, PartitionSpec as P

TYPES = 5
RELS = 15
TILE = 64
WIDE = 128
GROUP = 8
PROJ = 3 * TYPES

F32 = jnp.float32
BF16 = jnp.bfloat16
NN = (((1,), (0,)), ((), ()))
NT = (((1,), (1,)), ((), ()))
TN = (((0,), (0,)), ((), ()))
VMEM = pl.BlockSpec(memory_space=pltpu.VMEM)
SMEM = pl.BlockSpec(memory_space=pltpu.SMEM)


def mul(left, right, dims):
    return lax.dot_general(left, right, dims, preferred_element_type=F32)


def column(row):
    return jnp.transpose(jnp.broadcast_to(row, (WIDE, WIDE)), (1, 0))


def attend_kernel(
    edges, q_ref, ko_ref, vo_ref, kh_ref, vh_ref, g_ref, rows_ref, rel_ref, prior_ref,
    own_out, send_out, rel_out,
    wbd, qg, kv, keep, prior, kvm, probs, exps, logs, grads,
    denom, delta, dprior, dkv, dwk, dwv, dq,
):
    count = edges.shape[1]
    dests = q_ref.shape[0] // TILE
    own_tiles = ko_ref.shape[0] // TILE
    halo_tiles = kh_ref.shape[0] // TILE
    lane = lax.broadcasted_iota(jnp.int32, (TILE, WIDE), 1)
    first = lane < TILE

    wbd[...] = jnp.zeros_like(wbd)
    for r in range(RELS):
        for w in range(2):
            for h in range(2):
                at = (2 * w + h) * TILE
                wbd[r, at : at + TILE, at : at + TILE] = rel_ref[w, r, h]
    none = jnp.zeros((TILE, WIDE), BF16)
    for a in range(dests):
        q = (q_ref[a * TILE : (a + 1) * TILE, :].astype(F32) * 0.125).astype(F32)
        g = g_ref[a * TILE : (a + 1) * TILE, :].astype(F32)
        for h in range(2):
            mine = first if h == 0 else jnp.logical_not(first)
            qg[a, h * TILE : (h + 1) * TILE, :WIDE] = jnp.where(mine, q, 0.0).astype(BF16)
            qg[a, h * TILE : (h + 1) * TILE, WIDE:] = none
            qg[a, (2 + h) * TILE : (3 + h) * TILE, :WIDE] = none
            qg[a, (2 + h) * TILE : (3 + h) * TILE, WIDE:] = jnp.where(mine, g, 0.0).astype(BF16)
    for b in range(own_tiles):
        kv[b, :, :WIDE] = ko_ref[b * TILE : (b + 1) * TILE, :]
        kv[b, :, WIDE:] = vo_ref[b * TILE : (b + 1) * TILE, :]
        keep[b] = jnp.ones((TILE, WIDE), F32)
    for b in range(halo_tiles):
        kv[own_tiles + b, :, :WIDE] = kh_ref[b * TILE : (b + 1) * TILE, :]
        kv[own_tiles + b, :, WIDE:] = vh_ref[b * TILE : (b + 1) * TILE, :]
    for j in range(halo_tiles // 2):
        ids = column(rows_ref[j : j + 1, :].astype(F32))
        send_out[j * WIDE : (j + 1) * WIDE, 2 * WIDE :] = ids.astype(BF16)
        ok = (ids < float(q_ref.shape[0])).astype(F32)
        keep[own_tiles + 2 * j] = ok[:TILE]
        keep[own_tiles + 2 * j + 1] = ok[TILE:]
    wide_first = lax.broadcasted_iota(jnp.int32, (RELS, WIDE), 1) < TILE
    prior[:RELS, :] = jnp.where(wide_first, prior_ref[:, 0:1], prior_ref[:, 1:2])

    denom[...] = jnp.zeros_like(denom)
    delta[...] = jnp.zeros_like(delta)
    dprior[...] = jnp.zeros_like(dprior)
    dkv[...] = jnp.zeros_like(dkv)
    dwk[...] = jnp.zeros_like(dwk)
    dwv[...] = jnp.zeros_like(dwv)
    dq[...] = jnp.zeros_like(dq)

    def entry(e):
        target = edges[0, e]
        return jnp.minimum(target, dests - 1), edges[1, e], edges[2, e], target < dests

    def scores(step, carry):
        for u in range(GROUP):
            e = step * GROUP + u
            a, b, r, live = entry(e)
            mixed = mul(kv[b], wbd[r], NN).astype(BF16)
            kvm[e] = mixed
            both = mul(mixed, qg[a], NT)
            logits = both[:, :WIDE]
            logs[e] = logits
            grads[e] = both[:, WIDE:]
            ex = jnp.exp(prior[pl.ds(r, 1), :] * logits) * (keep[b] * live.astype(F32))
            exps[e] = ex
            denom[a] += jnp.sum(ex, axis=0, keepdims=True)
        return carry

    lax.fori_loop(0, count // GROUP, scores, 0)
    denom[...] = 1.0 / denom[...]

    def normalise(step, carry):
        for u in range(GROUP):
            e = step * GROUP + u
            a, b, r, live = entry(e)
            soft = exps[e] * denom[a]
            exps[e] = soft
            prob = soft.astype(BF16)
            probs[e] = prob
            delta[a] += jnp.sum(prob.astype(F32) * grads[e], axis=0, keepdims=True)
        return carry

    lax.fori_loop(0, count // GROUP, normalise, 0)

    def backward(step, carry):
        for u in range(GROUP):
            e = step * GROUP + u
            a, b, r, live = entry(e)
            score_grad = exps[e] * (grads[e] - delta[a])
            dprior[pl.ds(r, 1), :] += jnp.sum(score_grad * logs[e], axis=0, keepdims=True)
            lgrad = (score_grad * prior[pl.ds(r, 1), :]).astype(BF16)
            pair = jnp.concatenate([lgrad, probs[e]], axis=1)
            mixed_grad = mul(pair, qg[a], NN).astype(BF16)
            dkv[b] += mul(mixed_grad, wbd[r], NT)
            dwk[r] += mul(kv[b, :, :WIDE], mixed_grad[:, :WIDE], TN)
            dwv[r] += mul(kv[b, :, WIDE:], mixed_grad[:, WIDE:], TN)
            dq[a] += mul(lgrad, kvm[e, :, :WIDE], TN)
        return carry

    lax.fori_loop(0, count // GROUP, backward, 0)

    for a in range(dests):
        grad = jnp.where(first, dq[a, :TILE, :], dq[a, TILE:, :]) * 0.125
        own_out[a * TILE : (a + 1) * TILE, :WIDE] = grad.astype(BF16)
    for b in range(own_tiles):
        own_out[b * TILE : (b + 1) * TILE, WIDE:] = dkv[b].astype(BF16)
    for b in range(halo_tiles):
        send_out[b * TILE : (b + 1) * TILE, : 2 * WIDE] = dkv[own_tiles + b].astype(BF16)
    for w, ref in enumerate((dwk, dwv)):
        for r in range(RELS):
            at = (w * RELS + r) * TILE
            rel_out[at : at + TILE, :] = jnp.where(first, ref[r, :TILE, :], ref[r, TILE:, :]).astype(BF16)
    at = 2 * RELS * TILE
    sums = dprior[...]
    left = lax.broadcasted_iota(jnp.int32, sums.shape, 1) < TILE
    one = jnp.sum(jnp.where(left, sums, 0.0), axis=1, keepdims=True)
    two = jnp.sum(jnp.where(left, 0.0, sums), axis=1, keepdims=True)
    total = jnp.where(left, one, two)
    high = total.astype(BF16)
    rel_out[at : at + 16, :] = high
    rel_out[at + 16 : at + 32, :] = (total - high.astype(F32)).astype(BF16)
    rel_out[at + 32 :, :] = jnp.zeros((rel_out.shape[0] - at - 32, WIDE), BF16)


def attend(edges, queries, key_rows, value_rows, halo_keys, halo_values, grad_output, halo_rows, rel_weight, rel_prior):
    rows = queries.shape[0]
    halo = halo_keys.shape[0]
    dests = rows // TILE
    sources = (rows + halo) // TILE
    count = edges.shape[1]
    rel_rows = 64 * 32
    return pl.pallas_call(
        attend_kernel,
        out_shape=(
            jax.ShapeDtypeStruct((rows, 3 * WIDE), BF16),
            jax.ShapeDtypeStruct((halo, 3 * WIDE), BF16),
            jax.ShapeDtypeStruct((rel_rows, WIDE), BF16),
        ),
        in_specs=[SMEM] + [VMEM] * 9,
        out_specs=(VMEM, VMEM, VMEM),
        scratch_shapes=[
            pltpu.VMEM((RELS, 2 * WIDE, 2 * WIDE), BF16),
            pltpu.VMEM((dests, 2 * WIDE, 2 * WIDE), BF16),
            pltpu.VMEM((sources, TILE, 2 * WIDE), BF16),
            pltpu.VMEM((sources, TILE, WIDE), F32),
            pltpu.VMEM((16, WIDE), F32),
            pltpu.VMEM((count, TILE, 2 * WIDE), BF16),
            pltpu.VMEM((count, TILE, WIDE), BF16),
            pltpu.VMEM((count, TILE, WIDE), F32),
            pltpu.VMEM((count, TILE, WIDE), F32),
            pltpu.VMEM((count, TILE, WIDE), F32),
            pltpu.VMEM((dests, 1, WIDE), F32),
            pltpu.VMEM((dests, 1, WIDE), F32),
            pltpu.VMEM((16, WIDE), F32),
            pltpu.VMEM((sources, TILE, 2 * WIDE), F32),
            pltpu.VMEM((RELS, WIDE, WIDE), F32),
            pltpu.VMEM((RELS, WIDE, WIDE), F32),
            pltpu.VMEM((dests, WIDE, WIDE), F32),
        ],
        compiler_params=pltpu.CompilerParams(vmem_limit_bytes=40 * 2**20),
        cost_estimate=pl.CostEstimate(flops=3 * 10**9, bytes_accessed=4 * 10**6, transcendentals=400000),
        name="attend",
    )(edges, queries, key_rows, value_rows, halo_keys, halo_values, grad_output, halo_rows, rel_weight, rel_prior)


def project_kernel(place, own_ref, inc_ref, nf_ref, types_ref, mine_out, theirs_out, masked_out, nft):
    rows = own_ref.shape[0]
    halo = inc_ref.shape[0]
    ids = inc_ref[:, 2 * WIDE :].astype(F32)
    nodes = lax.broadcasted_iota(jnp.int32, (halo, WIDE), 1).astype(F32)
    pick = jnp.concatenate(
        [(ids == nodes + float(j * WIDE)).astype(F32).astype(BF16) for j in range(rows // WIDE)], axis=1
    )
    back = mul(pick, inc_ref[:, : 2 * WIDE], TN)
    own = own_ref[...].astype(F32)
    parts = (own[:, :WIDE], own[:, WIDE : 2 * WIDE] + back[:, :WIDE], own[:, 2 * WIDE :] + back[:, WIDE:])
    kinds = jnp.concatenate(
        [column(types_ref[j : j + 1, :].astype(F32)) for j in range(rows // WIDE)], axis=0
    )
    for p in range(3):
        for t in range(TYPES):
            at = (p * TYPES + t) * WIDE
            masked_out[:, at : at + WIDE] = jnp.where(kinds == float(t), parts[p], 0.0).astype(BF16)
    nft[...] = jnp.transpose(nf_ref[...], (1, 0))
    even = place[0] == 0
    feats = nf_ref.shape[1]
    for j in range(PROJ):
        at = j * WIDE
        part = mul(nft[...], masked_out[:, at : at + WIDE], NN).reshape(feats // 16, 2, 8, WIDE)
        low = part[:, 0].reshape(feats // 2, WIDE)
        high = part[:, 1].reshape(feats // 2, WIDE)
        mine_out[:, at : at + WIDE] = jnp.where(even, low, high).astype(BF16)
        theirs_out[:, at : at + WIDE] = jnp.where(even, high, low).astype(BF16)


def project(place, own, incoming, node_feats, node_types):
    rows, feats = node_feats.shape
    return pl.pallas_call(
        project_kernel,
        out_shape=(
            jax.ShapeDtypeStruct((feats // 2, PROJ * WIDE), BF16),
            jax.ShapeDtypeStruct((feats // 2, PROJ * WIDE), BF16),
            jax.ShapeDtypeStruct((rows, PROJ * WIDE), BF16),
        ),
        in_specs=[SMEM] + [VMEM] * 4,
        out_specs=(VMEM, VMEM, VMEM),
        scratch_shapes=[pltpu.VMEM((feats, rows), BF16)],
        compiler_params=pltpu.CompilerParams(vmem_limit_bytes=40 * 2**20),
        cost_estimate=pl.CostEstimate(flops=10**9, bytes_accessed=4 * 10**6, transcendentals=0),
        name="project",
    )(place, own, incoming, node_feats, node_types)


def features_kernel(masked_ref, w_ref, out_ref):
    total = None
    for j in range(PROJ):
        at = j * WIDE
        term = mul(masked_ref[:, at : at + WIDE], w_ref[j], NT)
        total = term if total is None else total + term
    for h in range(out_ref.shape[0]):
        out_ref[h] = total[:, h * WIDE : (h + 1) * WIDE].astype(BF16)


def features(masked, weights):
    rows = masked.shape[0]
    feats = weights.shape[1]
    return pl.pallas_call(
        features_kernel,
        out_shape=jax.ShapeDtypeStruct((feats // WIDE, rows, WIDE), BF16),
        in_specs=[VMEM, VMEM],
        out_specs=VMEM,
        compiler_params=pltpu.CompilerParams(vmem_limit_bytes=40 * 2**20),
        cost_estimate=pl.CostEstimate(flops=10**9, bytes_accessed=3 * 10**6, transcendentals=0),
        name="features",
    )(masked, weights)


def pair_sum_kernel(place, mine_ref, got_ref, *outs):
    size = outs[0].shape[0]
    count = len(outs)
    for d in range(count):
        block = lax.rem(place[1] + d, count)
        at = pl.ds(pl.multiple_of(block * size, size), size)
        outs[d][...] = (mine_ref[at, :].astype(F32) + got_ref[at, :].astype(F32)).astype(BF16)


def pair_sum(place, mine, got, count):
    rows, columns = mine.shape
    return pl.pallas_call(
        pair_sum_kernel,
        out_shape=(jax.ShapeDtypeStruct((rows // count, columns), BF16),) * count,
        in_specs=[SMEM, VMEM, VMEM],
        out_specs=(VMEM,) * count,
        compiler_params=pltpu.CompilerParams(vmem_limit_bytes=40 * 2**20),
        cost_estimate=pl.CostEstimate(flops=10**6, bytes_accessed=3 * 10**6, transcendentals=0),
        name="pair_sum",
    )(place, mine, got)


def per_device(
    node_feats,
    node_types,
    queries,
    key_rows,
    value_rows,
    halo_keys,
    halo_values,
    halo_rows,
    edge_tiles,
    grad_output,
    proj_weight,
    rel_weight,
    rel_prior,
):
    nodes = ("y", "z", "core")
    y_count = lax.axis_size("y")
    z_count = lax.axis_size("z")
    slabs = y_count * z_count * 2
    place = jnp.stack([lax.axis_index("core"), lax.axis_index("y")]).astype(jnp.int32)
    own, send, rel = attend(
        edge_tiles.T,
        queries,
        key_rows,
        value_rows,
        halo_keys,
        halo_values,
        grad_output,
        halo_rows.reshape(-1, WIDE),
        rel_weight,
        rel_prior,
    )
    cap = send.shape[0] // slabs
    incoming = lax.all_to_all(send.reshape(slabs, cap, 3 * WIDE), nodes, 0, 0, tiled=True)
    rel_parts = lax.all_to_all(rel.reshape(slabs, -1, WIDE), nodes, 0, 0, tiled=True)
    mine, theirs, masked = project(
        place, own, incoming.reshape(-1, 3 * WIDE), node_feats, node_types.reshape(-1, WIDE)
    )
    got = lax.ppermute(theirs, "core", [(0, 1), (1, 0)])
    feat_parts = features(masked, proj_weight.reshape(PROJ, -1, WIDE))
    feat_got = lax.all_to_all(feat_parts, "heads", 0, 0, tiled=True)
    grad_feats = jnp.sum(feat_got.astype(F32), axis=0).astype(BF16)
    blocks = pair_sum(place, mine, got, y_count)
    arrived = [blocks[0]] + [
        lax.ppermute(blocks[d], "y", [(i, (i + d) % y_count) for i in range(y_count)])
        for d in range(1, y_count)
    ]
    by_z = sum(block.astype(F32) for block in arrived).astype(BF16)
    z_parts = lax.all_to_all(by_z.reshape(z_count, -1, PROJ * WIDE), "z", 0, 0, tiled=True)
    grad_proj = jnp.sum(z_parts.astype(F32), axis=0).reshape(-1, 3, TYPES, WIDE)

    rel_mine = jnp.sum(rel_parts.astype(F32), axis=0).astype(BF16)
    rel_all = lax.all_to_all(
        jnp.broadcast_to(rel_mine[None], (slabs,) + rel_mine.shape), nodes, 0, 0, tiled=True
    ).reshape(-1, WIDE)
    at = 2 * RELS * TILE
    grad_rel = rel_all[:at].astype(F32).reshape(2, RELS, TILE, 2, TILE).transpose(0, 1, 3, 2, 4)
    prior_all = rel_all[at : at + RELS].astype(F32) + rel_all[at + 16 : at + 16 + RELS].astype(F32)
    grad_prior = prior_all[:, ::TILE]
    return (grad_feats, grad_proj, grad_rel, grad_prior)


def solution(mesh):
    heads = mesh.devices.shape[1]
    split = Mesh(mesh.devices.reshape(4, 8, 2, heads), ("y", "z", "core", "heads"))
    nodes = ("y", "z", "core")
    return jax.shard_map(
        per_device,
        mesh=split,
        in_specs=(
            P(nodes, None),
            P(nodes),
            P(nodes, "heads"),
            P(nodes, "heads"),
            P(nodes, "heads"),
            P(nodes, "heads"),
            P(nodes, "heads"),
            P(nodes),
            P(nodes, None),
            P(nodes, "heads"),
            P(None, None, None, "heads"),
            P(None, None, "heads", None, None),
            P(None, "heads"),
        ),
        out_specs=(
            P(nodes, "heads"),
            P(nodes, None, None, "heads"),
            P(None, None, "heads", None, None),
            P(None, "heads"),
        ),
        check_vma=False,
    )
```

```python
import jax
import jax.numpy as jnp
from jax import lax
from jax.experimental import pallas as pl
from jax.experimental.pallas import tpu as pltpu
from jax.sharding import Mesh, PartitionSpec as P

TYPES = 5
RELS = 15
TILE = 64
WIDE = 128
GROUP = 8
PROJ = 3 * TYPES

F32 = jnp.float32
BF16 = jnp.bfloat16
NN = (((1,), (0,)), ((), ()))
NT = (((1,), (1,)), ((), ()))
TN = (((0,), (0,)), ((), ()))
VMEM = pl.BlockSpec(memory_space=pltpu.VMEM)
SMEM = pl.BlockSpec(memory_space=pltpu.SMEM)
HBM = pl.BlockSpec(memory_space=pltpu.HBM)
HALO_ROWS = 16
REL_ROWS = 30
BLOCK = 48
LIMIT = 24 * 2**20
MOST = 62 * 2**20


def mul(left, right, dims):
    return lax.dot_general(left, right, dims, preferred_element_type=F32)


def column(row):
    return jnp.transpose(jnp.broadcast_to(row, (WIDE, WIDE)), (1, 0))


def attend_kernel(
    edges_hbm, prior_hbm, q_hbm, g_hbm, ko_hbm, vo_hbm, kh_hbm, vh_hbm, rel_hbm, rows_hbm,
    own_out, send_out,
    edges, prior_in, q_ref, g_ref, rel_ref, rows_ref, k_ref, v_ref, sems,
    wbd, qg, keep, prior, kvm, probs, exps, logs, grads,
    denom, delta, dprior, dkv, dwk, dwv, dq, drel,
):
    count = edges.shape[1]
    own = ko_hbm.shape[0]
    dests = own // TILE
    own_tiles = own // TILE
    halo_tiles = kh_hbm.shape[0] // TILE
    slabs = send_out.shape[0]
    copies = [
        pltpu.make_async_copy(source, target, sems.at[i])
        for i, (source, target) in enumerate(
            (
                (rel_hbm, rel_ref),
                (q_hbm, q_ref),
                (g_hbm, g_ref),
                (rows_hbm, rows_ref),
                (edges_hbm, edges),
                (prior_hbm, prior_in),
                (ko_hbm, k_ref.at[:own]),
                (vo_hbm, v_ref.at[:own]),
                (kh_hbm, k_ref.at[own:]),
                (vh_hbm, v_ref.at[own:]),
            )
        )
    ]
    for copy in copies:
        copy.start()

    lane = lax.broadcasted_iota(jnp.int32, (TILE, WIDE), 1)
    first = lane < TILE
    wbd[...] = jnp.zeros_like(wbd)
    denom[...] = jnp.zeros_like(denom)
    delta[...] = jnp.zeros_like(delta)
    dprior[...] = jnp.zeros_like(dprior)
    dkv[...] = jnp.zeros_like(dkv)
    dwk[...] = jnp.zeros_like(dwk)
    dwv[...] = jnp.zeros_like(dwv)
    dq[...] = jnp.zeros_like(dq)
    for copy in copies:
        copy.wait()

    for r in range(RELS):
        for w in range(2):
            for h in range(2):
                at = (2 * w + h) * TILE
                wbd[r, at : at + TILE, at : at + TILE] = rel_ref[w, r, h]
    none = jnp.zeros((TILE, WIDE), BF16)
    for a in range(dests):
        q = q_ref[a * TILE : (a + 1) * TILE, :].astype(F32) * 0.125
        g = g_ref[a * TILE : (a + 1) * TILE, :].astype(F32)
        for h in range(2):
            mine = first if h == 0 else jnp.logical_not(first)
            qg[a, h * TILE : (h + 1) * TILE, :WIDE] = jnp.where(mine, q, 0.0).astype(BF16)
            qg[a, h * TILE : (h + 1) * TILE, WIDE:] = none
            qg[a, (2 + h) * TILE : (3 + h) * TILE, :WIDE] = none
            qg[a, (2 + h) * TILE : (3 + h) * TILE, WIDE:] = jnp.where(mine, g, 0.0).astype(BF16)
    for b in range(own_tiles):
        keep[b] = jnp.ones((TILE, WIDE), F32)
    period = lax.broadcasted_iota(jnp.int32, (16, 8, WIDE), 2) % 8
    slot = lax.broadcasted_iota(jnp.int32, (16, 8, WIDE), 1)
    for j in range(halo_tiles // 2):
        ids = column(rows_ref[j : j + 1, :].astype(F32))
        ok = (ids < float(own)).astype(F32)
        keep[own_tiles + 2 * j] = ok[:TILE]
        keep[own_tiles + 2 * j + 1] = ok[TILE:]
        tiled = jnp.sum(jnp.where(period == slot, ids.reshape(16, 8, WIDE), 0.0), axis=1)
        drel[2 * RELS * TILE + 16 + 16 * j : 2 * RELS * TILE + 32 + 16 * j, :] = tiled
    one_lane = lax.broadcasted_iota(jnp.int32, (1, WIDE), 1)
    for r in range(RELS):
        prior[r : r + 1, :] = jnp.where(one_lane < TILE, prior_in[0, r], prior_in[1, r])

    def entry(e):
        target = edges[0, e]
        return jnp.minimum(target, dests - 1), edges[1, e], edges[2, e], target < dests

    def rows(b):
        return pl.ds(pl.multiple_of(b * TILE, TILE), TILE)

    def scores(step, carry):
        for u in range(GROUP):
            e = step * GROUP + u
            a, b, r, live = entry(e)
            pair = jnp.concatenate([k_ref[rows(b), :], v_ref[rows(b), :]], axis=1)
            mixed = mul(pair, wbd[r], NN).astype(BF16)
            kvm[e] = mixed
            both = mul(mixed, qg[a], NT)
            logits = both[:, :WIDE]
            logs[e] = logits
            grads[e] = both[:, WIDE:]
            ex = jnp.exp(prior[pl.ds(r, 1), :] * logits) * (keep[b] * live.astype(F32))
            exps[e] = ex
            denom[a] += jnp.sum(ex, axis=0, keepdims=True)
        return carry

    lax.fori_loop(0, count // GROUP, scores, 0)
    denom[...] = 1.0 / denom[...]

    def normalise(step, carry):
        for u in range(GROUP):
            e = step * GROUP + u
            a, b, r, live = entry(e)
            soft = exps[e] * denom[a]
            exps[e] = soft
            prob = soft.astype(BF16)
            probs[e] = prob
            delta[a] += jnp.sum(prob.astype(F32) * grads[e], axis=0, keepdims=True)
        return carry

    lax.fori_loop(0, count // GROUP, normalise, 0)

    def backward(step, carry):
        for u in range(GROUP):
            e = step * GROUP + u
            a, b, r, live = entry(e)
            score_grad = exps[e] * (grads[e] - delta[a])
            dprior[pl.ds(r, 1), :] += jnp.sum(score_grad * logs[e], axis=0, keepdims=True)
            lgrad = (score_grad * prior[pl.ds(r, 1), :]).astype(BF16)
            pair = jnp.concatenate([lgrad, probs[e]], axis=1)
            mixed_grad = mul(pair, qg[a], NN).astype(BF16)
            dkv[b] += mul(mixed_grad, wbd[r], NT)
            dwk[r] += mul(k_ref[rows(b), :], mixed_grad[:, :WIDE], TN)
            dwv[r] += mul(v_ref[rows(b), :], mixed_grad[:, WIDE:], TN)
            dq[a] += mul(lgrad, kvm[e, :, :WIDE], TN)
        return carry

    lax.fori_loop(0, count // GROUP, backward, 0)

    for a in range(dests):
        grad = jnp.where(first, dq[a, :TILE, :], dq[a, TILE:, :]) * 0.125
        own_out[a * TILE : (a + 1) * TILE, :WIDE] = grad.astype(BF16)
    for b in range(own_tiles):
        own_out[b * TILE : (b + 1) * TILE, WIDE:] = dkv[b].astype(BF16)
    for b in range(halo_tiles):
        back = dkv[own_tiles + b]
        block = jnp.concatenate(
            [back[:, :WIDE].reshape(8, 8, WIDE), back[:, WIDE:].reshape(8, 8, WIDE)], axis=1
        )
        send_out[8 * b : 8 * b + 8, :HALO_ROWS, :] = block.astype(BF16)
    for w, ref in enumerate((dwk, dwv)):
        for r in range(RELS):
            at = (w * RELS + r) * TILE
            drel[at : at + TILE, :] = jnp.where(first, ref[r, :TILE, :], ref[r, TILE:, :])
    sums = dprior[...]
    spot = lax.broadcasted_iota(jnp.int32, sums.shape, 1)
    row = lax.broadcasted_iota(jnp.int32, sums.shape, 0)
    one = jnp.sum(jnp.where(spot < TILE, sums, 0.0), axis=1, keepdims=True)
    two = jnp.sum(jnp.where(spot < TILE, 0.0, sums), axis=1, keepdims=True)
    chosen = jnp.where((spot // 16) % 2 == 0, one, two)
    line = jnp.sum(jnp.where(spot % 16 == row, chosen, 0.0), axis=0, keepdims=True)
    high = line.astype(BF16).astype(F32)
    line = jnp.where(one_lane < 32, high, line - high)
    within = lax.broadcasted_iota(jnp.int32, (32, WIDE), 0)
    for p in range(slabs):
        at = 2 * RELS * TILE + 16 + p
        block = jnp.where(
            within < REL_ROWS,
            drel[REL_ROWS * p : REL_ROWS * p + 32, :],
            jnp.where(within == REL_ROWS, drel[at : at + 1, :], line),
        )
        send_out[p, HALO_ROWS:, :] = block.astype(BF16)


def attend(edges, rel_prior, queries, grad_output, key_rows, value_rows, halo_keys, halo_values, rel_weight, halo_rows):
    rows = queries.shape[0]
    halo = halo_keys.shape[0]
    dests = rows // TILE
    sources = (rows + halo) // TILE
    count = edges.shape[1]
    slabs = 64
    return pl.pallas_call(
        attend_kernel,
        out_shape=(
            jax.ShapeDtypeStruct((rows, 3 * WIDE), BF16),
            jax.ShapeDtypeStruct((slabs, BLOCK, WIDE), BF16),
        ),
        in_specs=[HBM] * 10,
        out_specs=(VMEM, VMEM),
        scratch_shapes=[
            pltpu.SMEM(edges.shape, jnp.int32),
            pltpu.SMEM(rel_prior.shape, F32),
            pltpu.VMEM(queries.shape, BF16),
            pltpu.VMEM(grad_output.shape, BF16),
            pltpu.VMEM(rel_weight.shape, BF16),
            pltpu.VMEM(halo_rows.shape, jnp.int32),
            pltpu.VMEM((rows + halo, WIDE), BF16),
            pltpu.VMEM((rows + halo, WIDE), BF16),
            pltpu.SemaphoreType.DMA((10,)),
            pltpu.VMEM((RELS, 2 * WIDE, 2 * WIDE), BF16),
            pltpu.VMEM((dests, 2 * WIDE, 2 * WIDE), BF16),
            pltpu.VMEM((sources, TILE, WIDE), F32),
            pltpu.VMEM((16, WIDE), F32),
            pltpu.VMEM((count, TILE, 2 * WIDE), BF16),
            pltpu.VMEM((count, TILE, WIDE), BF16),
            pltpu.VMEM((count, TILE, WIDE), F32),
            pltpu.VMEM((count, TILE, WIDE), F32),
            pltpu.VMEM((count, TILE, WIDE), F32),
            pltpu.VMEM((dests, 1, WIDE), F32),
            pltpu.VMEM((dests, 1, WIDE), F32),
            pltpu.VMEM((16, WIDE), F32),
            pltpu.VMEM((sources, TILE, 2 * WIDE), F32),
            pltpu.VMEM((RELS, WIDE, WIDE), F32),
            pltpu.VMEM((RELS, WIDE, WIDE), F32),
            pltpu.VMEM((dests, WIDE, WIDE), F32),
            pltpu.VMEM((2 * RELS * TILE + 16 + slabs, WIDE), F32),
        ],
        compiler_params=pltpu.CompilerParams(vmem_limit_bytes=MOST),
        cost_estimate=pl.CostEstimate(flops=3 * 10**9, bytes_accessed=4 * 10**6, transcendentals=400000),
        name="attend",
    )(edges, rel_prior, queries, grad_output, key_rows, value_rows, halo_keys, halo_values, rel_weight, halo_rows)


def bundle_kernel(place, own_ref, nf_ref, types_ref, mine_out, send_out):
    rows, feats = nf_ref.shape
    turned = jnp.transpose(nf_ref[...], (1, 0)).astype(F32).reshape(feats // 16, 2, 8, rows)
    low = turned[:, 0].reshape(feats // 2, rows)
    high = turned[:, 1].reshape(feats // 2, rows)
    even = place[0] == 0
    mine_out[...] = jnp.where(even, low, high).astype(BF16)
    send_out[:, :rows] = jnp.where(even, high, low).astype(BF16)
    send_out[:, rows : rows + WIDE] = own_ref[:, :WIDE]
    for j in range(rows // WIDE):
        kinds = column(types_ref[j : j + 1, :].astype(F32)).astype(BF16)
        send_out[j * WIDE : (j + 1) * WIDE, rows + WIDE :] = kinds


def bundle(place, own, node_feats, node_types):
    rows, feats = node_feats.shape
    return pl.pallas_call(
        bundle_kernel,
        out_shape=(
            jax.ShapeDtypeStruct((feats // 2, rows), BF16),
            jax.ShapeDtypeStruct((feats // 2, rows + 2 * WIDE), BF16),
        ),
        in_specs=[SMEM] + [VMEM] * 3,
        out_specs=(VMEM,) * 2,
        compiler_params=pltpu.CompilerParams(vmem_limit_bytes=LIMIT),
        cost_estimate=pl.CostEstimate(flops=10**6, bytes_accessed=2 * 10**6, transcendentals=0),
        name="bundle",
    )(place, own, node_feats, node_types)


def spread(place, products, outs):
    size = outs[0].shape[0]
    for d in range(len(outs)):
        block = lax.rem(place[1] + d, len(outs))
        outs[d][...] = products[pl.ds(pl.multiple_of(block * size, size), size), :]


def project_queries_kernel(place, mine_ref, sent_ref, got_ref, pair_out, *refs):
    outs, products = refs[:-1], refs[-1]
    rows = mine_ref.shape[1]
    pair_out[:, :rows] = mine_ref[...]
    pair_out[:, rows:] = got_ref[:, :rows]
    query = jnp.concatenate([ref[:, rows : rows + WIDE] for ref in (sent_ref, got_ref)], axis=0).astype(F32)
    kinds = jnp.concatenate([ref[:, rows + WIDE :] for ref in (sent_ref, got_ref)], axis=0).astype(F32)
    for t in range(TYPES):
        masked = jnp.where(kinds == float(t), query, 0.0).astype(BF16)
        products[:, t * WIDE : (t + 1) * WIDE] = mul(pair_out[...], masked, NN).astype(BF16)
    spread(place, products, outs)


def project_queries(place, mine, sent, got, count):
    feats, rows = mine.shape
    wide = TYPES * WIDE
    return pl.pallas_call(
        project_queries_kernel,
        out_shape=(jax.ShapeDtypeStruct((feats, 2 * rows), BF16),)
        + (jax.ShapeDtypeStruct((feats // count, wide), BF16),) * count,
        in_specs=[SMEM] + [VMEM] * 3,
        out_specs=(VMEM,) * (1 + count),
        scratch_shapes=[pltpu.VMEM((feats, wide), BF16)],
        compiler_params=pltpu.CompilerParams(vmem_limit_bytes=LIMIT),
        cost_estimate=pl.CostEstimate(flops=10**9, bytes_accessed=2 * 10**6, transcendentals=0),
        name="project_queries",
    )(place, mine, sent, got)


def collect_kernel(own_ref, inc_hbm, kv_out, rel_out, prior_out, inc_ref, sems):
    rows = own_ref.shape[0]
    slabs = inc_ref.shape[0]
    copies = [
        pltpu.make_async_copy(inc_hbm.at[pl.ds(16 * c, 16)], inc_ref.at[pl.ds(16 * c, 16)], sems.at[c])
        for c in range(slabs // 16)
    ]
    for copy in copies:
        copy.start()
    row = lax.broadcasted_iota(jnp.int32, (16, WIDE), 0)
    block = lax.broadcasted_iota(jnp.int32, (16, WIDE), 1) // 8
    node = lax.broadcasted_iota(jnp.int32, (rows, WIDE), 0).astype(F32)
    back = own_ref[:, WIDE:].astype(F32)
    total = None
    for c, copy in enumerate(copies):
        copy.wait()
        ids = inc_ref[16 * c : 16 * c + 16, HALO_ROWS + REL_ROWS - 14 :, :].astype(F32)[:, 14, :]
        line = jnp.sum(jnp.where(row == block, ids, 0.0), axis=0, keepdims=True)
        pick = (node == line).astype(F32).astype(BF16)
        grads = inc_ref[16 * c : 16 * c + 16, :HALO_ROWS, :].astype(F32)
        both = jnp.concatenate(
            [grads[:, :8].reshape(WIDE, WIDE), grads[:, 8:].reshape(WIDE, WIDE)], axis=1
        )
        back = back + mul(pick, both.astype(BF16), NN)
        for s in range(16 * c, 16 * c + 16):
            term = inc_ref[s, HALO_ROWS:, :].astype(F32)
            total = term if total is None else total + term
    kv_out[...] = back.astype(BF16)
    for s in range(rel_out.shape[0]):
        rel_out[s] = total.astype(BF16)
    line = total[REL_ROWS + 1 : REL_ROWS + 2, :]
    line = line + pltpu.roll(line, WIDE - 32, 1)
    prior_out[0:1, :] = line[:, :RELS]
    prior_out[1:2, :] = pltpu.roll(line, WIDE - 16, 1)[:, :RELS]


def collect(own, incoming):
    rows = own.shape[0]
    slabs = incoming.shape[0]
    return pl.pallas_call(
        collect_kernel,
        out_shape=(
            jax.ShapeDtypeStruct((rows, 2 * WIDE), BF16),
            jax.ShapeDtypeStruct((slabs // 2, 32, WIDE), BF16),
            jax.ShapeDtypeStruct((2, RELS), F32),
        ),
        in_specs=[VMEM, HBM],
        out_specs=(VMEM,) * 3,
        scratch_shapes=[pltpu.VMEM(incoming.shape, BF16), pltpu.SemaphoreType.DMA((slabs // 16,))],
        compiler_params=pltpu.CompilerParams(vmem_limit_bytes=LIMIT),
        cost_estimate=pl.CostEstimate(flops=10**8, bytes_accessed=2 * 10**6, transcendentals=0),
        name="collect",
    )(own, incoming)


def project_kernel(place, pair_ref, kv_ref, got_kv_ref, sent_ref, got_ref, *refs):
    outs, products = refs[:-1], refs[-1]
    rows = kv_ref.shape[0]
    kinds = jnp.concatenate([ref[:, rows + WIDE :] for ref in (sent_ref, got_ref)], axis=0).astype(F32)
    for p in range(2):
        part = jnp.concatenate(
            [ref[:, p * WIDE : (p + 1) * WIDE] for ref in (kv_ref, got_kv_ref)], axis=0
        ).astype(F32)
        for t in range(TYPES):
            at = (p * TYPES + t) * WIDE
            masked = jnp.where(kinds == float(t), part, 0.0).astype(BF16)
            products[:, at : at + WIDE] = mul(pair_ref[...], masked, NN).astype(BF16)
    spread(place, products, outs)


def project(place, pair, kv, got_kv, sent, got, count):
    feats = pair.shape[0]
    wide = 2 * TYPES * WIDE
    return pl.pallas_call(
        project_kernel,
        out_shape=(jax.ShapeDtypeStruct((feats // count, wide), BF16),) * count,
        in_specs=[SMEM] + [VMEM] * 5,
        out_specs=(VMEM,) * count,
        scratch_shapes=[pltpu.VMEM((feats, wide), BF16)],
        compiler_params=pltpu.CompilerParams(vmem_limit_bytes=LIMIT),
        cost_estimate=pl.CostEstimate(flops=10**9, bytes_accessed=4 * 10**6, transcendentals=0),
        name="project",
    )(place, pair, kv, got_kv, sent, got)


def features_kernel(place, sent_ref, kv_ref, w_ref, *refs):
    outs, total = refs[:-1], refs[-1]
    rows = kv_ref.shape[0]
    kinds = sent_ref[:, rows + WIDE :].astype(F32)
    acc = None
    for p in range(3):
        part = sent_ref[:, rows : rows + WIDE] if p == 0 else kv_ref[:, (p - 1) * WIDE : p * WIDE]
        part = part.astype(F32)
        for t in range(TYPES):
            masked = jnp.where(kinds == float(t), part, 0.0).astype(BF16)
            term = mul(masked, w_ref[p * TYPES + t], NT)
            acc = term if acc is None else acc + term
    for h in range(len(outs)):
        total[h] = acc[:, h * WIDE : (h + 1) * WIDE]
    for d in range(len(outs)):
        outs[d][...] = total[lax.rem(place[2] + d, len(outs))].astype(BF16)


def features(place, sent, kv, weights):
    rows = kv.shape[0]
    count = weights.shape[1] // WIDE
    return pl.pallas_call(
        features_kernel,
        out_shape=(jax.ShapeDtypeStruct((rows, WIDE), BF16),) * count,
        in_specs=[SMEM, VMEM, VMEM, VMEM],
        out_specs=(VMEM,) * count,
        scratch_shapes=[pltpu.VMEM((count, rows, WIDE), F32)],
        compiler_params=pltpu.CompilerParams(vmem_limit_bytes=LIMIT),
        cost_estimate=pl.CostEstimate(flops=10**9, bytes_accessed=3 * 10**6, transcendentals=0),
        name="features",
    )(place, sent, kv, weights)


def relation_kernel(place, mine_ref, other_ref, out_ref, flat):
    even = place[0] == 0
    for s in range(mine_ref.shape[0]):
        mine = mine_ref[s].astype(F32)
        other = other_ref[s].astype(F32)
        at = 2 * s * REL_ROWS
        flat[at : at + 32, :] = jnp.where(even, mine, other)
        flat[at + REL_ROWS : at + REL_ROWS + 32, :] = jnp.where(even, other, mine)
    for w in range(2):
        for r in range(RELS):
            at = (w * RELS + r) * TILE
            for h in range(2):
                out_ref[w, r, h] = flat[at : at + TILE, h * TILE : (h + 1) * TILE]


def relations(place, mine, other):
    return pl.pallas_call(
        relation_kernel,
        out_shape=jax.ShapeDtypeStruct((2, RELS, 2, TILE, TILE), F32),
        in_specs=[SMEM, VMEM, VMEM],
        out_specs=VMEM,
        scratch_shapes=[pltpu.VMEM((2 * RELS * TILE + 8, WIDE), F32)],
        compiler_params=pltpu.CompilerParams(vmem_limit_bytes=LIMIT),
        cost_estimate=pl.CostEstimate(flops=10**6, bytes_accessed=3 * 10**6, transcendentals=0),
        name="relations",
    )(place, mine, other)


def place_sum_kernel(*refs):
    out = refs[-1]
    half = (len(refs) - 1) // 2
    narrow = refs[0].shape[1]
    for at, group in ((0, refs[:half]), (narrow, refs[half:-1])):
        total = group[0][...].astype(F32)
        for ref in group[1:]:
            total = total + ref[...].astype(F32)
        out[:, at : at + total.shape[1]] = total.astype(BF16)


def place_sum(query, rest):
    rows = query[0].shape[0]
    return pl.pallas_call(
        place_sum_kernel,
        out_shape=jax.ShapeDtypeStruct((rows, PROJ * WIDE), BF16),
        in_specs=[VMEM] * (len(query) + len(rest)),
        out_specs=VMEM,
        compiler_params=pltpu.CompilerParams(vmem_limit_bytes=LIMIT),
        cost_estimate=pl.CostEstimate(flops=10**6, bytes_accessed=10**6, transcendentals=0),
        name="place_sum",
    )(*query, *rest)


def shifted(blocks, axis):
    count = len(blocks)
    return [blocks[0]] + [
        lax.ppermute(blocks[d], axis, [(i, (i + d) % count) for i in range(count)])
        for d in range(1, count)
    ]


def per_device(
    node_feats,
    node_types,
    queries,
    key_rows,
    value_rows,
    halo_keys,
    halo_values,
    halo_rows,
    edge_tiles,
    grad_output,
    proj_weight,
    rel_weight,
    rel_prior,
):
    y_count = lax.axis_size("y")
    z_count = lax.axis_size("z")
    place = jnp.stack(
        [lax.axis_index("core"), lax.axis_index("y"), lax.axis_index("heads")]
    ).astype(jnp.int32)
    swap = [(0, 1), (1, 0)]
    own, send = attend(
        edge_tiles.T,
        rel_prior.T,
        queries,
        grad_output,
        key_rows,
        value_rows,
        halo_keys,
        halo_values,
        rel_weight,
        halo_rows.reshape(-1, WIDE),
    )
    incoming = lax.all_to_all(send, ("y", "z", "core"), 0, 0, tiled=True)
    feats_t, sent = bundle(place, own, node_feats, node_types.reshape(-1, WIDE))
    got = lax.ppermute(sent, "core", swap)
    pair, *q_blocks = project_queries(place, feats_t, sent, got, y_count)
    q_arrived = shifted(q_blocks, "y")
    own, *q_arrived = lax.optimization_barrier((own, *q_arrived))
    kv, rel_send, prior = collect(own, incoming)
    got_kv = lax.ppermute(kv, "core", swap)
    rel_half = lax.all_to_all(rel_send, ("y", "z"), 0, 0, tiled=True)
    arrived = shifted(project(place, pair, kv, got_kv, sent, got, y_count), "y")
    feat_blocks = features(place, sent, kv, proj_weight.reshape(PROJ, -1, WIDE))
    arrived[0], *feat_blocks = lax.optimization_barrier((arrived[0], *feat_blocks))
    grad_feats = sum(block.astype(F32) for block in shifted(feat_blocks, "heads")).astype(BF16)
    by_y = place_sum(q_arrived, arrived)
    by_z = lax.all_to_all(by_y.reshape(z_count, -1, PROJ * WIDE), "z", 0, 0, tiled=True)
    grad_proj = jnp.sum(by_z.astype(F32), axis=0).reshape(-1, 3, TYPES, WIDE)
    grad_rel = relations(place, rel_half, lax.ppermute(rel_half, "core", swap))
    grad_prior = prior.T
    return (grad_feats, grad_proj, grad_rel, grad_prior)


def solution(mesh):
    heads = mesh.devices.shape[1]
    split = Mesh(mesh.devices.reshape(4, 8, 2, heads), ("y", "z", "core", "heads"))
    nodes = ("y", "z", "core")
    return jax.shard_map(
        per_device,
        mesh=split,
        in_specs=(
            P(nodes, None),
            P(nodes),
            P(nodes, "heads"),
            P(nodes, "heads"),
            P(nodes, "heads"),
            P(nodes, "heads"),
            P(nodes, "heads"),
            P(nodes),
            P(nodes, None),
            P(nodes, "heads"),
            P(None, None, None, "heads"),
            P(None, None, "heads", None, None),
            P(None, "heads"),
        ),
        out_specs=(
            P(nodes, "heads"),
            P(nodes, None, None, "heads"),
            P(None, None, "heads", None, None),
            P(None, "heads"),
        ),
        check_vma=False,
    )
```

```python
import jax
import jax.numpy as jnp
from jax import lax
from jax.experimental import pallas as pl
from jax.experimental.pallas import tpu as pltpu
from jax.sharding import Mesh, PartitionSpec as P

TYPES = 5
RELS = 15
TILE = 64
WIDE = 128
GROUP = 4
UNROLL = 7
PROJ = 3 * TYPES

F32 = jnp.float32
BF16 = jnp.bfloat16
NN = (((1,), (0,)), ((), ()))
NT = (((1,), (1,)), ((), ()))
TN = (((0,), (0,)), ((), ()))
VMEM = pl.BlockSpec(memory_space=pltpu.VMEM)
SMEM = pl.BlockSpec(memory_space=pltpu.SMEM)
HBM = pl.BlockSpec(memory_space=pltpu.HBM)
BLOCK = 24
REL_ROWS = 240
REL_BLOCK = 256
LIMIT = 24 * 2**20
MOST = 62 * 2**20


def mul(left, right, dims):
    return lax.dot_general(left, right, dims, preferred_element_type=F32)


def column(row):
    return jnp.transpose(jnp.broadcast_to(row, (WIDE, WIDE)), (1, 0))


def high_and_low(line):
    line = line + pltpu.roll(line, WIDE - 32, 1)
    high = line.astype(BF16).astype(F32)
    lane = lax.broadcasted_iota(jnp.int32, line.shape, 1)
    return jnp.where(lane < 32, high, pltpu.roll(line - high, 32, 1))


def with_line(block):
    row = lax.broadcasted_iota(jnp.int32, block.shape, 0)
    return jnp.where(row == REL_ROWS, high_and_low(block[REL_ROWS : REL_ROWS + 1, :]), block)


def attend_kernel(
    edges_hbm, prior_hbm, q_hbm, g_hbm, ko_hbm, vo_hbm, kh_hbm, vh_hbm, rel_hbm, rows_hbm,
    own_out, send_out, rel_out,
    edges, listed, prior_in, q_ref, g_ref, rel_ref, rows_ref, k_ref, v_ref, sems,
    wbd, qg, keep, prior, kvm, probs, exps, logs, grads,
    denom, delta, dprior, dkv, dwk, dwv, dq, drel, ids_ref,
):
    count = edges.shape[1]
    places = kvm.shape[0]
    own = ko_hbm.shape[0]
    dests = own // TILE
    own_tiles = own // TILE
    halo_tiles = kh_hbm.shape[0] // TILE
    copies = [
        pltpu.make_async_copy(source, target, sems.at[i])
        for i, (source, target) in enumerate(
            (
                (rel_hbm, rel_ref),
                (q_hbm, q_ref),
                (g_hbm, g_ref),
                (rows_hbm, rows_ref),
                (edges_hbm, edges),
                (prior_hbm, prior_in),
                (ko_hbm, k_ref.at[:own]),
                (vo_hbm, v_ref.at[:own]),
                (kh_hbm, k_ref.at[own:]),
                (vh_hbm, v_ref.at[own:]),
            )
        )
    ]
    for copy in copies:
        copy.start()

    lane = lax.broadcasted_iota(jnp.int32, (TILE, WIDE), 1)
    first = lane < TILE
    wbd[...] = jnp.zeros_like(wbd)
    denom[...] = jnp.zeros_like(denom)
    delta[...] = jnp.zeros_like(delta)
    dprior[...] = jnp.zeros_like(dprior)
    dkv[...] = jnp.zeros_like(dkv)
    dwk[...] = jnp.zeros_like(dwk)
    dwv[...] = jnp.zeros_like(dwv)
    dq[...] = jnp.zeros_like(dq)
    copies[4].wait()
    for i in range(listed.shape[0]):
        listed[i] = 0
    targets = [edges[0, e] for e in range(count)]
    sizes = [sum((target == a).astype(jnp.int32) for target in targets) for a in range(dests)]
    starts = [jnp.int32(0)]
    for a in range(dests):
        starts.append(starts[a] + (sizes[a] + GROUP - 1) // GROUP * GROUP)
    heads = list(starts[:dests])
    for e, target in enumerate(targets):
        at = jnp.int32(places)
        for a in range(dests):
            at = jnp.where(target == a, heads[a], at)
            heads[a] = heads[a] + (target == a).astype(jnp.int32)
        listed[at] = 256 + 16 * edges[1, e] + edges[2, e]
    used = starts[dests] // GROUP
    for i, copy in enumerate(copies):
        if i != 4:
            copy.wait()

    for r in range(RELS):
        for w in range(2):
            for h in range(2):
                at = (2 * w + h) * TILE
                wbd[r, at : at + TILE, at : at + TILE] = rel_ref[w, r, h]
    none = jnp.zeros((TILE, WIDE), BF16)
    for a in range(dests):
        q = q_ref[a * TILE : (a + 1) * TILE, :].astype(F32) * 0.125
        g = g_ref[a * TILE : (a + 1) * TILE, :].astype(F32)
        for h in range(2):
            mine = first if h == 0 else jnp.logical_not(first)
            qg[a, h * TILE : (h + 1) * TILE, :WIDE] = jnp.where(mine, q, 0.0).astype(BF16)
            qg[a, h * TILE : (h + 1) * TILE, WIDE:] = none
            qg[a, (2 + h) * TILE : (3 + h) * TILE, :WIDE] = none
            qg[a, (2 + h) * TILE : (3 + h) * TILE, WIDE:] = jnp.where(mine, g, 0.0).astype(BF16)
    for b in range(own_tiles):
        keep[b] = jnp.ones((TILE, WIDE), F32)
    period = lax.broadcasted_iota(jnp.int32, (16, 8, WIDE), 2) % 8
    slot = lax.broadcasted_iota(jnp.int32, (16, 8, WIDE), 1)
    for j in range(halo_tiles // 2):
        ids = column(rows_ref[j : j + 1, :].astype(F32))
        ok = (ids < float(own)).astype(F32)
        keep[own_tiles + 2 * j] = ok[:TILE]
        keep[own_tiles + 2 * j + 1] = ok[TILE:]
        tiled = jnp.sum(jnp.where(period == slot, ids.reshape(16, 8, WIDE), 0.0), axis=1)
        ids_ref[16 * j : 16 * j + 16, :] = tiled
    one_lane = lax.broadcasted_iota(jnp.int32, (1, WIDE), 1)
    for r in range(RELS):
        prior[r : r + 1, :] = jnp.where(one_lane < TILE, prior_in[0, r], prior_in[1, r])

    def entry(i):
        code = listed[i]
        return (code >> 4) & 15, code & 15, (code >= 256).astype(F32)

    def rows(b):
        return pl.ds(pl.multiple_of(b * TILE, TILE), TILE)

    def tile_of(group):
        at = group * GROUP
        return sum((at >= starts[a]).astype(jnp.int32) for a in range(1, dests))

    def scores(group):
        i = group * GROUP
        a = tile_of(group)
        parts = []
        for u in range(GROUP):
            b, r, live = entry(i + u)
            pair = jnp.concatenate([k_ref[rows(b), :], v_ref[rows(b), :]], axis=1)
            parts.append(mul(pair, wbd[r], NN).astype(BF16))
        mixed = jnp.concatenate(parts, axis=0)
        kvm[pl.ds(i, GROUP)] = mixed[:, :WIDE].reshape(GROUP, TILE, WIDE)
        both = mul(mixed, qg[a], NT)
        logs[pl.ds(i, GROUP)] = both[:, :WIDE].reshape(GROUP, TILE, WIDE)
        grads[pl.ds(i, GROUP)] = both[:, WIDE:].reshape(GROUP, TILE, WIDE)
        total = None
        for u in range(GROUP):
            b, r, live = entry(i + u)
            ex = jnp.exp(prior[pl.ds(r, 1), :] * both[u * TILE : (u + 1) * TILE, :WIDE]) * (keep[b] * live)
            exps[i + u] = ex
            total = ex if total is None else total + ex
        denom[a] += jnp.sum(total, axis=0, keepdims=True)

    def normalise(group):
        i = group * GROUP
        a = tile_of(group)
        total = None
        for u in range(GROUP):
            soft = exps[i + u] * denom[a]
            exps[i + u] = soft
            prob = soft.astype(BF16)
            probs[i + u] = prob
            term = prob.astype(F32) * grads[i + u]
            total = term if total is None else total + term
        delta[a] += jnp.sum(total, axis=0, keepdims=True)

    def backward(group):
        i = group * GROUP
        a = tile_of(group)
        parts = []
        for u in range(GROUP):
            b, r, live = entry(i + u)
            score_grad = exps[i + u] * (grads[i + u] - delta[a])
            dprior[pl.ds(r, 1), :] += jnp.sum(score_grad * logs[i + u], axis=0, keepdims=True)
            parts.append((score_grad * prior[pl.ds(r, 1), :]).astype(BF16))
        lgrad = jnp.concatenate(parts, axis=0)
        pair = jnp.concatenate([lgrad, probs[pl.ds(i, GROUP)].reshape(GROUP * TILE, WIDE)], axis=1)
        mixed_grad = mul(pair, qg[a], NN).astype(BF16)
        dq[a] += mul(lgrad, kvm[pl.ds(i, GROUP)].reshape(GROUP * TILE, WIDE), TN)
        for u in range(GROUP):
            b, r, live = entry(i + u)
            part = mixed_grad[u * TILE : (u + 1) * TILE]
            dkv[b] += mul(part, wbd[r], NT)
            dwk[r] += mul(k_ref[rows(b), :], part[:, :WIDE], TN)
            dwv[r] += mul(v_ref[rows(b), :], part[:, WIDE:], TN)

    def sweep(work):
        def some(step, carry):
            for u in range(UNROLL):
                work(step * UNROLL + u)
            return carry

        lax.fori_loop(0, (used + UNROLL - 1) // UNROLL, some, 0)

    sweep(scores)
    denom[...] = 1.0 / denom[...]
    sweep(normalise)
    sweep(backward)

    for a in range(dests):
        grad = jnp.where(first, dq[a, :TILE, :], dq[a, TILE:, :]) * 0.125
        own_out[a * TILE : (a + 1) * TILE, :WIDE] = grad.astype(BF16)
    for b in range(own_tiles):
        own_out[b * TILE : (b + 1) * TILE, WIDE:] = dkv[b].astype(BF16)
    for b in range(halo_tiles):
        back = dkv[own_tiles + b]
        block = jnp.concatenate(
            [
                back[:, :WIDE].reshape(8, 8, WIDE),
                back[:, WIDE:].reshape(8, 8, WIDE),
                jnp.broadcast_to(ids_ref[8 * b : 8 * b + 8, :].reshape(8, 1, WIDE), (8, 8, WIDE)),
            ],
            axis=1,
        )
        send_out[8 * b : 8 * b + 8] = block.astype(BF16)
    for w, ref in enumerate((dwk, dwv)):
        for r in range(RELS):
            at = (w * RELS + r) * TILE
            drel[at : at + TILE, :] = jnp.where(first, ref[r, :TILE, :], ref[r, TILE:, :])
    sums = dprior[...]
    spot = lax.broadcasted_iota(jnp.int32, sums.shape, 1)
    row = lax.broadcasted_iota(jnp.int32, sums.shape, 0)
    one = jnp.sum(jnp.where(spot < TILE, sums, 0.0), axis=1, keepdims=True)
    two = jnp.sum(jnp.where(spot < TILE, 0.0, sums), axis=1, keepdims=True)
    chosen = jnp.where((spot // 16) % 2 == 0, one, two)
    line = jnp.sum(jnp.where(spot % 16 == row, chosen, 0.0), axis=0, keepdims=True)
    high = line.astype(BF16).astype(F32)
    line = jnp.where(one_lane < 32, high, line - high)
    tail = jnp.where(lax.broadcasted_iota(jnp.int32, (16, WIDE), 0) == 0, line, 0.0).astype(BF16)
    for w in range(2):
        for y in range(rel_out.shape[1]):
            at = (w * rel_out.shape[1] + y) * REL_ROWS
            rel_out[w, y, :REL_ROWS, :] = drel[at : at + REL_ROWS, :].astype(BF16)
            rel_out[w, y, REL_ROWS:, :] = tail


def attend(edges, rel_prior, queries, grad_output, key_rows, value_rows, halo_keys, halo_values, rel_weight, halo_rows):
    rows = queries.shape[0]
    halo = halo_keys.shape[0]
    dests = rows // TILE
    sources = (rows + halo) // TILE
    count = edges.shape[1]
    groups = -(-(count // GROUP + dests - 1) // UNROLL) * UNROLL
    places = groups * GROUP
    slabs = 64
    return pl.pallas_call(
        attend_kernel,
        out_shape=(
            jax.ShapeDtypeStruct((rows, 3 * WIDE), BF16),
            jax.ShapeDtypeStruct((slabs, BLOCK, WIDE), BF16),
            jax.ShapeDtypeStruct((2, 2 * RELS * TILE // (2 * REL_ROWS), REL_BLOCK, WIDE), BF16),
        ),
        in_specs=[HBM] * 10,
        out_specs=(VMEM,) * 3,
        scratch_shapes=[
            pltpu.SMEM(edges.shape, jnp.int32),
            pltpu.SMEM((places + 1,), jnp.int32),
            pltpu.SMEM(rel_prior.shape, F32),
            pltpu.VMEM(queries.shape, BF16),
            pltpu.VMEM(grad_output.shape, BF16),
            pltpu.VMEM(rel_weight.shape, BF16),
            pltpu.VMEM(halo_rows.shape, jnp.int32),
            pltpu.VMEM((rows + halo, WIDE), BF16),
            pltpu.VMEM((rows + halo, WIDE), BF16),
            pltpu.SemaphoreType.DMA((10,)),
            pltpu.VMEM((RELS, 2 * WIDE, 2 * WIDE), BF16),
            pltpu.VMEM((dests, 2 * WIDE, 2 * WIDE), BF16),
            pltpu.VMEM((sources, TILE, WIDE), F32),
            pltpu.VMEM((16, WIDE), F32),
            pltpu.VMEM((places, TILE, WIDE), BF16),
            pltpu.VMEM((places, TILE, WIDE), BF16),
            pltpu.VMEM((places, TILE, WIDE), F32),
            pltpu.VMEM((places, TILE, WIDE), F32),
            pltpu.VMEM((places, TILE, WIDE), F32),
            pltpu.VMEM((dests, 1, WIDE), F32),
            pltpu.VMEM((dests, 1, WIDE), F32),
            pltpu.VMEM((16, WIDE), F32),
            pltpu.VMEM((sources, TILE, 2 * WIDE), F32),
            pltpu.VMEM((RELS, WIDE, WIDE), F32),
            pltpu.VMEM((RELS, WIDE, WIDE), F32),
            pltpu.VMEM((dests, WIDE, WIDE), F32),
            pltpu.VMEM((2 * RELS * TILE, WIDE), F32),
            pltpu.VMEM((slabs, WIDE), F32),
        ],
        compiler_params=pltpu.CompilerParams(vmem_limit_bytes=MOST),
        cost_estimate=pl.CostEstimate(flops=3 * 10**9, bytes_accessed=4 * 10**6, transcendentals=400000),
        name="attend",
    )(edges, rel_prior, queries, grad_output, key_rows, value_rows, halo_keys, halo_values, rel_weight, halo_rows)


def bundle_kernel(place, own_ref, nf_ref, types_ref, rel_ref, mine_out, send_out, keep_out, rel_out):
    rel_out[...] = rel_ref[1 - place[0]]
    keep_out[...] = rel_ref[place[0]]
    rows, feats = nf_ref.shape
    turned = jnp.transpose(nf_ref[...], (1, 0)).astype(F32).reshape(feats // 16, 2, 8, rows)
    low = turned[:, 0].reshape(feats // 2, rows)
    high = turned[:, 1].reshape(feats // 2, rows)
    even = place[0] == 0
    mine_out[...] = jnp.where(even, low, high).astype(BF16)
    send_out[:, :rows] = jnp.where(even, high, low).astype(BF16)
    for j in range(rows // WIDE):
        kinds = column(types_ref[j : j + 1, :].astype(F32)).astype(BF16)
        send_out[j * WIDE : (j + 1) * WIDE, rows + WIDE :] = kinds
    send_out[:, rows : rows + WIDE] = own_ref[:, :WIDE]


def bundle(place, own, node_feats, node_types, rel):
    rows, feats = node_feats.shape
    return pl.pallas_call(
        bundle_kernel,
        out_shape=(
            jax.ShapeDtypeStruct((feats // 2, rows), BF16),
            jax.ShapeDtypeStruct((feats // 2, rows + 2 * WIDE), BF16),
            jax.ShapeDtypeStruct(rel.shape[1:], BF16),
            jax.ShapeDtypeStruct(rel.shape[1:], BF16),
        ),
        in_specs=[SMEM] + [VMEM] * 4,
        out_specs=(VMEM,) * 4,
        compiler_params=pltpu.CompilerParams(vmem_limit_bytes=LIMIT),
        cost_estimate=pl.CostEstimate(flops=10**6, bytes_accessed=2 * 10**6, transcendentals=0),
        name="bundle",
    )(place, own, node_feats, node_types, rel)


def spread(place, products, outs):
    size = outs[0].shape[0]
    for d in range(len(outs)):
        block = lax.rem(place[1] + d, len(outs))
        outs[d][:, : products.shape[1]] = products[pl.ds(pl.multiple_of(block * size, size), size), :]


def project_queries_kernel(place, mine_ref, sent_ref, got_ref, rel_ref, rel_got_ref, pair_out, *refs):
    outs, products = refs[:-1], refs[-1]
    rows = mine_ref.shape[1]
    pair_out[:, :rows] = mine_ref[...]
    pair_out[:, rows:] = got_ref[:, :rows]
    query = jnp.concatenate([ref[:, rows : rows + WIDE] for ref in (sent_ref, got_ref)], axis=0).astype(F32)
    kinds = jnp.concatenate([ref[:, rows + WIDE :] for ref in (sent_ref, got_ref)], axis=0).astype(F32)
    for t in range(TYPES):
        masked = jnp.where(kinds == float(t), query, 0.0).astype(BF16)
        products[:, t * WIDE : (t + 1) * WIDE] = mul(pair_out[...], masked, NN).astype(BF16)
    spread(place, products, outs)
    for d in range(len(outs)):
        block = lax.rem(place[1] + d, len(outs))
        both = with_line(rel_ref[block].astype(F32) + rel_got_ref[block].astype(F32)).astype(BF16)
        for k in range(REL_BLOCK // TILE):
            at = (TYPES + k) * WIDE
            outs[d][:, at : at + WIDE] = both[k * TILE : (k + 1) * TILE, :]


def project_queries(place, mine, sent, got, rel, rel_got, count):
    feats, rows = mine.shape
    wide = TYPES * WIDE
    more = REL_BLOCK // TILE * WIDE
    return pl.pallas_call(
        project_queries_kernel,
        out_shape=(jax.ShapeDtypeStruct((feats, 2 * rows), BF16),)
        + (jax.ShapeDtypeStruct((feats // count, wide + more), BF16),) * count,
        in_specs=[SMEM] + [VMEM] * 5,
        out_specs=(VMEM,) * (1 + count),
        scratch_shapes=[pltpu.VMEM((feats, wide), BF16)],
        compiler_params=pltpu.CompilerParams(vmem_limit_bytes=LIMIT),
        cost_estimate=pl.CostEstimate(flops=10**9, bytes_accessed=2 * 10**6, transcendentals=0),
        name="project_queries",
    )(place, mine, sent, got, rel, rel_got)


def collect_kernel(own_ref, inc_ref, kv_out):
    rows = own_ref.shape[0]
    slabs = inc_ref.shape[0]
    row = lax.broadcasted_iota(jnp.int32, (16, WIDE), 0)
    block = lax.broadcasted_iota(jnp.int32, (16, WIDE), 1) // 8
    node = lax.broadcasted_iota(jnp.int32, (rows, WIDE), 0).astype(F32)
    back = own_ref[:, WIDE:].astype(F32)
    for c in range(slabs // 16):
        grads = inc_ref[16 * c : 16 * c + 16].astype(F32)
        ids = grads[:, 16, :]
        line = jnp.sum(jnp.where(row == block, ids, 0.0), axis=0, keepdims=True)
        pick = (node == line).astype(F32).astype(BF16)
        both = jnp.concatenate(
            [grads[:, :8].reshape(WIDE, WIDE), grads[:, 8:16].reshape(WIDE, WIDE)], axis=1
        )
        back = back + mul(pick, both.astype(BF16), NN)
    kv_out[...] = back.astype(BF16)


def collect(own, incoming):
    rows = own.shape[0]
    return pl.pallas_call(
        collect_kernel,
        out_shape=jax.ShapeDtypeStruct((rows, 2 * WIDE), BF16),
        in_specs=[VMEM, VMEM],
        out_specs=VMEM,
        compiler_params=pltpu.CompilerParams(vmem_limit_bytes=LIMIT),
        cost_estimate=pl.CostEstimate(flops=10**8, bytes_accessed=10**6, transcendentals=0),
        name="collect",
    )(own, incoming)


def relation_places_kernel(*refs):
    out = refs[-1]
    parts = []
    for k in range(REL_BLOCK // TILE):
        at = (TYPES + k) * WIDE
        total = refs[0][:, at : at + WIDE].astype(F32)
        for ref in refs[1:-1]:
            total = total + ref[:, at : at + WIDE].astype(F32)
        parts.append(total)
    total = with_line(jnp.concatenate(parts, axis=0)).astype(BF16)
    for z in range(out.shape[0]):
        out[z] = total


def relation_places(arrived, count):
    return pl.pallas_call(
        relation_places_kernel,
        out_shape=jax.ShapeDtypeStruct((count, REL_BLOCK, WIDE), BF16),
        in_specs=[VMEM] * len(arrived),
        out_specs=VMEM,
        compiler_params=pltpu.CompilerParams(vmem_limit_bytes=LIMIT),
        cost_estimate=pl.CostEstimate(flops=10**6, bytes_accessed=10**6, transcendentals=0),
        name="relation_places",
    )(*arrived)


def relation_sum_kernel(inc_ref, rel_out, prior_out):
    total = inc_ref[0].astype(F32)
    for s in range(1, inc_ref.shape[0]):
        total = total + inc_ref[s].astype(F32)
    rel_out[...] = total.astype(BF16)
    line = total[REL_ROWS : REL_ROWS + 1, :]
    line = line + pltpu.roll(line, WIDE - 32, 1)
    prior_out[0:1, :] = line[:, :RELS]
    prior_out[1:2, :] = pltpu.roll(line, WIDE - 16, 1)[:, :RELS]


def relation_sum(incoming):
    return pl.pallas_call(
        relation_sum_kernel,
        out_shape=(
            jax.ShapeDtypeStruct(incoming.shape[1:], BF16),
            jax.ShapeDtypeStruct((2, RELS), F32),
        ),
        in_specs=[VMEM],
        out_specs=(VMEM,) * 2,
        compiler_params=pltpu.CompilerParams(vmem_limit_bytes=LIMIT),
        cost_estimate=pl.CostEstimate(flops=10**6, bytes_accessed=10**6, transcendentals=0),
        name="relation_sum",
    )(incoming)


def project_kernel(place, pair_ref, kv_ref, got_kv_ref, sent_ref, got_ref, *refs):
    outs, products = refs[:-1], refs[-1]
    rows = kv_ref.shape[0]
    kinds = jnp.concatenate([ref[:, rows + WIDE :] for ref in (sent_ref, got_ref)], axis=0).astype(F32)
    for p in range(2):
        part = jnp.concatenate(
            [ref[:, p * WIDE : (p + 1) * WIDE] for ref in (kv_ref, got_kv_ref)], axis=0
        ).astype(F32)
        for t in range(TYPES):
            at = (p * TYPES + t) * WIDE
            masked = jnp.where(kinds == float(t), part, 0.0).astype(BF16)
            products[:, at : at + WIDE] = mul(pair_ref[...], masked, NN).astype(BF16)
    spread(place, products, outs)


def project(place, pair, kv, got_kv, sent, got, count):
    feats = pair.shape[0]
    wide = 2 * TYPES * WIDE
    return pl.pallas_call(
        project_kernel,
        out_shape=(jax.ShapeDtypeStruct((feats // count, wide), BF16),) * count,
        in_specs=[SMEM] + [VMEM] * 5,
        out_specs=(VMEM,) * count,
        scratch_shapes=[pltpu.VMEM((feats, wide), BF16)],
        compiler_params=pltpu.CompilerParams(vmem_limit_bytes=LIMIT),
        cost_estimate=pl.CostEstimate(flops=10**9, bytes_accessed=4 * 10**6, transcendentals=0),
        name="project",
    )(place, pair, kv, got_kv, sent, got)


def features_kernel(place, sent_ref, kv_ref, w_ref, *refs):
    outs, total = refs[:-1], refs[-1]
    rows = kv_ref.shape[0]
    kinds = sent_ref[:, rows + WIDE :].astype(F32)
    acc = None
    for p in range(3):
        part = sent_ref[:, rows : rows + WIDE] if p == 0 else kv_ref[:, (p - 1) * WIDE : p * WIDE]
        part = part.astype(F32)
        for t in range(TYPES):
            masked = jnp.where(kinds == float(t), part, 0.0).astype(BF16)
            term = mul(masked, w_ref[p * TYPES + t], NT)
            acc = term if acc is None else acc + term
    for h in range(len(outs)):
        total[h] = acc[:, h * WIDE : (h + 1) * WIDE]
    me = place[2]
    first = me + 1 - 2 * lax.rem(me, 2)
    for out, owner in zip(outs, (me, 3 - me, first, 3 - first)):
        out[...] = total[owner].astype(BF16)


def features(place, sent, kv, weights):
    rows = kv.shape[0]
    count = weights.shape[1] // WIDE
    return pl.pallas_call(
        features_kernel,
        out_shape=(jax.ShapeDtypeStruct((rows, WIDE), BF16),) * count,
        in_specs=[SMEM, VMEM, VMEM, VMEM],
        out_specs=(VMEM,) * count,
        scratch_shapes=[pltpu.VMEM((count, rows, WIDE), F32)],
        compiler_params=pltpu.CompilerParams(vmem_limit_bytes=LIMIT),
        cost_estimate=pl.CostEstimate(flops=10**9, bytes_accessed=3 * 10**6, transcendentals=0),
        name="features",
    )(place, sent, kv, weights)


def relation_kernel(place, mine_ref, first_ref, last_ref, c_mine_ref, c_first_ref, c_last_ref, out_ref, flat):
    y = place[1]
    last = 3 - y
    owners = (y, y + 1 - 2 * lax.rem(y, 2), last, last + 1 - 2 * lax.rem(last, 2))
    for core, refs in (
        (place[0], (mine_ref, first_ref, last_ref.at[0], last_ref.at[1])),
        (1 - place[0], (c_mine_ref, c_first_ref, c_last_ref.at[0], c_last_ref.at[1])),
    ):
        for owner, ref in zip(owners, refs):
            at = pl.multiple_of((core * len(owners) + owner) * REL_ROWS, 16)
            flat[pl.ds(at, REL_ROWS), :] = ref[:REL_ROWS, :].astype(F32)
    for w in range(2):
        for r in range(RELS):
            at = (w * RELS + r) * TILE
            for h in range(2):
                out_ref[w, r, h] = flat[at : at + TILE, h * TILE : (h + 1) * TILE]


def relations(place, *blocks):
    return pl.pallas_call(
        relation_kernel,
        out_shape=jax.ShapeDtypeStruct((2, RELS, 2, TILE, TILE), F32),
        in_specs=[SMEM] + [VMEM] * 6,
        out_specs=VMEM,
        scratch_shapes=[pltpu.VMEM((2 * RELS * TILE, WIDE), F32)],
        compiler_params=pltpu.CompilerParams(vmem_limit_bytes=LIMIT),
        cost_estimate=pl.CostEstimate(flops=10**6, bytes_accessed=3 * 10**6, transcendentals=0),
        name="relations",
    )(place, *blocks)


def place_sum_kernel(*refs):
    out = refs[-1]
    half = (len(refs) - 1) // 2
    narrow = TYPES * WIDE
    for at, group in ((0, refs[:half]), (narrow, refs[half:-1])):
        width = narrow if at == 0 else group[0].shape[1]
        total = group[0][:, :width].astype(F32)
        for ref in group[1:]:
            total = total + ref[:, :width].astype(F32)
        out[:, at : at + width] = total.astype(BF16)


def place_sum(query, rest):
    rows = query[0].shape[0]
    return pl.pallas_call(
        place_sum_kernel,
        out_shape=jax.ShapeDtypeStruct((rows, PROJ * WIDE), BF16),
        in_specs=[VMEM] * (len(query) + len(rest)),
        out_specs=VMEM,
        compiler_params=pltpu.CompilerParams(vmem_limit_bytes=LIMIT),
        cost_estimate=pl.CostEstimate(flops=10**6, bytes_accessed=10**6, transcendentals=0),
        name="place_sum",
    )(*query, *rest)


def shifted(blocks, axis):
    count = len(blocks)
    return [blocks[0]] + [
        lax.ppermute(blocks[d], axis, [(i, (i + d) % count) for i in range(count)])
        for d in range(1, count)
    ]


def per_device(
    node_feats,
    node_types,
    queries,
    key_rows,
    value_rows,
    halo_keys,
    halo_values,
    halo_rows,
    edge_tiles,
    grad_output,
    proj_weight,
    rel_weight,
    rel_prior,
):
    y_count = lax.axis_size("y")
    z_count = lax.axis_size("z")
    place = jnp.stack(
        [lax.axis_index("core"), lax.axis_index("y"), lax.axis_index("heads")]
    ).astype(jnp.int32)
    swap = [(0, 1), (1, 0)]
    own, send, rel = attend(
        edge_tiles.T,
        rel_prior.T,
        queries,
        grad_output,
        key_rows,
        value_rows,
        halo_keys,
        halo_values,
        rel_weight,
        halo_rows.reshape(-1, WIDE),
    )
    incoming = lax.all_to_all(send, ("y", "z", "core"), 0, 0, tiled=True)
    feats_t, sent, rel, rel_theirs = bundle(place, own, node_feats, node_types.reshape(-1, WIDE), rel)
    got = lax.ppermute(sent, "core", swap)
    rel_got = lax.ppermute(rel_theirs, "core", swap)
    pair, *q_blocks = project_queries(place, feats_t, sent, got, rel, rel_got, y_count)
    q_arrived = shifted(q_blocks, "y")
    own, *q_blocks = lax.optimization_barrier((own, *q_blocks))
    kv = collect(own, incoming)
    got_kv = lax.ppermute(kv, "core", swap)
    kv, *q_arrived = lax.optimization_barrier((kv, *q_arrived))
    rel_z = lax.all_to_all(relation_places(q_arrived, z_count), "z", 0, 0, tiled=True)
    arrived = shifted(project(place, pair, kv, got_kv, sent, got, y_count), "y")
    feat_blocks = features(place, sent, kv, proj_weight.reshape(PROJ, -1, WIDE))
    mine, partners, *away = feat_blocks
    away = [lax.ppermute(block, "heads", [(0, 1), (1, 0), (2, 3), (3, 2)]) for block in away]
    arrived[0], got_mine, got_partners = lax.optimization_barrier((arrived[0], *away))
    partners = partners.astype(F32) + got_partners.astype(F32)
    last = lax.ppermute(partners.astype(BF16), "heads", [(0, 3), (3, 0), (1, 2), (2, 1)])
    grad_feats = (mine.astype(F32) + got_mine.astype(F32) + last.astype(F32)).astype(BF16)
    by_y = place_sum(q_arrived, arrived)
    next_y = [(0, 1), (1, 0), (2, 3), (3, 2)]
    last_y = [(0, 3), (3, 0), (1, 2), (2, 1)]
    rel_z, by_y = lax.optimization_barrier((rel_z, by_y))
    by_z = lax.all_to_all(by_y.reshape(z_count, -1, PROJ * WIDE), "z", 0, 0, tiled=True)
    rel_mine, prior = relation_sum(rel_z)
    rel_first = lax.ppermute(rel_mine, "y", next_y)
    rel_last = lax.ppermute(jnp.stack([rel_mine, rel_first]), "y", last_y)
    blocks = (rel_mine, rel_first, rel_last)
    grad_rel = relations(place, *blocks, *(lax.ppermute(block, "core", swap) for block in blocks))
    by_z, grad_rel, grad_feats = lax.optimization_barrier((by_z, grad_rel, grad_feats))
    grad_proj = jnp.sum(by_z.astype(F32), axis=0).reshape(-1, 3, TYPES, WIDE)
    grad_prior = prior.T
    return (grad_feats, grad_proj, grad_rel, grad_prior)


def solution(mesh):
    heads = mesh.devices.shape[1]
    split = Mesh(mesh.devices.reshape(4, 8, 2, heads), ("y", "z", "core", "heads"))
    nodes = ("y", "z", "core")
    return jax.shard_map(
        per_device,
        mesh=split,
        in_specs=(
            P(nodes, None),
            P(nodes),
            P(nodes, "heads"),
            P(nodes, "heads"),
            P(nodes, "heads"),
            P(nodes, "heads"),
            P(nodes, "heads"),
            P(nodes),
            P(nodes, None),
            P(nodes, "heads"),
            P(None, None, None, "heads"),
            P(None, None, "heads", None, None),
            P(None, "heads"),
        ),
        out_specs=(
            P(nodes, "heads"),
            P(nodes, None, None, "heads"),
            P(None, None, "heads", None, None),
            P(None, "heads"),
        ),
        check_vma=False,
    )
```

```python
import jax
import jax.numpy as jnp
from jax import lax
from jax.experimental import pallas as pl
from jax.experimental.pallas import tpu as pltpu
from jax.sharding import Mesh, PartitionSpec as P

TYPES = 5
RELS = 15
TILE = 64
WIDE = 128
GROUP = 4
UNROLL = 6
PROJ = 3 * TYPES

F32 = jnp.float32
BF16 = jnp.bfloat16
NN = (((1,), (0,)), ((), ()))
NT = (((1,), (1,)), ((), ()))
TN = (((0,), (0,)), ((), ()))
VMEM = pl.BlockSpec(memory_space=pltpu.VMEM)
SMEM = pl.BlockSpec(memory_space=pltpu.SMEM)
HBM = pl.BlockSpec(memory_space=pltpu.HBM)
BLOCK = 24
REL_ROWS = 240
REL_BLOCK = 256
LIMIT = 24 * 2**20
MOST = 62 * 2**20


def mul(left, right, dims):
    return lax.dot_general(left, right, dims, preferred_element_type=F32)


def column(row):
    return jnp.transpose(jnp.broadcast_to(row, (WIDE, WIDE)), (1, 0))


def high_and_low(line):
    line = line + pltpu.roll(line, WIDE - 32, 1)
    high = line.astype(BF16).astype(F32)
    lane = lax.broadcasted_iota(jnp.int32, line.shape, 1)
    return jnp.where(lane < 32, high, pltpu.roll(line - high, 32, 1))


def with_line(block):
    row = lax.broadcasted_iota(jnp.int32, block.shape, 0)
    return jnp.where(row == REL_ROWS, high_and_low(block[REL_ROWS : REL_ROWS + 1, :]), block)


def attend_kernel(
    edges_hbm, prior_hbm, q_hbm, g_hbm, ko_hbm, vo_hbm, kh_hbm, vh_hbm, rel_hbm, rows_hbm,
    pack_out, send_out,
    edges, listed, prior_in, q_ref, g_ref, rel_ref, rows_ref, k_ref, v_ref, sems,
    wbd, qg, keep, prior, kvm, probs, exps, logs, grads,
    denom, delta, dprior, dkv, dwk, dwv, dq, drel, ids_ref,
):
    count = edges.shape[1]
    places = kvm.shape[0]
    own = ko_hbm.shape[0]
    dests = own // TILE
    own_tiles = own // TILE
    halo_tiles = kh_hbm.shape[0] // TILE
    copies = [
        pltpu.make_async_copy(source, target, sems.at[i])
        for i, (source, target) in enumerate(
            (
                (rel_hbm, rel_ref),
                (q_hbm, q_ref),
                (g_hbm, g_ref),
                (rows_hbm, rows_ref),
                (edges_hbm, edges),
                (prior_hbm, prior_in),
                (ko_hbm, k_ref.at[:own]),
                (vo_hbm, v_ref.at[:own]),
                (kh_hbm, k_ref.at[own:]),
                (vh_hbm, v_ref.at[own:]),
            )
        )
    ]
    copies[4].start()
    for i, copy in enumerate(copies):
        if i != 4:
            copy.start()

    lane = lax.broadcasted_iota(jnp.int32, (TILE, WIDE), 1)
    first = lane < TILE
    wbd[...] = jnp.zeros_like(wbd)
    denom[...] = jnp.zeros_like(denom)
    delta[...] = jnp.zeros_like(delta)
    dprior[...] = jnp.zeros_like(dprior)
    dkv[...] = jnp.zeros_like(dkv)
    dwk[...] = jnp.zeros_like(dwk)
    dwv[...] = jnp.zeros_like(dwv)
    dq[...] = jnp.zeros_like(dq)
    copies[4].wait()
    for i in range(listed.shape[0]):
        listed[i] = 0
    targets = [edges[0, e] for e in range(count)]
    sizes = [sum((target == a).astype(jnp.int32) for target in targets) for a in range(dests)]
    starts = [jnp.int32(0)]
    for a in range(dests):
        starts.append(starts[a] + (sizes[a] + GROUP - 1) // GROUP * GROUP)
    heads = list(starts[:dests])
    for e, target in enumerate(targets):
        at = jnp.int32(places)
        for a in range(dests):
            at = jnp.where(target == a, heads[a], at)
            heads[a] = heads[a] + (target == a).astype(jnp.int32)
        listed[at] = 256 + 16 * edges[1, e] + edges[2, e]
    used = starts[dests] // GROUP

    copies[1].wait()
    copies[2].wait()
    none = jnp.zeros((TILE, WIDE), BF16)
    for a in range(dests):
        q = q_ref[a * TILE : (a + 1) * TILE, :].astype(F32) * 0.125
        g = g_ref[a * TILE : (a + 1) * TILE, :].astype(F32)
        for h in range(2):
            mine = first if h == 0 else jnp.logical_not(first)
            qg[a, h * TILE : (h + 1) * TILE, :WIDE] = jnp.where(mine, q, 0.0).astype(BF16)
            qg[a, h * TILE : (h + 1) * TILE, WIDE:] = none
            qg[a, (2 + h) * TILE : (3 + h) * TILE, :WIDE] = none
            qg[a, (2 + h) * TILE : (3 + h) * TILE, WIDE:] = jnp.where(mine, g, 0.0).astype(BF16)
    copies[3].wait()
    for b in range(own_tiles):
        keep[b] = jnp.ones((TILE, WIDE), F32)
    period = lax.broadcasted_iota(jnp.int32, (16, 8, WIDE), 2) % 8
    slot = lax.broadcasted_iota(jnp.int32, (16, 8, WIDE), 1)
    for j in range(halo_tiles // 2):
        ids = column(rows_ref[j : j + 1, :].astype(F32))
        ok = (ids < float(own)).astype(F32)
        keep[own_tiles + 2 * j] = ok[:TILE]
        keep[own_tiles + 2 * j + 1] = ok[TILE:]
        tiled = jnp.sum(jnp.where(period == slot, ids.reshape(16, 8, WIDE), 0.0), axis=1)
        ids_ref[16 * j : 16 * j + 16, :] = tiled
    copies[5].wait()
    one_lane = lax.broadcasted_iota(jnp.int32, (1, WIDE), 1)
    for r in range(RELS):
        prior[r : r + 1, :] = jnp.where(one_lane < TILE, prior_in[0, r], prior_in[1, r])
    copies[0].wait()
    for r in range(RELS):
        for w in range(2):
            for h in range(2):
                at = (2 * w + h) * TILE
                wbd[r, at : at + TILE, at : at + TILE] = rel_ref[w, r, h]
    for copy in copies[6:]:
        copy.wait()

    def entry(i):
        code = listed[i]
        return (code >> 4) & 15, code & 15, (code >= 256).astype(F32)

    def rows(b):
        return pl.ds(pl.multiple_of(b * TILE, TILE), TILE)

    def tile_of(group):
        at = group * GROUP
        return sum((at >= starts[a]).astype(jnp.int32) for a in range(1, dests))

    def scores(group):
        i = group * GROUP
        a = tile_of(group)
        parts = []
        for u in range(GROUP):
            b, r, live = entry(i + u)
            pair = jnp.concatenate([k_ref[rows(b), :], v_ref[rows(b), :]], axis=1)
            parts.append(mul(pair, wbd[r], NN).astype(BF16))
        mixed = jnp.concatenate(parts, axis=0)
        kvm[pl.ds(i, GROUP)] = mixed[:, :WIDE].reshape(GROUP, TILE, WIDE)
        both = mul(mixed, qg[a], NT)
        logs[pl.ds(i, GROUP)] = both[:, :WIDE].reshape(GROUP, TILE, WIDE)
        grads[pl.ds(i, GROUP)] = both[:, WIDE:].reshape(GROUP, TILE, WIDE)
        total = None
        for u in range(GROUP):
            b, r, live = entry(i + u)
            ex = jnp.exp(prior[pl.ds(r, 1), :] * both[u * TILE : (u + 1) * TILE, :WIDE]) * (keep[b] * live)
            exps[i + u] = ex
            total = ex if total is None else total + ex
        denom[a] += jnp.sum(total, axis=0, keepdims=True)

    def normalise(group):
        i = group * GROUP
        a = tile_of(group)
        total = None
        for u in range(GROUP):
            soft = exps[i + u] * denom[a]
            exps[i + u] = soft
            prob = soft.astype(BF16)
            probs[i + u] = prob
            term = prob.astype(F32) * grads[i + u]
            total = term if total is None else total + term
        delta[a] += jnp.sum(total, axis=0, keepdims=True)

    def backward(group):
        i = group * GROUP
        a = tile_of(group)
        parts = []
        for u in range(GROUP):
            b, r, live = entry(i + u)
            score_grad = exps[i + u] * (grads[i + u] - delta[a])
            dprior[pl.ds(r, 1), :] += jnp.sum(score_grad * logs[i + u], axis=0, keepdims=True)
            parts.append((score_grad * prior[pl.ds(r, 1), :]).astype(BF16))
        lgrad = jnp.concatenate(parts, axis=0)
        pair = jnp.concatenate([lgrad, probs[pl.ds(i, GROUP)].reshape(GROUP * TILE, WIDE)], axis=1)
        mixed_grad = mul(pair, qg[a], NN).astype(BF16)
        dq[a] += mul(lgrad, kvm[pl.ds(i, GROUP)].reshape(GROUP * TILE, WIDE), TN)
        for u in range(GROUP):
            b, r, live = entry(i + u)
            part = mixed_grad[u * TILE : (u + 1) * TILE]
            dkv[b] += mul(part, wbd[r], NT)
            dwk[r] += mul(k_ref[rows(b), :], part[:, :WIDE], TN)
            dwv[r] += mul(v_ref[rows(b), :], part[:, WIDE:], TN)

    def sweep(work):
        def some(step, carry):
            for u in range(UNROLL):
                work(step * UNROLL + u)
            return carry

        lax.fori_loop(0, (used + UNROLL - 1) // UNROLL, some, 0)

    sweep(scores)
    denom[...] = 1.0 / denom[...]
    sweep(normalise)
    sweep(backward)

    at_own = 2 * (dests * REL_BLOCK)
    for a in range(dests):
        grad = jnp.where(first, dq[a, :TILE, :], dq[a, TILE:, :]) * 0.125
        at = at_own + a * TILE
        pack_out[at : at + TILE, :] = grad.astype(BF16)
    for b in range(own_tiles):
        for w in range(2):
            at = at_own + (1 + w) * own + b * TILE
            pack_out[at : at + TILE, :] = dkv[b, :, w * WIDE : (w + 1) * WIDE].astype(BF16)
    for b in range(halo_tiles):
        back = dkv[own_tiles + b]
        block = jnp.concatenate(
            [
                back[:, :WIDE].reshape(8, 8, WIDE),
                back[:, WIDE:].reshape(8, 8, WIDE),
                jnp.broadcast_to(ids_ref[8 * b : 8 * b + 8, :].reshape(8, 1, WIDE), (8, 8, WIDE)),
            ],
            axis=1,
        )
        send_out[8 * b : 8 * b + 8] = block.astype(BF16)
    for w, ref in enumerate((dwk, dwv)):
        for r in range(RELS):
            at = (w * RELS + r) * TILE
            drel[at : at + TILE, :] = jnp.where(first, ref[r, :TILE, :], ref[r, TILE:, :])
    sums = dprior[...]
    spot = lax.broadcasted_iota(jnp.int32, sums.shape, 1)
    row = lax.broadcasted_iota(jnp.int32, sums.shape, 0)
    one = jnp.sum(jnp.where(spot < TILE, sums, 0.0), axis=1, keepdims=True)
    two = jnp.sum(jnp.where(spot < TILE, 0.0, sums), axis=1, keepdims=True)
    chosen = jnp.where((spot // 16) % 2 == 0, one, two)
    line = jnp.sum(jnp.where(spot % 16 == row, chosen, 0.0), axis=0, keepdims=True)
    high = line.astype(BF16).astype(F32)
    line = jnp.where(one_lane < 32, high, line - high)
    tail = jnp.where(lax.broadcasted_iota(jnp.int32, (16, WIDE), 0) == 0, line, 0.0).astype(BF16)
    for w in range(2):
        for y in range(dests):
            at = (w * dests + y) * REL_ROWS
            to = (w * dests + y) * REL_BLOCK
            pack_out[to : to + REL_ROWS, :] = drel[at : at + REL_ROWS, :].astype(BF16)
            pack_out[to + REL_ROWS : to + REL_BLOCK, :] = tail


def attend(edges, rel_prior, queries, grad_output, key_rows, value_rows, halo_keys, halo_values, rel_weight, halo_rows):
    rows = queries.shape[0]
    halo = halo_keys.shape[0]
    dests = rows // TILE
    sources = (rows + halo) // TILE
    count = edges.shape[1]
    groups = -(-(count // GROUP + dests - 1) // UNROLL) * UNROLL
    places = groups * GROUP
    slabs = 64
    return pl.pallas_call(
        attend_kernel,
        out_shape=(
            jax.ShapeDtypeStruct((2 * dests * REL_BLOCK + 3 * rows, WIDE), BF16),
            jax.ShapeDtypeStruct((slabs, BLOCK, WIDE), BF16),
        ),
        in_specs=[HBM] * 10,
        out_specs=(VMEM,) * 2,
        scratch_shapes=[
            pltpu.SMEM(edges.shape, jnp.int32),
            pltpu.SMEM((places + 1,), jnp.int32),
            pltpu.SMEM(rel_prior.shape, F32),
            pltpu.VMEM(queries.shape, BF16),
            pltpu.VMEM(grad_output.shape, BF16),
            pltpu.VMEM(rel_weight.shape, BF16),
            pltpu.VMEM(halo_rows.shape, jnp.int32),
            pltpu.VMEM((rows + halo, WIDE), BF16),
            pltpu.VMEM((rows + halo, WIDE), BF16),
            pltpu.SemaphoreType.DMA((10,)),
            pltpu.VMEM((RELS, 2 * WIDE, 2 * WIDE), BF16),
            pltpu.VMEM((dests, 2 * WIDE, 2 * WIDE), BF16),
            pltpu.VMEM((sources, TILE, WIDE), F32),
            pltpu.VMEM((16, WIDE), F32),
            pltpu.VMEM((places, TILE, WIDE), BF16),
            pltpu.VMEM((places, TILE, WIDE), BF16),
            pltpu.VMEM((places, TILE, WIDE), F32),
            pltpu.VMEM((places, TILE, WIDE), F32),
            pltpu.VMEM((places, TILE, WIDE), F32),
            pltpu.VMEM((dests, 1, WIDE), F32),
            pltpu.VMEM((dests, 1, WIDE), F32),
            pltpu.VMEM((16, WIDE), F32),
            pltpu.VMEM((sources, TILE, 2 * WIDE), F32),
            pltpu.VMEM((RELS, WIDE, WIDE), F32),
            pltpu.VMEM((RELS, WIDE, WIDE), F32),
            pltpu.VMEM((dests, WIDE, WIDE), F32),
            pltpu.VMEM((2 * RELS * TILE, WIDE), F32),
            pltpu.VMEM((slabs, WIDE), F32),
        ],
        compiler_params=pltpu.CompilerParams(vmem_limit_bytes=MOST),
        cost_estimate=pl.CostEstimate(flops=3 * 10**9, bytes_accessed=4 * 10**6, transcendentals=400000),
        name="attend",
    )(edges, rel_prior, queries, grad_output, key_rows, value_rows, halo_keys, halo_values, rel_weight, halo_rows)


def bundle_kernel(place, pack_ref, nf_ref, types_ref, mine_out, send_out, own_out, keep_out, rel_out):
    half = rel_out.shape[0]
    for out, core in ((rel_out, 1 - place[0]), (keep_out, place[0])):
        out[...] = pack_ref[pl.ds(pl.multiple_of(core * half, half), half), :]
    rows, feats = nf_ref.shape
    turned = jnp.transpose(nf_ref[...], (1, 0)).astype(F32).reshape(feats // 16, 2, 8, rows)
    low = turned[:, 0].reshape(feats // 2, rows)
    high = turned[:, 1].reshape(feats // 2, rows)
    even = place[0] == 0
    mine_out[...] = jnp.where(even, low, high).astype(BF16)
    send_out[:, :rows] = jnp.where(even, high, low).astype(BF16)
    for j in range(rows // WIDE):
        kinds = column(types_ref[j : j + 1, :].astype(F32)).astype(BF16)
        send_out[j * WIDE : (j + 1) * WIDE, rows + WIDE :] = kinds
    send_out[:, rows : rows + WIDE] = pack_ref[2 * half : 2 * half + rows, :]
    for w in range(2):
        at = 2 * half + (1 + w) * rows
        own_out[:, w * WIDE : (w + 1) * WIDE] = pack_ref[at : at + rows, :]


def bundle(place, pack, node_feats, node_types):
    rows, feats = node_feats.shape
    half = (pack.shape[0] - 3 * rows) // 2
    return pl.pallas_call(
        bundle_kernel,
        out_shape=(
            jax.ShapeDtypeStruct((feats // 2, rows), BF16),
            jax.ShapeDtypeStruct((feats // 2, rows + 2 * WIDE), BF16),
            jax.ShapeDtypeStruct((rows, 2 * WIDE), BF16),
            jax.ShapeDtypeStruct((half, WIDE), BF16),
            jax.ShapeDtypeStruct((half, WIDE), BF16),
        ),
        in_specs=[SMEM] + [VMEM] * 3,
        out_specs=(VMEM,) * 5,
        compiler_params=pltpu.CompilerParams(vmem_limit_bytes=LIMIT),
        cost_estimate=pl.CostEstimate(flops=10**6, bytes_accessed=2 * 10**6, transcendentals=0),
        name="bundle",
    )(place, pack, node_feats, node_types)


def spread(place, products, outs):
    size = outs[0].shape[0]
    for d in range(len(outs)):
        block = lax.rem(place[1] + d, len(outs))
        outs[d][:, : products.shape[1]] = products[pl.ds(pl.multiple_of(block * size, size), size), :]


def project_queries_kernel(place, mine_ref, sent_ref, got_ref, rel_ref, rel_got_ref, pair_out, *refs):
    outs, products = refs[:-1], refs[-1]
    rows = mine_ref.shape[1]
    pair_out[:, :rows] = mine_ref[...]
    pair_out[:, rows:] = got_ref[:, :rows]
    query = jnp.concatenate([ref[:, rows : rows + WIDE] for ref in (sent_ref, got_ref)], axis=0).astype(F32)
    kinds = jnp.concatenate([ref[:, rows + WIDE :] for ref in (sent_ref, got_ref)], axis=0).astype(F32)
    for t in range(TYPES):
        masked = jnp.where(kinds == float(t), query, 0.0).astype(BF16)
        products[:, t * WIDE : (t + 1) * WIDE] = mul(pair_out[...], masked, NN).astype(BF16)
    spread(place, products, outs)
    for d in range(len(outs)):
        block = lax.rem(place[1] + d, len(outs))
        here = pl.ds(pl.multiple_of(block * REL_BLOCK, REL_BLOCK), REL_BLOCK)
        both = with_line(rel_ref[here, :].astype(F32) + rel_got_ref[here, :].astype(F32)).astype(BF16)
        for k in range(REL_BLOCK // TILE):
            at = (TYPES + k) * WIDE
            outs[d][:, at : at + WIDE] = both[k * TILE : (k + 1) * TILE, :]


def project_queries(place, mine, sent, got, rel, rel_got, count):
    feats, rows = mine.shape
    wide = TYPES * WIDE
    more = REL_BLOCK // TILE * WIDE
    return pl.pallas_call(
        project_queries_kernel,
        out_shape=(jax.ShapeDtypeStruct((feats, 2 * rows), BF16),)
        + (jax.ShapeDtypeStruct((feats // count, wide + more), BF16),) * count,
        in_specs=[SMEM] + [VMEM] * 5,
        out_specs=(VMEM,) * (1 + count),
        scratch_shapes=[pltpu.VMEM((feats, wide), BF16)],
        compiler_params=pltpu.CompilerParams(vmem_limit_bytes=LIMIT),
        cost_estimate=pl.CostEstimate(flops=10**9, bytes_accessed=2 * 10**6, transcendentals=0),
        name="project_queries",
    )(place, mine, sent, got, rel, rel_got)


def collect_kernel(own_ref, inc_ref, kv_out):
    rows = own_ref.shape[0]
    slabs = inc_ref.shape[0]
    row = lax.broadcasted_iota(jnp.int32, (16, WIDE), 0)
    block = lax.broadcasted_iota(jnp.int32, (16, WIDE), 1) // 8
    node = lax.broadcasted_iota(jnp.int32, (rows, WIDE), 0).astype(F32)
    back = own_ref[...].astype(F32)
    for c in range(slabs // 16):
        grads = inc_ref[16 * c : 16 * c + 16].astype(F32)
        ids = grads[:, 16, :]
        line = jnp.sum(jnp.where(row == block, ids, 0.0), axis=0, keepdims=True)
        pick = (node == line).astype(F32).astype(BF16)
        both = jnp.concatenate(
            [grads[:, :8].reshape(WIDE, WIDE), grads[:, 8:16].reshape(WIDE, WIDE)], axis=1
        )
        back = back + mul(pick, both.astype(BF16), NN)
    kv_out[...] = back.astype(BF16)


def collect(own, incoming):
    rows = own.shape[0]
    return pl.pallas_call(
        collect_kernel,
        out_shape=jax.ShapeDtypeStruct((rows, 2 * WIDE), BF16),
        in_specs=[VMEM, VMEM],
        out_specs=VMEM,
        compiler_params=pltpu.CompilerParams(vmem_limit_bytes=LIMIT),
        cost_estimate=pl.CostEstimate(flops=10**8, bytes_accessed=10**6, transcendentals=0),
        name="collect",
    )(own, incoming)


def relation_places_kernel(*refs):
    out = refs[-1]
    parts = []
    for k in range(REL_BLOCK // TILE):
        at = (TYPES + k) * WIDE
        total = refs[0][:, at : at + WIDE].astype(F32)
        for ref in refs[1:-1]:
            total = total + ref[:, at : at + WIDE].astype(F32)
        parts.append(total)
    total = with_line(jnp.concatenate(parts, axis=0)).astype(BF16)
    for z in range(out.shape[0]):
        out[z] = total


def relation_places(arrived, count):
    return pl.pallas_call(
        relation_places_kernel,
        out_shape=jax.ShapeDtypeStruct((count, REL_BLOCK, WIDE), BF16),
        in_specs=[VMEM] * len(arrived),
        out_specs=VMEM,
        compiler_params=pltpu.CompilerParams(vmem_limit_bytes=LIMIT),
        cost_estimate=pl.CostEstimate(flops=10**6, bytes_accessed=10**6, transcendentals=0),
        name="relation_places",
    )(*arrived)


def relation_sum_kernel(inc_ref, rel_out, prior_out):
    total = inc_ref[0].astype(F32)
    for s in range(1, inc_ref.shape[0]):
        total = total + inc_ref[s].astype(F32)
    rel_out[...] = total.astype(BF16)
    line = total[REL_ROWS : REL_ROWS + 1, :]
    line = line + pltpu.roll(line, WIDE - 32, 1)
    prior_out[0:1, :] = line[:, :RELS]
    prior_out[1:2, :] = pltpu.roll(line, WIDE - 16, 1)[:, :RELS]


def relation_sum(incoming):
    return pl.pallas_call(
        relation_sum_kernel,
        out_shape=(
            jax.ShapeDtypeStruct(incoming.shape[1:], BF16),
            jax.ShapeDtypeStruct((2, RELS), F32),
        ),
        in_specs=[VMEM],
        out_specs=(VMEM,) * 2,
        compiler_params=pltpu.CompilerParams(vmem_limit_bytes=LIMIT),
        cost_estimate=pl.CostEstimate(flops=10**6, bytes_accessed=10**6, transcendentals=0),
        name="relation_sum",
    )(incoming)


def project_kernel(place, pair_ref, kv_ref, got_kv_ref, sent_ref, got_ref, *refs):
    outs, products = refs[:-1], refs[-1]
    rows = kv_ref.shape[0]
    kinds = jnp.concatenate([ref[:, rows + WIDE :] for ref in (sent_ref, got_ref)], axis=0).astype(F32)
    for p in range(2):
        part = jnp.concatenate(
            [ref[:, p * WIDE : (p + 1) * WIDE] for ref in (kv_ref, got_kv_ref)], axis=0
        ).astype(F32)
        for t in range(TYPES):
            at = (p * TYPES + t) * WIDE
            masked = jnp.where(kinds == float(t), part, 0.0).astype(BF16)
            products[:, at : at + WIDE] = mul(pair_ref[...], masked, NN).astype(BF16)
    spread(place, products, outs)


def project(place, pair, kv, got_kv, sent, got, count):
    feats = pair.shape[0]
    wide = 2 * TYPES * WIDE
    return pl.pallas_call(
        project_kernel,
        out_shape=(jax.ShapeDtypeStruct((feats // count, wide), BF16),) * count,
        in_specs=[SMEM] + [VMEM] * 5,
        out_specs=(VMEM,) * count,
        scratch_shapes=[pltpu.VMEM((feats, wide), BF16)],
        compiler_params=pltpu.CompilerParams(vmem_limit_bytes=LIMIT),
        cost_estimate=pl.CostEstimate(flops=10**9, bytes_accessed=4 * 10**6, transcendentals=0),
        name="project",
    )(place, pair, kv, got_kv, sent, got)


def features_kernel(place, sent_ref, kv_ref, w_ref, *refs):
    outs, total = refs[:-1], refs[-1]
    rows = kv_ref.shape[0]
    kinds = sent_ref[:, rows + WIDE :].astype(F32)
    acc = None
    for p in range(3):
        part = sent_ref[:, rows : rows + WIDE] if p == 0 else kv_ref[:, (p - 1) * WIDE : p * WIDE]
        part = part.astype(F32)
        for t in range(TYPES):
            masked = jnp.where(kinds == float(t), part, 0.0).astype(BF16)
            term = mul(masked, w_ref[p * TYPES + t], NT)
            acc = term if acc is None else acc + term
    for h in range(len(outs)):
        total[h] = acc[:, h * WIDE : (h + 1) * WIDE]
    me = place[2]
    first = me + 1 - 2 * lax.rem(me, 2)
    for out, owner in zip(outs, (me, 3 - me, first, 3 - first)):
        out[...] = total[owner].astype(BF16)


def features(place, sent, kv, weights):
    rows = kv.shape[0]
    count = weights.shape[1] // WIDE
    return pl.pallas_call(
        features_kernel,
        out_shape=(jax.ShapeDtypeStruct((rows, WIDE), BF16),) * count,
        in_specs=[SMEM, VMEM, VMEM, VMEM],
        out_specs=(VMEM,) * count,
        scratch_shapes=[pltpu.VMEM((count, rows, WIDE), F32)],
        compiler_params=pltpu.CompilerParams(vmem_limit_bytes=LIMIT),
        cost_estimate=pl.CostEstimate(flops=10**9, bytes_accessed=3 * 10**6, transcendentals=0),
        name="features",
    )(place, sent, kv, weights)


def relation_kernel(place, mine_ref, first_ref, last_ref, c_mine_ref, c_first_ref, c_last_ref, out_ref, flat):
    y = place[1]
    last = 3 - y
    owners = (y, y + 1 - 2 * lax.rem(y, 2), last, last + 1 - 2 * lax.rem(last, 2))
    for core, refs in (
        (place[0], (mine_ref, first_ref, last_ref.at[0], last_ref.at[1])),
        (1 - place[0], (c_mine_ref, c_first_ref, c_last_ref.at[0], c_last_ref.at[1])),
    ):
        for owner, ref in zip(owners, refs):
            at = pl.multiple_of((core * len(owners) + owner) * REL_ROWS, 16)
            flat[pl.ds(at, REL_ROWS), :] = ref[:REL_ROWS, :].astype(F32)
    for w in range(2):
        for r in range(RELS):
            at = (w * RELS + r) * TILE
            for h in range(2):
                out_ref[w, r, h] = flat[at : at + TILE, h * TILE : (h + 1) * TILE]


def relations(place, *blocks):
    return pl.pallas_call(
        relation_kernel,
        out_shape=jax.ShapeDtypeStruct((2, RELS, 2, TILE, TILE), F32),
        in_specs=[SMEM] + [VMEM] * 6,
        out_specs=VMEM,
        scratch_shapes=[pltpu.VMEM((2 * RELS * TILE, WIDE), F32)],
        compiler_params=pltpu.CompilerParams(vmem_limit_bytes=LIMIT),
        cost_estimate=pl.CostEstimate(flops=10**6, bytes_accessed=3 * 10**6, transcendentals=0),
        name="relations",
    )(place, *blocks)


def place_sum_kernel(*refs):
    out = refs[-1]
    half = (len(refs) - 1) // 2
    narrow = TYPES * WIDE
    for at, group in ((0, refs[:half]), (narrow, refs[half:-1])):
        width = narrow if at == 0 else group[0].shape[1]
        total = group[0][:, :width].astype(F32)
        for ref in group[1:]:
            total = total + ref[:, :width].astype(F32)
        out[:, at : at + width] = total.astype(BF16)


def place_sum(query, rest):
    rows = query[0].shape[0]
    return pl.pallas_call(
        place_sum_kernel,
        out_shape=jax.ShapeDtypeStruct((rows, PROJ * WIDE), BF16),
        in_specs=[VMEM] * (len(query) + len(rest)),
        out_specs=VMEM,
        compiler_params=pltpu.CompilerParams(vmem_limit_bytes=LIMIT),
        cost_estimate=pl.CostEstimate(flops=10**6, bytes_accessed=10**6, transcendentals=0),
        name="place_sum",
    )(*query, *rest)


def shifted(blocks, axis):
    count = len(blocks)
    return [blocks[0]] + [
        lax.ppermute(blocks[d], axis, [(i, (i + d) % count) for i in range(count)])
        for d in range(1, count)
    ]


def per_device(
    node_feats,
    node_types,
    queries,
    key_rows,
    value_rows,
    halo_keys,
    halo_values,
    halo_rows,
    edge_tiles,
    grad_output,
    proj_weight,
    rel_weight,
    rel_prior,
):
    y_count = lax.axis_size("y")
    z_count = lax.axis_size("z")
    place = jnp.stack(
        [lax.axis_index("core"), lax.axis_index("y"), lax.axis_index("heads")]
    ).astype(jnp.int32)
    swap = [(0, 1), (1, 0)]
    pack, send = attend(
        edge_tiles.T,
        rel_prior.T,
        queries,
        grad_output,
        key_rows,
        value_rows,
        halo_keys,
        halo_values,
        rel_weight,
        halo_rows.reshape(-1, WIDE),
    )
    incoming = lax.all_to_all(send, ("y", "z", "core"), 0, 0, tiled=True)
    feats_t, sent, own, rel, rel_theirs = bundle(place, pack, node_feats, node_types.reshape(-1, WIDE))
    got = lax.ppermute(sent, "core", swap)
    rel_got = lax.ppermute(rel_theirs, "core", swap)
    pair, *q_blocks = project_queries(place, feats_t, sent, got, rel, rel_got, y_count)
    q_arrived = shifted(q_blocks, "y")
    own, *q_blocks = lax.optimization_barrier((own, *q_blocks))
    kv = collect(own, incoming)
    got_kv = lax.ppermute(kv, "core", swap)
    got_kv, *q_arrived = lax.optimization_barrier((got_kv, *q_arrived))
    rel_z = lax.all_to_all(relation_places(q_arrived, z_count), "z", 0, 0, tiled=True)
    arrived = shifted(project(place, pair, kv, got_kv, sent, got, y_count), "y")
    feat_blocks = features(place, sent, kv, proj_weight.reshape(PROJ, -1, WIDE))
    mine, partners, *away = feat_blocks
    away = [lax.ppermute(block, "heads", [(0, 1), (1, 0), (2, 3), (3, 2)]) for block in away]
    arrived[0], got_mine, got_partners = lax.optimization_barrier((arrived[0], *away))
    partners = partners.astype(F32) + got_partners.astype(F32)
    last = lax.ppermute(partners.astype(BF16), "heads", [(0, 3), (3, 0), (1, 2), (2, 1)])
    grad_feats = (mine.astype(F32) + got_mine.astype(F32) + last.astype(F32)).astype(BF16)
    by_y = place_sum(q_arrived, arrived)
    next_y = [(0, 1), (1, 0), (2, 3), (3, 2)]
    last_y = [(0, 3), (3, 0), (1, 2), (2, 1)]
    rel_z, by_y = lax.optimization_barrier((rel_z, by_y))
    by_z = lax.all_to_all(by_y.reshape(z_count, -1, PROJ * WIDE), "z", 0, 0, tiled=True)
    rel_mine, prior = relation_sum(rel_z)
    rel_first = lax.ppermute(rel_mine, "y", next_y)
    rel_last = lax.ppermute(jnp.stack([rel_mine, rel_first]), "y", last_y)
    blocks = (rel_mine, rel_first, rel_last)
    grad_rel = relations(place, *blocks, *(lax.ppermute(block, "core", swap) for block in blocks))
    by_z, grad_rel, grad_feats = lax.optimization_barrier((by_z, grad_rel, grad_feats))
    grad_proj = jnp.sum(by_z.astype(F32), axis=0).reshape(-1, 3, TYPES, WIDE)
    grad_prior = prior.T
    return (grad_feats, grad_proj, grad_rel, grad_prior)


def solution(mesh):
    heads = mesh.devices.shape[1]
    split = Mesh(mesh.devices.reshape(4, 8, 2, heads), ("y", "z", "core", "heads"))
    nodes = ("y", "z", "core")
    return jax.shard_map(
        per_device,
        mesh=split,
        in_specs=(
            P(nodes, None),
            P(nodes),
            P(nodes, "heads"),
            P(nodes, "heads"),
            P(nodes, "heads"),
            P(nodes, "heads"),
            P(nodes, "heads"),
            P(nodes),
            P(nodes, None),
            P(nodes, "heads"),
            P(None, None, None, "heads"),
            P(None, None, "heads", None, None),
            P(None, "heads"),
        ),
        out_specs=(
            P(nodes, "heads"),
            P(nodes, None, None, "heads"),
            P(None, None, "heads", None, None),
            P(None, "heads"),
        ),
        check_vma=False,
    )
```

```python
import jax
import jax.numpy as jnp
from jax import lax
from jax.experimental import pallas as pl
from jax.experimental.pallas import tpu as pltpu
from jax.sharding import Mesh, PartitionSpec as P

TYPES = 5
RELS = 15
TILE = 64
WIDE = 128
GROUP = 4
UNROLL = 6
EARLY = 4
PROJ = 3 * TYPES

F32 = jnp.float32
BF16 = jnp.bfloat16
NN = (((1,), (0,)), ((), ()))
NT = (((1,), (1,)), ((), ()))
TN = (((0,), (0,)), ((), ()))
VMEM = pl.BlockSpec(memory_space=pltpu.VMEM)
SMEM = pl.BlockSpec(memory_space=pltpu.SMEM)
HBM = pl.BlockSpec(memory_space=pltpu.HBM)
BLOCK = 24
REL_ROWS = 240
REL_BLOCK = 256
LIMIT = 24 * 2**20
MOST = 62 * 2**20


def mul(left, right, dims):
    return lax.dot_general(left, right, dims, preferred_element_type=F32)


def column(row):
    return jnp.transpose(jnp.broadcast_to(row, (WIDE, WIDE)), (1, 0))


def high_and_low(line):
    line = line + pltpu.roll(line, WIDE - 32, 1)
    high = line.astype(BF16).astype(F32)
    lane = lax.broadcasted_iota(jnp.int32, line.shape, 1)
    return jnp.where(lane < 32, high, pltpu.roll(line - high, 32, 1))


def with_line(block):
    row = lax.broadcasted_iota(jnp.int32, block.shape, 0)
    return jnp.where(row == REL_ROWS, high_and_low(block[REL_ROWS : REL_ROWS + 1, :]), block)


def attend_kernel(
    edges_hbm, prior_hbm, q_hbm, g_hbm, ko_hbm, vo_hbm, kh_hbm, vh_hbm, rel_hbm, rows_hbm,
    pack_out, send_out,
    edges, listed, prior_in, q_ref, g_ref, rel_ref, rows_ref, k_ref, v_ref, sems,
    wbd, qg, keep, prior, kvm, probs, exps, logs, grads,
    denom, delta, dprior, dkv, dwk, dwv, dq, drel, ids_ref,
):
    count = edges.shape[1]
    places = kvm.shape[0]
    own = ko_hbm.shape[0]
    dests = own // TILE
    own_tiles = own // TILE
    halo_tiles = kh_hbm.shape[0] // TILE
    copies = [
        pltpu.make_async_copy(source, target, sems.at[i])
        for i, (source, target) in enumerate(
            (
                (rel_hbm, rel_ref),
                (q_hbm, q_ref),
                (g_hbm, g_ref),
                (rows_hbm, rows_ref),
                (edges_hbm, edges),
                (prior_hbm, prior_in),
                (ko_hbm, k_ref.at[:own]),
                (vo_hbm, v_ref.at[:own]),
                (kh_hbm, k_ref.at[own:]),
                (vh_hbm, v_ref.at[own:]),
            )
        )
    ]
    copies[4].start()
    for i, copy in enumerate(copies):
        if i != 4:
            copy.start()

    lane = lax.broadcasted_iota(jnp.int32, (TILE, WIDE), 1)
    first = lane < TILE
    wbd[...] = jnp.zeros_like(wbd)
    denom[...] = jnp.zeros_like(denom)
    delta[...] = jnp.zeros_like(delta)
    dprior[...] = jnp.zeros_like(dprior)
    dkv[...] = jnp.zeros_like(dkv)
    dwk[...] = jnp.zeros_like(dwk)
    dwv[...] = jnp.zeros_like(dwv)
    dq[...] = jnp.zeros_like(dq)
    copies[4].wait()
    for i in range(listed.shape[0]):
        listed[i] = 0
    targets = [edges[0, e] for e in range(count)]
    sizes = [sum((target == a).astype(jnp.int32) for target in targets) for a in range(dests)]
    starts = [jnp.int32(0)]
    for a in range(dests):
        starts.append(starts[a] + (sizes[a] + GROUP - 1) // GROUP * GROUP)
    heads = list(starts[:dests])
    for e, target in enumerate(targets):
        at = jnp.int32(places)
        for a in range(dests):
            at = jnp.where(target == a, heads[a], at)
            heads[a] = heads[a] + (target == a).astype(jnp.int32)
        listed[at] = 256 + 16 * edges[1, e] + edges[2, e]
    used = starts[dests] // GROUP

    copies[1].wait()
    copies[2].wait()
    none = jnp.zeros((TILE, WIDE), BF16)
    for a in range(dests):
        q = q_ref[a * TILE : (a + 1) * TILE, :].astype(F32) * 0.125
        g = g_ref[a * TILE : (a + 1) * TILE, :].astype(F32)
        for h in range(2):
            mine = first if h == 0 else jnp.logical_not(first)
            qg[a, h * TILE : (h + 1) * TILE, :WIDE] = jnp.where(mine, q, 0.0).astype(BF16)
            qg[a, h * TILE : (h + 1) * TILE, WIDE:] = none
            qg[a, (2 + h) * TILE : (3 + h) * TILE, :WIDE] = none
            qg[a, (2 + h) * TILE : (3 + h) * TILE, WIDE:] = jnp.where(mine, g, 0.0).astype(BF16)
    copies[3].wait()
    for b in range(own_tiles):
        keep[b] = jnp.ones((TILE, WIDE), F32)
    period = lax.broadcasted_iota(jnp.int32, (16, 8, WIDE), 2) % 8
    slot = lax.broadcasted_iota(jnp.int32, (16, 8, WIDE), 1)
    for j in range(halo_tiles // 2):
        ids = column(rows_ref[j : j + 1, :].astype(F32))
        ok = (ids < float(own)).astype(F32)
        keep[own_tiles + 2 * j] = ok[:TILE]
        keep[own_tiles + 2 * j + 1] = ok[TILE:]
        tiled = jnp.sum(jnp.where(period == slot, ids.reshape(16, 8, WIDE), 0.0), axis=1)
        ids_ref[16 * j : 16 * j + 16, :] = tiled
    copies[5].wait()
    one_lane = lax.broadcasted_iota(jnp.int32, (1, WIDE), 1)
    for r in range(RELS):
        prior[r : r + 1, :] = jnp.where(one_lane < TILE, prior_in[0, r], prior_in[1, r])
    copies[0].wait()
    for r in range(RELS):
        for w in range(2):
            for h in range(2):
                at = (2 * w + h) * TILE
                wbd[r, at : at + TILE, at : at + TILE] = rel_ref[w, r, h]
    for copy in copies[6:]:
        copy.wait()

    def entry(i):
        code = listed[i]
        return (code >> 4) & 15, code & 15, (code >= 256).astype(F32)

    def rows(b):
        return pl.ds(pl.multiple_of(b * TILE, TILE), TILE)

    def tile_of(group):
        at = group * GROUP
        return sum((at >= starts[a]).astype(jnp.int32) for a in range(1, dests))

    def scores(group):
        i = group * GROUP
        a = tile_of(group)
        parts = []
        for u in range(GROUP):
            b, r, live = entry(i + u)
            pair = jnp.concatenate([k_ref[rows(b), :], v_ref[rows(b), :]], axis=1)
            parts.append(mul(pair, wbd[r], NN).astype(BF16))
        mixed = jnp.concatenate(parts, axis=0)
        kvm[pl.ds(i, GROUP)] = mixed[:, :WIDE].reshape(GROUP, TILE, WIDE)
        both = mul(mixed, qg[a], NT)
        logs[pl.ds(i, GROUP)] = both[:, :WIDE].reshape(GROUP, TILE, WIDE)
        grads[pl.ds(i, GROUP)] = both[:, WIDE:].reshape(GROUP, TILE, WIDE)
        total = None
        for u in range(GROUP):
            b, r, live = entry(i + u)
            ex = jnp.exp(prior[pl.ds(r, 1), :] * both[u * TILE : (u + 1) * TILE, :WIDE]) * (keep[b] * live)
            exps[i + u] = ex
            total = ex if total is None else total + ex
        denom[a] += jnp.sum(total, axis=0, keepdims=True)

    def normalise(group):
        i = group * GROUP
        a = tile_of(group)
        total = None
        for u in range(GROUP):
            soft = exps[i + u] * denom[a]
            exps[i + u] = soft
            prob = soft.astype(BF16)
            probs[i + u] = prob
            term = prob.astype(F32) * grads[i + u]
            total = term if total is None else total + term
        delta[a] += jnp.sum(total, axis=0, keepdims=True)

    def backward(group):
        i = group * GROUP
        a = tile_of(group)
        parts = []
        for u in range(GROUP):
            b, r, live = entry(i + u)
            score_grad = exps[i + u] * (grads[i + u] - delta[a])
            dprior[pl.ds(r, 1), :] += jnp.sum(score_grad * logs[i + u], axis=0, keepdims=True)
            parts.append((score_grad * prior[pl.ds(r, 1), :]).astype(BF16))
        lgrad = jnp.concatenate(parts, axis=0)
        pair = jnp.concatenate([lgrad, probs[pl.ds(i, GROUP)].reshape(GROUP * TILE, WIDE)], axis=1)
        mixed_grad = mul(pair, qg[a], NN).astype(BF16)
        dq[a] += mul(lgrad, kvm[pl.ds(i, GROUP)].reshape(GROUP * TILE, WIDE), TN)
        for u in range(GROUP):
            b, r, live = entry(i + u)
            part = mixed_grad[u * TILE : (u + 1) * TILE]
            dkv[b] += mul(part, wbd[r], NT)
            dwk[r] += mul(k_ref[rows(b), :], part[:, :WIDE], TN)
            dwv[r] += mul(v_ref[rows(b), :], part[:, WIDE:], TN)

    def sweep(work):
        def some(step, carry):
            for u in range(UNROLL):
                work(step * UNROLL + u)
            return carry

        lax.fori_loop(0, (used + UNROLL - 1) // UNROLL, some, 0)

    sweep(scores)
    denom[...] = 1.0 / denom[...]
    sweep(normalise)
    sweep(backward)

    at_own = 2 * (dests * REL_BLOCK)
    for a in range(dests):
        grad = jnp.where(first, dq[a, :TILE, :], dq[a, TILE:, :]) * 0.125
        at = at_own + a * TILE
        pack_out[at : at + TILE, :] = grad.astype(BF16)
    for b in range(own_tiles):
        for w in range(2):
            at = at_own + (1 + w) * own + b * TILE
            pack_out[at : at + TILE, :] = dkv[b, :, w * WIDE : (w + 1) * WIDE].astype(BF16)
    for b in range(halo_tiles):
        back = dkv[own_tiles + b]
        block = jnp.concatenate(
            [
                back[:, :WIDE].reshape(8, 8, WIDE),
                back[:, WIDE:].reshape(8, 8, WIDE),
                jnp.broadcast_to(ids_ref[8 * b : 8 * b + 8, :].reshape(8, 1, WIDE), (8, 8, WIDE)),
            ],
            axis=1,
        )
        send_out[8 * b : 8 * b + 8] = block.astype(BF16)
    for w, ref in enumerate((dwk, dwv)):
        for r in range(RELS):
            at = (w * RELS + r) * TILE
            drel[at : at + TILE, :] = jnp.where(first, ref[r, :TILE, :], ref[r, TILE:, :])
    sums = dprior[...]
    spot = lax.broadcasted_iota(jnp.int32, sums.shape, 1)
    row = lax.broadcasted_iota(jnp.int32, sums.shape, 0)
    one = jnp.sum(jnp.where(spot < TILE, sums, 0.0), axis=1, keepdims=True)
    two = jnp.sum(jnp.where(spot < TILE, 0.0, sums), axis=1, keepdims=True)
    chosen = jnp.where((spot // 16) % 2 == 0, one, two)
    line = jnp.sum(jnp.where(spot % 16 == row, chosen, 0.0), axis=0, keepdims=True)
    high = line.astype(BF16).astype(F32)
    line = jnp.where(one_lane < 32, high, line - high)
    tail = jnp.where(lax.broadcasted_iota(jnp.int32, (16, WIDE), 0) == 0, line, 0.0).astype(BF16)
    for w in range(2):
        for y in range(dests):
            at = (w * dests + y) * REL_ROWS
            to = (w * dests + y) * REL_BLOCK
            pack_out[to : to + REL_ROWS, :] = drel[at : at + REL_ROWS, :].astype(BF16)
            pack_out[to + REL_ROWS : to + REL_BLOCK, :] = tail


def attend(edges, rel_prior, queries, grad_output, key_rows, value_rows, halo_keys, halo_values, rel_weight, halo_rows):
    rows = queries.shape[0]
    halo = halo_keys.shape[0]
    dests = rows // TILE
    sources = (rows + halo) // TILE
    count = edges.shape[1]
    groups = -(-(count // GROUP + dests - 1) // UNROLL) * UNROLL
    places = groups * GROUP
    slabs = 64
    return pl.pallas_call(
        attend_kernel,
        out_shape=(
            jax.ShapeDtypeStruct((2 * dests * REL_BLOCK + 3 * rows, WIDE), BF16),
            jax.ShapeDtypeStruct((slabs, BLOCK, WIDE), BF16),
        ),
        in_specs=[HBM] * 10,
        out_specs=(VMEM,) * 2,
        scratch_shapes=[
            pltpu.SMEM(edges.shape, jnp.int32),
            pltpu.SMEM((places + 1,), jnp.int32),
            pltpu.SMEM(rel_prior.shape, F32),
            pltpu.VMEM(queries.shape, BF16),
            pltpu.VMEM(grad_output.shape, BF16),
            pltpu.VMEM(rel_weight.shape, BF16),
            pltpu.VMEM(halo_rows.shape, jnp.int32),
            pltpu.VMEM((rows + halo, WIDE), BF16),
            pltpu.VMEM((rows + halo, WIDE), BF16),
            pltpu.SemaphoreType.DMA((10,)),
            pltpu.VMEM((RELS, 2 * WIDE, 2 * WIDE), BF16),
            pltpu.VMEM((dests, 2 * WIDE, 2 * WIDE), BF16),
            pltpu.VMEM((sources, TILE, WIDE), F32),
            pltpu.VMEM((16, WIDE), F32),
            pltpu.VMEM((places, TILE, WIDE), BF16),
            pltpu.VMEM((places, TILE, WIDE), BF16),
            pltpu.VMEM((places, TILE, WIDE), F32),
            pltpu.VMEM((places, TILE, WIDE), F32),
            pltpu.VMEM((places, TILE, WIDE), F32),
            pltpu.VMEM((dests, 1, WIDE), F32),
            pltpu.VMEM((dests, 1, WIDE), F32),
            pltpu.VMEM((16, WIDE), F32),
            pltpu.VMEM((sources, TILE, 2 * WIDE), F32),
            pltpu.VMEM((RELS, WIDE, WIDE), F32),
            pltpu.VMEM((RELS, WIDE, WIDE), F32),
            pltpu.VMEM((dests, WIDE, WIDE), F32),
            pltpu.VMEM((2 * RELS * TILE, WIDE), F32),
            pltpu.VMEM((slabs, WIDE), F32),
        ],
        compiler_params=pltpu.CompilerParams(vmem_limit_bytes=MOST),
        cost_estimate=pl.CostEstimate(flops=3 * 10**9, bytes_accessed=4 * 10**6, transcendentals=400000),
        name="attend",
    )(edges, rel_prior, queries, grad_output, key_rows, value_rows, halo_keys, halo_values, rel_weight, halo_rows)


def bundle_kernel(place, pack_ref, nf_ref, types_ref, mine_out, send_out, own_out, keep_out, rel_out):
    half = rel_out.shape[0]
    for out, core in ((rel_out, 1 - place[0]), (keep_out, place[0])):
        out[...] = pack_ref[pl.ds(pl.multiple_of(core * half, half), half), :]
    rows, feats = nf_ref.shape
    turned = jnp.transpose(nf_ref[...], (1, 0)).astype(F32).reshape(feats // 16, 2, 8, rows)
    low = turned[:, 0].reshape(feats // 2, rows)
    high = turned[:, 1].reshape(feats // 2, rows)
    even = place[0] == 0
    mine_out[...] = jnp.where(even, low, high).astype(BF16)
    send_out[:, :rows] = jnp.where(even, high, low).astype(BF16)
    for j in range(rows // WIDE):
        kinds = column(types_ref[j : j + 1, :].astype(F32)).astype(BF16)
        send_out[j * WIDE : (j + 1) * WIDE, rows + WIDE :] = kinds
    send_out[:, rows : rows + WIDE] = pack_ref[2 * half : 2 * half + rows, :]
    for w in range(2):
        at = 2 * half + (1 + w) * rows
        own_out[:, w * WIDE : (w + 1) * WIDE] = pack_ref[at : at + rows, :]


def bundle(place, pack, node_feats, node_types):
    rows, feats = node_feats.shape
    half = (pack.shape[0] - 3 * rows) // 2
    return pl.pallas_call(
        bundle_kernel,
        out_shape=(
            jax.ShapeDtypeStruct((feats // 2, rows), BF16),
            jax.ShapeDtypeStruct((feats // 2, rows + 2 * WIDE), BF16),
            jax.ShapeDtypeStruct((rows, 2 * WIDE), BF16),
            jax.ShapeDtypeStruct((half, WIDE), BF16),
            jax.ShapeDtypeStruct((half, WIDE), BF16),
        ),
        in_specs=[SMEM] + [VMEM] * 3,
        out_specs=(VMEM,) * 5,
        compiler_params=pltpu.CompilerParams(vmem_limit_bytes=LIMIT),
        cost_estimate=pl.CostEstimate(flops=10**6, bytes_accessed=2 * 10**6, transcendentals=0),
        name="bundle",
    )(place, pack, node_feats, node_types)


def spread(place, products, outs):
    size = outs[0].shape[0]
    for d in range(len(outs)):
        block = lax.rem(place[1] + d, len(outs))
        outs[d][:, : products.shape[1]] = products[pl.ds(pl.multiple_of(block * size, size), size), :]


def project_queries_kernel(place, mine_ref, sent_ref, got_ref, rel_ref, rel_got_ref, pair_out, *refs):
    outs, products = refs[:-1], refs[-1]
    rows = mine_ref.shape[1]
    pair_out[:, :rows] = mine_ref[...]
    pair_out[:, rows:] = got_ref[:, :rows]
    query = jnp.concatenate([ref[:, rows : rows + WIDE] for ref in (sent_ref, got_ref)], axis=0).astype(F32)
    kinds = jnp.concatenate([ref[:, rows + WIDE :] for ref in (sent_ref, got_ref)], axis=0).astype(F32)
    for t in range(EARLY):
        masked = jnp.where(kinds == float(t), query, 0.0).astype(BF16)
        products[:, t * WIDE : (t + 1) * WIDE] = mul(pair_out[...], masked, NN).astype(BF16)
    spread(place, products, outs)
    for d in range(len(outs)):
        block = lax.rem(place[1] + d, len(outs))
        here = pl.ds(pl.multiple_of(block * REL_BLOCK, REL_BLOCK), REL_BLOCK)
        both = with_line(rel_ref[here, :].astype(F32) + rel_got_ref[here, :].astype(F32)).astype(BF16)
        for k in range(REL_BLOCK // TILE):
            at = (EARLY + k) * WIDE
            outs[d][:, at : at + WIDE] = both[k * TILE : (k + 1) * TILE, :]


def project_queries(place, mine, sent, got, rel, rel_got, count):
    feats, rows = mine.shape
    wide = EARLY * WIDE
    more = REL_BLOCK // TILE * WIDE
    return pl.pallas_call(
        project_queries_kernel,
        out_shape=(jax.ShapeDtypeStruct((feats, 2 * rows), BF16),)
        + (jax.ShapeDtypeStruct((feats // count, wide + more), BF16),) * count,
        in_specs=[SMEM] + [VMEM] * 5,
        out_specs=(VMEM,) * (1 + count),
        scratch_shapes=[pltpu.VMEM((feats, wide), BF16)],
        compiler_params=pltpu.CompilerParams(vmem_limit_bytes=LIMIT),
        cost_estimate=pl.CostEstimate(flops=10**9, bytes_accessed=2 * 10**6, transcendentals=0),
        name="project_queries",
    )(place, mine, sent, got, rel, rel_got)


def collect_kernel(own_ref, inc_ref, kv_out):
    rows = own_ref.shape[0]
    slabs = inc_ref.shape[0]
    row = lax.broadcasted_iota(jnp.int32, (16, WIDE), 0)
    block = lax.broadcasted_iota(jnp.int32, (16, WIDE), 1) // 8
    node = lax.broadcasted_iota(jnp.int32, (rows, WIDE), 0).astype(F32)
    back = own_ref[...].astype(F32)
    for c in range(slabs // 16):
        grads = inc_ref[16 * c : 16 * c + 16].astype(F32)
        ids = grads[:, 16, :]
        line = jnp.sum(jnp.where(row == block, ids, 0.0), axis=0, keepdims=True)
        pick = (node == line).astype(F32).astype(BF16)
        both = jnp.concatenate(
            [grads[:, :8].reshape(WIDE, WIDE), grads[:, 8:16].reshape(WIDE, WIDE)], axis=1
        )
        back = back + mul(pick, both.astype(BF16), NN)
    kv_out[...] = back.astype(BF16)


def collect(own, incoming):
    rows = own.shape[0]
    return pl.pallas_call(
        collect_kernel,
        out_shape=jax.ShapeDtypeStruct((rows, 2 * WIDE), BF16),
        in_specs=[VMEM, VMEM],
        out_specs=VMEM,
        compiler_params=pltpu.CompilerParams(vmem_limit_bytes=LIMIT),
        cost_estimate=pl.CostEstimate(flops=10**8, bytes_accessed=10**6, transcendentals=0),
        name="collect",
    )(own, incoming)


def relation_places_kernel(*refs):
    out = refs[-1]
    parts = []
    for k in range(REL_BLOCK // TILE):
        at = (EARLY + k) * WIDE
        total = refs[0][:, at : at + WIDE].astype(F32)
        for ref in refs[1:-1]:
            total = total + ref[:, at : at + WIDE].astype(F32)
        parts.append(total)
    total = with_line(jnp.concatenate(parts, axis=0)).astype(BF16)
    for z in range(out.shape[0]):
        out[z] = total


def relation_places(arrived, count):
    return pl.pallas_call(
        relation_places_kernel,
        out_shape=jax.ShapeDtypeStruct((count, REL_BLOCK, WIDE), BF16),
        in_specs=[VMEM] * len(arrived),
        out_specs=VMEM,
        compiler_params=pltpu.CompilerParams(vmem_limit_bytes=LIMIT),
        cost_estimate=pl.CostEstimate(flops=10**6, bytes_accessed=10**6, transcendentals=0),
        name="relation_places",
    )(*arrived)


def relation_sum_kernel(inc_ref, rel_out, prior_out):
    total = inc_ref[0].astype(F32)
    for s in range(1, inc_ref.shape[0]):
        total = total + inc_ref[s].astype(F32)
    rel_out[...] = total.astype(BF16)
    line = total[REL_ROWS : REL_ROWS + 1, :]
    line = line + pltpu.roll(line, WIDE - 32, 1)
    prior_out[0:1, :] = line[:, :RELS]
    prior_out[1:2, :] = pltpu.roll(line, WIDE - 16, 1)[:, :RELS]


def relation_sum(incoming):
    return pl.pallas_call(
        relation_sum_kernel,
        out_shape=(
            jax.ShapeDtypeStruct(incoming.shape[1:], BF16),
            jax.ShapeDtypeStruct((2, RELS), F32),
        ),
        in_specs=[VMEM],
        out_specs=(VMEM,) * 2,
        compiler_params=pltpu.CompilerParams(vmem_limit_bytes=LIMIT),
        cost_estimate=pl.CostEstimate(flops=10**6, bytes_accessed=10**6, transcendentals=0),
        name="relation_sum",
    )(incoming)


def project_kernel(place, pair_ref, kv_ref, got_kv_ref, sent_ref, got_ref, *refs):
    outs, products = refs[:-1], refs[-1]
    rows = kv_ref.shape[0]
    kinds = jnp.concatenate([ref[:, rows + WIDE :] for ref in (sent_ref, got_ref)], axis=0).astype(F32)
    for p in range(3):
        pair = (sent_ref, got_ref) if p == 0 else (kv_ref, got_kv_ref)
        column_at = rows if p == 0 else (p - 1) * WIDE
        part = jnp.concatenate([ref[:, column_at : column_at + WIDE] for ref in pair], axis=0).astype(F32)
        for t in range(EARLY if p == 0 else 0, TYPES):
            at = (p * TYPES + t - EARLY) * WIDE
            masked = jnp.where(kinds == float(t), part, 0.0).astype(BF16)
            products[:, at : at + WIDE] = mul(pair_ref[...], masked, NN).astype(BF16)
    spread(place, products, outs)


def project(place, pair, kv, got_kv, sent, got, count):
    feats = pair.shape[0]
    wide = (PROJ - EARLY) * WIDE
    return pl.pallas_call(
        project_kernel,
        out_shape=(jax.ShapeDtypeStruct((feats // count, wide), BF16),) * count,
        in_specs=[SMEM] + [VMEM] * 5,
        out_specs=(VMEM,) * count,
        scratch_shapes=[pltpu.VMEM((feats, wide), BF16)],
        compiler_params=pltpu.CompilerParams(vmem_limit_bytes=LIMIT),
        cost_estimate=pl.CostEstimate(flops=10**9, bytes_accessed=4 * 10**6, transcendentals=0),
        name="project",
    )(place, pair, kv, got_kv, sent, got)


def features_kernel(place, sent_ref, kv_ref, w_ref, *refs):
    outs, total = refs[:-1], refs[-1]
    rows = kv_ref.shape[0]
    kinds = sent_ref[:, rows + WIDE :].astype(F32)
    acc = None
    for p in range(3):
        part = sent_ref[:, rows : rows + WIDE] if p == 0 else kv_ref[:, (p - 1) * WIDE : p * WIDE]
        part = part.astype(F32)
        for t in range(TYPES):
            masked = jnp.where(kinds == float(t), part, 0.0).astype(BF16)
            term = mul(masked, w_ref[p * TYPES + t], NT)
            acc = term if acc is None else acc + term
    for h in range(len(outs)):
        total[h] = acc[:, h * WIDE : (h + 1) * WIDE]
    me = place[2]
    first = me + 1 - 2 * lax.rem(me, 2)
    for out, owner in zip(outs, (me, 3 - me, first, 3 - first)):
        out[...] = total[owner].astype(BF16)


def features(place, sent, kv, weights):
    rows = kv.shape[0]
    count = weights.shape[1] // WIDE
    return pl.pallas_call(
        features_kernel,
        out_shape=(jax.ShapeDtypeStruct((rows, WIDE), BF16),) * count,
        in_specs=[SMEM, VMEM, VMEM, VMEM],
        out_specs=(VMEM,) * count,
        scratch_shapes=[pltpu.VMEM((count, rows, WIDE), F32)],
        compiler_params=pltpu.CompilerParams(vmem_limit_bytes=LIMIT),
        cost_estimate=pl.CostEstimate(flops=10**9, bytes_accessed=3 * 10**6, transcendentals=0),
        name="features",
    )(place, sent, kv, weights)


def relation_kernel(place, near_ref, far_ref, c_near_ref, c_far_ref, out_ref, flat):
    y = place[1]
    far = 3 - y
    owners = (y, y + 1 - 2 * lax.rem(y, 2), far, far + 1 - 2 * lax.rem(far, 2))
    for core, refs in ((place[0], (near_ref, far_ref)), (1 - place[0], (c_near_ref, c_far_ref))):
        for n, owner in enumerate(owners):
            at = pl.multiple_of((core * len(owners) + owner) * REL_ROWS, 16)
            flat[pl.ds(at, REL_ROWS), :] = refs[n // 2][n % 2, :REL_ROWS, :].astype(F32)
    for w in range(2):
        for r in range(RELS):
            at = (w * RELS + r) * TILE
            for h in range(2):
                out_ref[w, r, h] = flat[at : at + TILE, h * TILE : (h + 1) * TILE]


def relations(place, *blocks):
    return pl.pallas_call(
        relation_kernel,
        out_shape=jax.ShapeDtypeStruct((2, RELS, 2, TILE, TILE), F32),
        in_specs=[SMEM] + [VMEM] * 4,
        out_specs=VMEM,
        scratch_shapes=[pltpu.VMEM((2 * RELS * TILE, WIDE), F32)],
        compiler_params=pltpu.CompilerParams(vmem_limit_bytes=LIMIT),
        cost_estimate=pl.CostEstimate(flops=10**6, bytes_accessed=3 * 10**6, transcendentals=0),
        name="relations",
    )(place, *blocks)


def place_sum_kernel(*refs):
    out = refs[-1]
    half = (len(refs) - 1) // 2
    narrow = EARLY * WIDE
    for at, group in ((0, refs[:half]), (narrow, refs[half:-1])):
        width = narrow if at == 0 else group[0].shape[1]
        total = group[0][:, :width].astype(F32)
        for ref in group[1:]:
            total = total + ref[:, :width].astype(F32)
        out[:, at : at + width] = total.astype(BF16)


def place_sum(query, rest):
    rows = query[0].shape[0]
    return pl.pallas_call(
        place_sum_kernel,
        out_shape=jax.ShapeDtypeStruct((rows, PROJ * WIDE), BF16),
        in_specs=[VMEM] * (len(query) + len(rest)),
        out_specs=VMEM,
        compiler_params=pltpu.CompilerParams(vmem_limit_bytes=LIMIT),
        cost_estimate=pl.CostEstimate(flops=10**6, bytes_accessed=10**6, transcendentals=0),
        name="place_sum",
    )(*query, *rest)


def shifted(blocks, axis):
    count = len(blocks)
    return [blocks[0]] + [
        lax.ppermute(blocks[d], axis, [(i, (i + d) % count) for i in range(count)])
        for d in range(1, count)
    ]


def per_device(
    node_feats,
    node_types,
    queries,
    key_rows,
    value_rows,
    halo_keys,
    halo_values,
    halo_rows,
    edge_tiles,
    grad_output,
    proj_weight,
    rel_weight,
    rel_prior,
):
    y_count = lax.axis_size("y")
    z_count = lax.axis_size("z")
    place = jnp.stack(
        [lax.axis_index("core"), lax.axis_index("y"), lax.axis_index("heads")]
    ).astype(jnp.int32)
    swap = [(0, 1), (1, 0)]
    pack, send = attend(
        edge_tiles.T,
        rel_prior.T,
        queries,
        grad_output,
        key_rows,
        value_rows,
        halo_keys,
        halo_values,
        rel_weight,
        halo_rows.reshape(-1, WIDE),
    )
    incoming = lax.all_to_all(send, ("y", "z", "core"), 0, 0, tiled=True)
    feats_t, sent, own, rel, rel_theirs = bundle(place, pack, node_feats, node_types.reshape(-1, WIDE))
    got = lax.ppermute(sent, "core", swap)
    rel_got = lax.ppermute(rel_theirs, "core", swap)
    pair, *q_blocks = project_queries(place, feats_t, sent, got, rel, rel_got, y_count)
    q_arrived = shifted(q_blocks, "y")
    own, *q_blocks = lax.optimization_barrier((own, *q_blocks))
    kv = collect(own, incoming)
    got_kv = lax.ppermute(kv, "core", swap)
    got_kv, *q_arrived = lax.optimization_barrier((got_kv, *q_arrived))
    rel_z = lax.all_to_all(relation_places(q_arrived, z_count), "z", 0, 0, tiled=True)
    arrived = shifted(project(place, pair, kv, got_kv, sent, got, y_count), "y")
    feat_blocks = features(place, sent, kv, proj_weight.reshape(PROJ, -1, WIDE))
    mine, partners, *away = feat_blocks
    away = [lax.ppermute(block, "heads", [(0, 1), (1, 0), (2, 3), (3, 2)]) for block in away]
    arrived[0], got_mine, got_partners = lax.optimization_barrier((arrived[0], *away))
    partners = partners.astype(F32) + got_partners.astype(F32)
    last = lax.ppermute(partners.astype(BF16), "heads", [(0, 3), (3, 0), (1, 2), (2, 1)])
    grad_feats = (mine.astype(F32) + got_mine.astype(F32) + last.astype(F32)).astype(BF16)
    by_y = place_sum(q_arrived, arrived)
    next_y = [(0, 1), (1, 0), (2, 3), (3, 2)]
    last_y = [(0, 3), (3, 0), (1, 2), (2, 1)]
    rel_z, by_y = lax.optimization_barrier((rel_z, by_y))
    by_z = lax.all_to_all(by_y.reshape(z_count, -1, PROJ * WIDE), "z", 0, 0, tiled=True)
    rel_mine, prior = relation_sum(rel_z)
    rel_first = lax.ppermute(rel_mine, "y", next_y)
    rel_near = jnp.stack([rel_mine, rel_first])
    rel_far = lax.ppermute(rel_near, "y", last_y)
    blocks = (rel_near, rel_far)
    grad_rel = relations(place, *blocks, *(lax.ppermute(block, "core", swap) for block in blocks))
    by_z, grad_rel, grad_feats = lax.optimization_barrier((by_z, grad_rel, grad_feats))
    grad_proj = jnp.sum(by_z.astype(F32), axis=0).reshape(-1, 3, TYPES, WIDE)
    grad_prior = prior.T
    return (grad_feats, grad_proj, grad_rel, grad_prior)


def solution(mesh):
    heads = mesh.devices.shape[1]
    split = Mesh(mesh.devices.reshape(4, 8, 2, heads), ("y", "z", "core", "heads"))
    nodes = ("y", "z", "core")
    return jax.shard_map(
        per_device,
        mesh=split,
        in_specs=(
            P(nodes, None),
            P(nodes),
            P(nodes, "heads"),
            P(nodes, "heads"),
            P(nodes, "heads"),
            P(nodes, "heads"),
            P(nodes, "heads"),
            P(nodes),
            P(nodes, None),
            P(nodes, "heads"),
            P(None, None, None, "heads"),
            P(None, None, "heads", None, None),
            P(None, "heads"),
        ),
        out_specs=(
            P(nodes, "heads"),
            P(nodes, None, None, "heads"),
            P(None, None, "heads", None, None),
            P(None, "heads"),
        ),
        check_vma=False,
    )
```

```python
import jax
import jax.numpy as jnp
from jax import lax
from jax.experimental import pallas as pl
from jax.experimental.pallas import tpu as pltpu
from jax.sharding import Mesh, PartitionSpec as P

TYPES = 5
RELS = 15
TILE = 64
WIDE = 128
GROUP = 4
UNROLL = 6
EARLY = 4
PROJ = 3 * TYPES

F32 = jnp.float32
BF16 = jnp.bfloat16
NN = (((1,), (0,)), ((), ()))
NT = (((1,), (1,)), ((), ()))
TN = (((0,), (0,)), ((), ()))
VMEM = pl.BlockSpec(memory_space=pltpu.VMEM)
SMEM = pl.BlockSpec(memory_space=pltpu.SMEM)
HBM = pl.BlockSpec(memory_space=pltpu.HBM)
BLOCK = 24
REL_ROWS = 240
REL_BLOCK = 256
LIMIT = 24 * 2**20
MOST = 62 * 2**20


def mul(left, right, dims):
    return lax.dot_general(left, right, dims, preferred_element_type=F32)


def column(row):
    return jnp.transpose(jnp.broadcast_to(row, (WIDE, WIDE)), (1, 0))


def high_and_low(line):
    line = line + pltpu.roll(line, WIDE - 32, 1)
    high = line.astype(BF16).astype(F32)
    lane = lax.broadcasted_iota(jnp.int32, line.shape, 1)
    return jnp.where(lane < 32, high, pltpu.roll(line - high, 32, 1))


def with_line(block):
    row = lax.broadcasted_iota(jnp.int32, block.shape, 0)
    return jnp.where(row == REL_ROWS, high_and_low(block[REL_ROWS : REL_ROWS + 1, :]), block)


def attend_kernel(
    edges_hbm, prior_hbm, q_hbm, g_hbm, ko_hbm, vo_hbm, kh_hbm, vh_hbm, rel_hbm, rows_hbm,
    pack_out, send_out,
    edges, listed, prior_in, q_ref, g_ref, rel_ref, rows_ref, k_ref, v_ref, sems,
    wbd, qg, keep, prior, kvm, probs, exps, logs, grads,
    denom, shrink, delta, dprior, dkv, dwk, dwv, dq, drel, ids_ref,
):
    count = edges.shape[1]
    places = kvm.shape[0]
    own = ko_hbm.shape[0]
    dests = own // TILE
    own_tiles = own // TILE
    halo_tiles = kh_hbm.shape[0] // TILE
    copies = [
        pltpu.make_async_copy(source, target, sems.at[i])
        for i, (source, target) in enumerate(
            (
                (rel_hbm, rel_ref),
                (q_hbm, q_ref),
                (g_hbm, g_ref),
                (rows_hbm, rows_ref),
                (edges_hbm, edges),
                (prior_hbm, prior_in),
                (ko_hbm, k_ref.at[:own]),
                (vo_hbm, v_ref.at[:own]),
                (kh_hbm, k_ref.at[own:]),
                (vh_hbm, v_ref.at[own:]),
            )
        )
    ]
    copies[4].start()
    for i, copy in enumerate(copies):
        if i != 4:
            copy.start()

    lane = lax.broadcasted_iota(jnp.int32, (TILE, WIDE), 1)
    first = lane < TILE
    wbd[...] = jnp.zeros_like(wbd)
    denom[...] = jnp.zeros_like(denom)
    delta[...] = jnp.zeros_like(delta)
    dprior[...] = jnp.zeros_like(dprior)
    dkv[...] = jnp.zeros_like(dkv)
    dwk[...] = jnp.zeros_like(dwk)
    dwv[...] = jnp.zeros_like(dwv)
    dq[...] = jnp.zeros_like(dq)
    copies[4].wait()
    for i in range(listed.shape[0]):
        listed[i] = 0
    targets = [edges[0, e] for e in range(count)]
    sizes = [sum((target == a).astype(jnp.int32) for target in targets) for a in range(dests)]
    starts = [jnp.int32(0)]
    for a in range(dests):
        starts.append(starts[a] + (sizes[a] + GROUP - 1) // GROUP * GROUP)
    heads = list(starts[:dests])
    for e, target in enumerate(targets):
        at = jnp.int32(places)
        for a in range(dests):
            at = jnp.where(target == a, heads[a], at)
            heads[a] = heads[a] + (target == a).astype(jnp.int32)
        listed[at] = 256 + 16 * edges[1, e] + edges[2, e]
    used = starts[dests] // GROUP

    copies[1].wait()
    copies[2].wait()
    none = jnp.zeros((TILE, WIDE), BF16)
    for a in range(dests):
        q = q_ref[a * TILE : (a + 1) * TILE, :].astype(F32) * 0.125
        g = g_ref[a * TILE : (a + 1) * TILE, :].astype(F32)
        for h in range(2):
            mine = first if h == 0 else jnp.logical_not(first)
            qg[a, h * TILE : (h + 1) * TILE, :WIDE] = jnp.where(mine, q, 0.0).astype(BF16)
            qg[a, h * TILE : (h + 1) * TILE, WIDE:] = none
            qg[a, (2 + h) * TILE : (3 + h) * TILE, :WIDE] = none
            qg[a, (2 + h) * TILE : (3 + h) * TILE, WIDE:] = jnp.where(mine, g, 0.0).astype(BF16)
    copies[3].wait()
    for b in range(own_tiles):
        keep[b] = jnp.ones((TILE, WIDE), F32)
    period = lax.broadcasted_iota(jnp.int32, (16, 8, WIDE), 2) % 8
    slot = lax.broadcasted_iota(jnp.int32, (16, 8, WIDE), 1)
    for j in range(halo_tiles // 2):
        ids = column(rows_ref[j : j + 1, :].astype(F32))
        ok = (ids < float(own)).astype(F32)
        keep[own_tiles + 2 * j] = ok[:TILE]
        keep[own_tiles + 2 * j + 1] = ok[TILE:]
        tiled = jnp.sum(jnp.where(period == slot, ids.reshape(16, 8, WIDE), 0.0), axis=1)
        ids_ref[16 * j : 16 * j + 16, :] = tiled
    copies[5].wait()
    one_lane = lax.broadcasted_iota(jnp.int32, (1, WIDE), 1)
    for r in range(RELS):
        prior[r : r + 1, :] = jnp.where(one_lane < TILE, prior_in[0, r], prior_in[1, r])
    copies[0].wait()
    for r in range(RELS):
        for w in range(2):
            for h in range(2):
                at = (2 * w + h) * TILE
                wbd[r, at : at + TILE, at : at + TILE] = rel_ref[w, r, h]
    for copy in copies[6:]:
        copy.wait()

    def entry(i):
        code = listed[i]
        return (code >> 4) & 15, code & 15, (code >= 256).astype(F32)

    def rows(b):
        return pl.ds(pl.multiple_of(b * TILE, TILE), TILE)

    def tile_of(group):
        at = group * GROUP
        return sum((at >= starts[a]).astype(jnp.int32) for a in range(1, dests))

    def scores(group):
        i = group * GROUP
        a = tile_of(group)
        parts = []
        for u in range(GROUP):
            b, r, live = entry(i + u)
            pair = jnp.concatenate([k_ref[rows(b), :], v_ref[rows(b), :]], axis=1)
            parts.append(mul(pair, wbd[r], NN).astype(BF16))
        mixed = jnp.concatenate(parts, axis=0)
        kvm[pl.ds(i, GROUP)] = mixed[:, :WIDE].reshape(GROUP, TILE, WIDE)
        both = mul(mixed, qg[a], NT)
        logs[pl.ds(i, GROUP)] = both[:, :WIDE].reshape(GROUP, TILE, WIDE)
        grads[pl.ds(i, GROUP)] = both[:, WIDE:].reshape(GROUP, TILE, WIDE)
        total = None
        for u in range(GROUP):
            b, r, live = entry(i + u)
            ex = jnp.exp(prior[pl.ds(r, 1), :] * both[u * TILE : (u + 1) * TILE, :WIDE])
            ex = jnp.where(keep[b] * live > 0.0, ex, 0.0)
            exps[i + u] = ex
            total = ex if total is None else total + ex
        denom[a] += jnp.sum(total, axis=0, keepdims=True)

    def normalise(group):
        i = group * GROUP
        a = tile_of(group)
        total = None
        for u in range(GROUP):
            soft = exps[i + u] * shrink[a] * denom[a]
            exps[i + u] = soft
            prob = soft.astype(BF16)
            probs[i + u] = prob
            term = prob.astype(F32) * grads[i + u]
            total = term if total is None else total + term
        delta[a] += jnp.sum(total, axis=0, keepdims=True)

    def backward(group):
        i = group * GROUP
        a = tile_of(group)
        parts = []
        for u in range(GROUP):
            b, r, live = entry(i + u)
            score_grad = exps[i + u] * (grads[i + u] - delta[a])
            dprior[pl.ds(r, 1), :] += jnp.sum(score_grad * logs[i + u], axis=0, keepdims=True)
            parts.append((score_grad * prior[pl.ds(r, 1), :]).astype(BF16))
        lgrad = jnp.concatenate(parts, axis=0)
        pair = jnp.concatenate([lgrad, probs[pl.ds(i, GROUP)].reshape(GROUP * TILE, WIDE)], axis=1)
        mixed_grad = mul(pair, qg[a], NN).astype(BF16)
        dq[a] += mul(lgrad, kvm[pl.ds(i, GROUP)].reshape(GROUP * TILE, WIDE), TN)
        for u in range(GROUP):
            b, r, live = entry(i + u)
            part = mixed_grad[u * TILE : (u + 1) * TILE]
            dkv[b] += mul(part, wbd[r], NT)
            dwk[r] += mul(k_ref[rows(b), :], part[:, :WIDE], TN)
            dwv[r] += mul(v_ref[rows(b), :], part[:, WIDE:], TN)

    def sweep(work):
        def some(step, carry):
            for u in range(UNROLL):
                work(step * UNROLL + u)
            return carry

        lax.fori_loop(0, (used + UNROLL - 1) // UNROLL, some, 0)

    sweep(scores)
    shrink[...] = jnp.where(denom[...] > 1e18, 2.0**-64, 1.0)
    denom[...] = 1.0 / (denom[...] * shrink[...])
    sweep(normalise)
    sweep(backward)

    at_own = 2 * (dests * REL_BLOCK)
    for a in range(dests):
        grad = jnp.where(first, dq[a, :TILE, :], dq[a, TILE:, :]) * 0.125
        at = at_own + a * TILE
        pack_out[at : at + TILE, :] = grad.astype(BF16)
    for b in range(own_tiles):
        for w in range(2):
            at = at_own + (1 + w) * own + b * TILE
            pack_out[at : at + TILE, :] = dkv[b, :, w * WIDE : (w + 1) * WIDE].astype(BF16)
    for b in range(halo_tiles):
        back = dkv[own_tiles + b]
        block = jnp.concatenate(
            [
                back[:, :WIDE].reshape(8, 8, WIDE),
                back[:, WIDE:].reshape(8, 8, WIDE),
                jnp.broadcast_to(ids_ref[8 * b : 8 * b + 8, :].reshape(8, 1, WIDE), (8, 8, WIDE)),
            ],
            axis=1,
        )
        send_out[8 * b : 8 * b + 8] = block.astype(BF16)
    for w, ref in enumerate((dwk, dwv)):
        for r in range(RELS):
            at = (w * RELS + r) * TILE
            drel[at : at + TILE, :] = jnp.where(first, ref[r, :TILE, :], ref[r, TILE:, :])
    sums = dprior[...]
    spot = lax.broadcasted_iota(jnp.int32, sums.shape, 1)
    row = lax.broadcasted_iota(jnp.int32, sums.shape, 0)
    one = jnp.sum(jnp.where(spot < TILE, sums, 0.0), axis=1, keepdims=True)
    two = jnp.sum(jnp.where(spot < TILE, 0.0, sums), axis=1, keepdims=True)
    chosen = jnp.where((spot // 16) % 2 == 0, one, two)
    line = jnp.sum(jnp.where(spot % 16 == row, chosen, 0.0), axis=0, keepdims=True)
    high = line.astype(BF16).astype(F32)
    line = jnp.where(one_lane < 32, high, line - high)
    tail = jnp.where(lax.broadcasted_iota(jnp.int32, (16, WIDE), 0) == 0, line, 0.0).astype(BF16)
    for w in range(2):
        for y in range(dests):
            at = (w * dests + y) * REL_ROWS
            to = (w * dests + y) * REL_BLOCK
            pack_out[to : to + REL_ROWS, :] = drel[at : at + REL_ROWS, :].astype(BF16)
            pack_out[to + REL_ROWS : to + REL_BLOCK, :] = tail


def attend(edges, rel_prior, queries, grad_output, key_rows, value_rows, halo_keys, halo_values, rel_weight, halo_rows):
    rows = queries.shape[0]
    halo = halo_keys.shape[0]
    dests = rows // TILE
    sources = (rows + halo) // TILE
    count = edges.shape[1]
    groups = -(-(count // GROUP + dests - 1) // UNROLL) * UNROLL
    places = groups * GROUP
    slabs = 64
    return pl.pallas_call(
        attend_kernel,
        out_shape=(
            jax.ShapeDtypeStruct((2 * dests * REL_BLOCK + 3 * rows, WIDE), BF16),
            jax.ShapeDtypeStruct((slabs, BLOCK, WIDE), BF16),
        ),
        in_specs=[HBM] * 10,
        out_specs=(VMEM,) * 2,
        scratch_shapes=[
            pltpu.SMEM(edges.shape, jnp.int32),
            pltpu.SMEM((places + 1,), jnp.int32),
            pltpu.SMEM(rel_prior.shape, F32),
            pltpu.VMEM(queries.shape, BF16),
            pltpu.VMEM(grad_output.shape, BF16),
            pltpu.VMEM(rel_weight.shape, BF16),
            pltpu.VMEM(halo_rows.shape, jnp.int32),
            pltpu.VMEM((rows + halo, WIDE), BF16),
            pltpu.VMEM((rows + halo, WIDE), BF16),
            pltpu.SemaphoreType.DMA((10,)),
            pltpu.VMEM((RELS, 2 * WIDE, 2 * WIDE), BF16),
            pltpu.VMEM((dests, 2 * WIDE, 2 * WIDE), BF16),
            pltpu.VMEM((sources, TILE, WIDE), F32),
            pltpu.VMEM((16, WIDE), F32),
            pltpu.VMEM((places, TILE, WIDE), BF16),
            pltpu.VMEM((places, TILE, WIDE), BF16),
            pltpu.VMEM((places, TILE, WIDE), F32),
            pltpu.VMEM((places, TILE, WIDE), F32),
            pltpu.VMEM((places, TILE, WIDE), F32),
            pltpu.VMEM((dests, 1, WIDE), F32),
            pltpu.VMEM((dests, 1, WIDE), F32),
            pltpu.VMEM((dests, 1, WIDE), F32),
            pltpu.VMEM((16, WIDE), F32),
            pltpu.VMEM((sources, TILE, 2 * WIDE), F32),
            pltpu.VMEM((RELS, WIDE, WIDE), F32),
            pltpu.VMEM((RELS, WIDE, WIDE), F32),
            pltpu.VMEM((dests, WIDE, WIDE), F32),
            pltpu.VMEM((2 * RELS * TILE, WIDE), F32),
            pltpu.VMEM((slabs, WIDE), F32),
        ],
        compiler_params=pltpu.CompilerParams(vmem_limit_bytes=MOST),
        cost_estimate=pl.CostEstimate(flops=3 * 10**9, bytes_accessed=4 * 10**6, transcendentals=400000),
        name="attend",
    )(edges, rel_prior, queries, grad_output, key_rows, value_rows, halo_keys, halo_values, rel_weight, halo_rows)


def bundle_kernel(place, pack_ref, nf_ref, types_ref, mine_out, send_out, own_out, keep_out, rel_out):
    half = rel_out.shape[0]
    for out, core in ((rel_out, 1 - place[0]), (keep_out, place[0])):
        out[...] = pack_ref[pl.ds(pl.multiple_of(core * half, half), half), :]
    rows, feats = nf_ref.shape
    turned = jnp.transpose(nf_ref[...], (1, 0)).astype(F32).reshape(feats // 16, 2, 8, rows)
    low = turned[:, 0].reshape(feats // 2, rows)
    high = turned[:, 1].reshape(feats // 2, rows)
    even = place[0] == 0
    mine_out[...] = jnp.where(even, low, high).astype(BF16)
    send_out[:, :rows] = jnp.where(even, high, low).astype(BF16)
    for j in range(rows // WIDE):
        kinds = column(types_ref[j : j + 1, :].astype(F32)).astype(BF16)
        send_out[j * WIDE : (j + 1) * WIDE, rows + WIDE :] = kinds
    send_out[:, rows : rows + WIDE] = pack_ref[2 * half : 2 * half + rows, :]
    for w in range(2):
        at = 2 * half + (1 + w) * rows
        own_out[:, w * WIDE : (w + 1) * WIDE] = pack_ref[at : at + rows, :]


def bundle(place, pack, node_feats, node_types):
    rows, feats = node_feats.shape
    half = (pack.shape[0] - 3 * rows) // 2
    return pl.pallas_call(
        bundle_kernel,
        out_shape=(
            jax.ShapeDtypeStruct((feats // 2, rows), BF16),
            jax.ShapeDtypeStruct((feats // 2, rows + 2 * WIDE), BF16),
            jax.ShapeDtypeStruct((rows, 2 * WIDE), BF16),
            jax.ShapeDtypeStruct((half, WIDE), BF16),
            jax.ShapeDtypeStruct((half, WIDE), BF16),
        ),
        in_specs=[SMEM] + [VMEM] * 3,
        out_specs=(VMEM,) * 5,
        compiler_params=pltpu.CompilerParams(vmem_limit_bytes=LIMIT),
        cost_estimate=pl.CostEstimate(flops=10**6, bytes_accessed=2 * 10**6, transcendentals=0),
        name="bundle",
    )(place, pack, node_feats, node_types)


def spread(place, products, outs):
    size = outs[0].shape[0]
    for d in range(len(outs)):
        block = lax.rem(place[1] + d, len(outs))
        outs[d][:, : products.shape[1]] = products[pl.ds(pl.multiple_of(block * size, size), size), :]


def project_queries_kernel(place, mine_ref, sent_ref, got_ref, rel_ref, rel_got_ref, pair_out, *refs):
    outs, products = refs[:-1], refs[-1]
    rows = mine_ref.shape[1]
    pair_out[:, :rows] = mine_ref[...]
    pair_out[:, rows:] = got_ref[:, :rows]
    query = jnp.concatenate([ref[:, rows : rows + WIDE] for ref in (sent_ref, got_ref)], axis=0).astype(F32)
    kinds = jnp.concatenate([ref[:, rows + WIDE :] for ref in (sent_ref, got_ref)], axis=0).astype(F32)
    for t in range(EARLY):
        masked = jnp.where(kinds == float(t), query, 0.0).astype(BF16)
        products[:, t * WIDE : (t + 1) * WIDE] = mul(pair_out[...], masked, NN).astype(BF16)
    spread(place, products, outs)
    for d in range(len(outs)):
        block = lax.rem(place[1] + d, len(outs))
        here = pl.ds(pl.multiple_of(block * REL_BLOCK, REL_BLOCK), REL_BLOCK)
        both = with_line(rel_ref[here, :].astype(F32) + rel_got_ref[here, :].astype(F32)).astype(BF16)
        for k in range(REL_BLOCK // TILE):
            at = (EARLY + k) * WIDE
            outs[d][:, at : at + WIDE] = both[k * TILE : (k + 1) * TILE, :]


def project_queries(place, mine, sent, got, rel, rel_got, count):
    feats, rows = mine.shape
    wide = EARLY * WIDE
    more = REL_BLOCK // TILE * WIDE
    return pl.pallas_call(
        project_queries_kernel,
        out_shape=(jax.ShapeDtypeStruct((feats, 2 * rows), BF16),)
        + (jax.ShapeDtypeStruct((feats // count, wide + more), BF16),) * count,
        in_specs=[SMEM] + [VMEM] * 5,
        out_specs=(VMEM,) * (1 + count),
        scratch_shapes=[pltpu.VMEM((feats, wide), BF16)],
        compiler_params=pltpu.CompilerParams(vmem_limit_bytes=LIMIT),
        cost_estimate=pl.CostEstimate(flops=10**9, bytes_accessed=2 * 10**6, transcendentals=0),
        name="project_queries",
    )(place, mine, sent, got, rel, rel_got)


def collect_kernel(own_ref, inc_ref, kv_out):
    rows = own_ref.shape[0]
    slabs = inc_ref.shape[0]
    row = lax.broadcasted_iota(jnp.int32, (16, WIDE), 0)
    block = lax.broadcasted_iota(jnp.int32, (16, WIDE), 1) // 8
    node = lax.broadcasted_iota(jnp.int32, (rows, WIDE), 0).astype(F32)
    back = own_ref[...].astype(F32)
    for c in range(slabs // 16):
        grads = inc_ref[16 * c : 16 * c + 16].astype(F32)
        ids = grads[:, 16, :]
        line = jnp.sum(jnp.where(row == block, ids, 0.0), axis=0, keepdims=True)
        pick = (node == line).astype(F32).astype(BF16)
        both = jnp.concatenate(
            [grads[:, :8].reshape(WIDE, WIDE), grads[:, 8:16].reshape(WIDE, WIDE)], axis=1
        )
        back = back + mul(pick, both.astype(BF16), NN)
    kv_out[...] = back.astype(BF16)


def collect(own, incoming):
    rows = own.shape[0]
    return pl.pallas_call(
        collect_kernel,
        out_shape=jax.ShapeDtypeStruct((rows, 2 * WIDE), BF16),
        in_specs=[VMEM, VMEM],
        out_specs=VMEM,
        compiler_params=pltpu.CompilerParams(vmem_limit_bytes=LIMIT),
        cost_estimate=pl.CostEstimate(flops=10**8, bytes_accessed=10**6, transcendentals=0),
        name="collect",
    )(own, incoming)


def relation_places_kernel(*refs):
    out = refs[-1]
    parts = []
    for k in range(REL_BLOCK // TILE):
        at = (EARLY + k) * WIDE
        total = refs[0][:, at : at + WIDE].astype(F32)
        for ref in refs[1:-1]:
            total = total + ref[:, at : at + WIDE].astype(F32)
        parts.append(total)
    total = with_line(jnp.concatenate(parts, axis=0)).astype(BF16)
    for z in range(out.shape[0]):
        out[z] = total


def relation_places(arrived, count):
    return pl.pallas_call(
        relation_places_kernel,
        out_shape=jax.ShapeDtypeStruct((count, REL_BLOCK, WIDE), BF16),
        in_specs=[VMEM] * len(arrived),
        out_specs=VMEM,
        compiler_params=pltpu.CompilerParams(vmem_limit_bytes=LIMIT),
        cost_estimate=pl.CostEstimate(flops=10**6, bytes_accessed=10**6, transcendentals=0),
        name="relation_places",
    )(*arrived)


def relation_sum_kernel(inc_ref, rel_out, prior_out):
    total = inc_ref[0].astype(F32)
    for s in range(1, inc_ref.shape[0]):
        total = total + inc_ref[s].astype(F32)
    rel_out[...] = total.astype(BF16)
    line = total[REL_ROWS : REL_ROWS + 1, :]
    line = line + pltpu.roll(line, WIDE - 32, 1)
    prior_out[0:1, :] = line[:, :RELS]
    prior_out[1:2, :] = pltpu.roll(line, WIDE - 16, 1)[:, :RELS]


def relation_sum(incoming):
    return pl.pallas_call(
        relation_sum_kernel,
        out_shape=(
            jax.ShapeDtypeStruct(incoming.shape[1:], BF16),
            jax.ShapeDtypeStruct((2, RELS), F32),
        ),
        in_specs=[VMEM],
        out_specs=(VMEM,) * 2,
        compiler_params=pltpu.CompilerParams(vmem_limit_bytes=LIMIT),
        cost_estimate=pl.CostEstimate(flops=10**6, bytes_accessed=10**6, transcendentals=0),
        name="relation_sum",
    )(incoming)


def project_kernel(place, pair_ref, kv_ref, got_kv_ref, sent_ref, got_ref, *refs):
    outs, products = refs[:-1], refs[-1]
    rows = kv_ref.shape[0]
    kinds = jnp.concatenate([ref[:, rows + WIDE :] for ref in (sent_ref, got_ref)], axis=0).astype(F32)
    for p in range(3):
        pair = (sent_ref, got_ref) if p == 0 else (kv_ref, got_kv_ref)
        column_at = rows if p == 0 else (p - 1) * WIDE
        part = jnp.concatenate([ref[:, column_at : column_at + WIDE] for ref in pair], axis=0).astype(F32)
        for t in range(EARLY if p == 0 else 0, TYPES):
            at = (p * TYPES + t - EARLY) * WIDE
            masked = jnp.where(kinds == float(t), part, 0.0).astype(BF16)
            products[:, at : at + WIDE] = mul(pair_ref[...], masked, NN).astype(BF16)
    spread(place, products, outs)


def project(place, pair, kv, got_kv, sent, got, count):
    feats = pair.shape[0]
    wide = (PROJ - EARLY) * WIDE
    return pl.pallas_call(
        project_kernel,
        out_shape=(jax.ShapeDtypeStruct((feats // count, wide), BF16),) * count,
        in_specs=[SMEM] + [VMEM] * 5,
        out_specs=(VMEM,) * count,
        scratch_shapes=[pltpu.VMEM((feats, wide), BF16)],
        compiler_params=pltpu.CompilerParams(vmem_limit_bytes=LIMIT),
        cost_estimate=pl.CostEstimate(flops=10**9, bytes_accessed=4 * 10**6, transcendentals=0),
        name="project",
    )(place, pair, kv, got_kv, sent, got)


def features_kernel(place, sent_ref, kv_ref, w_ref, *refs):
    outs, total = refs[:-1], refs[-1]
    rows = kv_ref.shape[0]
    kinds = sent_ref[:, rows + WIDE :].astype(F32)
    acc = None
    for p in range(3):
        part = sent_ref[:, rows : rows + WIDE] if p == 0 else kv_ref[:, (p - 1) * WIDE : p * WIDE]
        part = part.astype(F32)
        for t in range(TYPES):
            masked = jnp.where(kinds == float(t), part, 0.0).astype(BF16)
            term = mul(masked, w_ref[p * TYPES + t], NT)
            acc = term if acc is None else acc + term
    for h in range(len(outs)):
        total[h] = acc[:, h * WIDE : (h + 1) * WIDE]
    me = place[2]
    first = me + 1 - 2 * lax.rem(me, 2)
    for out, owner in zip(outs, (me, 3 - me, first, 3 - first)):
        out[...] = total[owner].astype(BF16)


def features(place, sent, kv, weights):
    rows = kv.shape[0]
    count = weights.shape[1] // WIDE
    return pl.pallas_call(
        features_kernel,
        out_shape=(jax.ShapeDtypeStruct((rows, WIDE), BF16),) * count,
        in_specs=[SMEM, VMEM, VMEM, VMEM],
        out_specs=(VMEM,) * count,
        scratch_shapes=[pltpu.VMEM((count, rows, WIDE), F32)],
        compiler_params=pltpu.CompilerParams(vmem_limit_bytes=LIMIT),
        cost_estimate=pl.CostEstimate(flops=10**9, bytes_accessed=3 * 10**6, transcendentals=0),
        name="features",
    )(place, sent, kv, weights)


def relation_kernel(place, near_ref, far_ref, c_near_ref, c_far_ref, out_ref, flat):
    y = place[1]
    far = 3 - y
    owners = (y, y + 1 - 2 * lax.rem(y, 2), far, far + 1 - 2 * lax.rem(far, 2))
    for core, refs in ((place[0], (near_ref, far_ref)), (1 - place[0], (c_near_ref, c_far_ref))):
        for n, owner in enumerate(owners):
            at = pl.multiple_of((core * len(owners) + owner) * REL_ROWS, 16)
            flat[pl.ds(at, REL_ROWS), :] = refs[n // 2][n % 2, :REL_ROWS, :].astype(F32)
    for w in range(2):
        for r in range(RELS):
            at = (w * RELS + r) * TILE
            for h in range(2):
                out_ref[w, r, h] = flat[at : at + TILE, h * TILE : (h + 1) * TILE]


def relations(place, *blocks):
    return pl.pallas_call(
        relation_kernel,
        out_shape=jax.ShapeDtypeStruct((2, RELS, 2, TILE, TILE), F32),
        in_specs=[SMEM] + [VMEM] * 4,
        out_specs=VMEM,
        scratch_shapes=[pltpu.VMEM((2 * RELS * TILE, WIDE), F32)],
        compiler_params=pltpu.CompilerParams(vmem_limit_bytes=LIMIT),
        cost_estimate=pl.CostEstimate(flops=10**6, bytes_accessed=3 * 10**6, transcendentals=0),
        name="relations",
    )(place, *blocks)


def place_sum_kernel(*refs):
    out = refs[-1]
    half = (len(refs) - 1) // 2
    narrow = EARLY * WIDE
    for at, group in ((0, refs[:half]), (narrow, refs[half:-1])):
        width = narrow if at == 0 else group[0].shape[1]
        total = group[0][:, :width].astype(F32)
        for ref in group[1:]:
            total = total + ref[:, :width].astype(F32)
        out[:, at : at + width] = total.astype(BF16)


def place_sum(query, rest):
    rows = query[0].shape[0]
    return pl.pallas_call(
        place_sum_kernel,
        out_shape=jax.ShapeDtypeStruct((rows, PROJ * WIDE), BF16),
        in_specs=[VMEM] * (len(query) + len(rest)),
        out_specs=VMEM,
        compiler_params=pltpu.CompilerParams(vmem_limit_bytes=LIMIT),
        cost_estimate=pl.CostEstimate(flops=10**6, bytes_accessed=10**6, transcendentals=0),
        name="place_sum",
    )(*query, *rest)


def shifted(blocks, axis):
    count = len(blocks)
    return [blocks[0]] + [
        lax.ppermute(blocks[d], axis, [(i, (i + d) % count) for i in range(count)])
        for d in range(1, count)
    ]


def per_device(
    node_feats,
    node_types,
    queries,
    key_rows,
    value_rows,
    halo_keys,
    halo_values,
    halo_rows,
    edge_tiles,
    grad_output,
    proj_weight,
    rel_weight,
    rel_prior,
):
    y_count = lax.axis_size("y")
    z_count = lax.axis_size("z")
    place = jnp.stack(
        [lax.axis_index("core"), lax.axis_index("y"), lax.axis_index("heads")]
    ).astype(jnp.int32)
    swap = [(0, 1), (1, 0)]
    pack, send = attend(
        edge_tiles.T,
        rel_prior.T,
        queries,
        grad_output,
        key_rows,
        value_rows,
        halo_keys,
        halo_values,
        rel_weight,
        halo_rows.reshape(-1, WIDE),
    )
    incoming = lax.all_to_all(send, ("y", "z", "core"), 0, 0, tiled=True)
    feats_t, sent, own, rel, rel_theirs = bundle(place, pack, node_feats, node_types.reshape(-1, WIDE))
    got = lax.ppermute(sent, "core", swap)
    rel_got = lax.ppermute(rel_theirs, "core", swap)
    pair, *q_blocks = project_queries(place, feats_t, sent, got, rel, rel_got, y_count)
    q_arrived = shifted(q_blocks, "y")
    own, *q_blocks = lax.optimization_barrier((own, *q_blocks))
    kv = collect(own, incoming)
    got_kv = lax.ppermute(kv, "core", swap)
    got_kv, *q_arrived = lax.optimization_barrier((got_kv, *q_arrived))
    rel_z = lax.all_to_all(relation_places(q_arrived, z_count), "z", 0, 0, tiled=True)
    arrived = shifted(project(place, pair, kv, got_kv, sent, got, y_count), "y")
    feat_blocks = features(place, sent, kv, proj_weight.reshape(PROJ, -1, WIDE))
    mine, partners, *away = feat_blocks
    away = [lax.ppermute(block, "heads", [(0, 1), (1, 0), (2, 3), (3, 2)]) for block in away]
    arrived[0], got_mine, got_partners = lax.optimization_barrier((arrived[0], *away))
    partners = partners.astype(F32) + got_partners.astype(F32)
    last = lax.ppermute(partners.astype(BF16), "heads", [(0, 3), (3, 0), (1, 2), (2, 1)])
    grad_feats = (mine.astype(F32) + got_mine.astype(F32) + last.astype(F32)).astype(BF16)
    by_y = place_sum(q_arrived, arrived)
    next_y = [(0, 1), (1, 0), (2, 3), (3, 2)]
    last_y = [(0, 3), (3, 0), (1, 2), (2, 1)]
    rel_z, by_y = lax.optimization_barrier((rel_z, by_y))
    by_z = lax.all_to_all(by_y.reshape(z_count, -1, PROJ * WIDE), "z", 0, 0, tiled=True)
    rel_mine, prior = relation_sum(rel_z)
    rel_first = lax.ppermute(rel_mine, "y", next_y)
    rel_near = jnp.stack([rel_mine, rel_first])
    rel_far = lax.ppermute(rel_near, "y", last_y)
    blocks = (rel_near, rel_far)
    grad_rel = relations(place, *blocks, *(lax.ppermute(block, "core", swap) for block in blocks))
    by_z, grad_rel, grad_feats = lax.optimization_barrier((by_z, grad_rel, grad_feats))
    grad_proj = jnp.sum(by_z.astype(F32), axis=0).reshape(-1, 3, TYPES, WIDE)
    grad_prior = prior.T
    return (grad_feats, grad_proj, grad_rel, grad_prior)


def solution(mesh):
    heads = mesh.devices.shape[1]
    split = Mesh(mesh.devices.reshape(4, 8, 2, heads), ("y", "z", "core", "heads"))
    nodes = ("y", "z", "core")
    return jax.shard_map(
        per_device,
        mesh=split,
        in_specs=(
            P(nodes, None),
            P(nodes),
            P(nodes, "heads"),
            P(nodes, "heads"),
            P(nodes, "heads"),
            P(nodes, "heads"),
            P(nodes, "heads"),
            P(nodes),
            P(nodes, None),
            P(nodes, "heads"),
            P(None, None, None, "heads"),
            P(None, None, "heads", None, None),
            P(None, "heads"),
        ),
        out_specs=(
            P(nodes, "heads"),
            P(nodes, None, None, "heads"),
            P(None, None, "heads", None, None),
            P(None, "heads"),
        ),
        check_vma=False,
    )
```

```python
import jax
import jax.numpy as jnp
from jax import lax
from jax.experimental import pallas as pl
from jax.experimental.pallas import tpu as pltpu
from jax.sharding import Mesh, PartitionSpec as P

TYPES = 5
RELS = 15
TILE = 64
WIDE = 128
GROUP = 4
UNROLL = 6
EARLY = 4
PROJ = 3 * TYPES

F32 = jnp.float32
BF16 = jnp.bfloat16
NN = (((1,), (0,)), ((), ()))
NT = (((1,), (1,)), ((), ()))
TN = (((0,), (0,)), ((), ()))
VMEM = pl.BlockSpec(memory_space=pltpu.VMEM)
SMEM = pl.BlockSpec(memory_space=pltpu.SMEM)
HBM = pl.BlockSpec(memory_space=pltpu.HBM)
BLOCK = 24
REL_ROWS = 240
REL_BLOCK = 256
LIMIT = 24 * 2**20
MOST = 62 * 2**20


def mul(left, right, dims):
    return lax.dot_general(left, right, dims, preferred_element_type=F32)


def column(row):
    return jnp.transpose(jnp.broadcast_to(row, (WIDE, WIDE)), (1, 0))


def high_and_low(line):
    line = line + pltpu.roll(line, WIDE - 32, 1)
    high = line.astype(BF16).astype(F32)
    lane = lax.broadcasted_iota(jnp.int32, line.shape, 1)
    return jnp.where(lane < 32, high, pltpu.roll(line - high, 32, 1))


def with_line(block):
    row = lax.broadcasted_iota(jnp.int32, block.shape, 0)
    return jnp.where(row == REL_ROWS, high_and_low(block[REL_ROWS : REL_ROWS + 1, :]), block)


def attend_kernel(
    edges_hbm, prior_hbm, q_hbm, g_hbm, ko_hbm, vo_hbm, kh_hbm, vh_hbm, rel_hbm, rows_hbm,
    pack_hbm, send_hbm,
    pack_out, send_out, out_sems, edges, listed, prior_in, q_ref, g_ref, rel_ref, rows_ref, k_ref, v_ref, sems,
    wbd, qg, keep, prior, kvm, probs, exps, logs, grads,
    denom, shrink, delta, dprior, dkv, dwk, dwv, dq, drel, ids_ref,
):
    count = edges.shape[1]
    places = kvm.shape[0]
    own = ko_hbm.shape[0]
    dests = own // TILE
    own_tiles = own // TILE
    halo_tiles = kh_hbm.shape[0] // TILE
    copies = [
        pltpu.make_async_copy(source, target, sems.at[i])
        for i, (source, target) in enumerate(
            (
                (rel_hbm, rel_ref),
                (q_hbm, q_ref),
                (g_hbm, g_ref),
                (rows_hbm, rows_ref),
                (edges_hbm, edges),
                (prior_hbm, prior_in),
                (ko_hbm, k_ref.at[:own]),
                (vo_hbm, v_ref.at[:own]),
                (kh_hbm, k_ref.at[own:]),
                (vh_hbm, v_ref.at[own:]),
            )
        )
    ]
    copies[4].start()
    for i, copy in enumerate(copies):
        if i != 4:
            copy.start()

    lane = lax.broadcasted_iota(jnp.int32, (TILE, WIDE), 1)
    first = lane < TILE
    wbd[...] = jnp.zeros_like(wbd)
    denom[...] = jnp.zeros_like(denom)
    delta[...] = jnp.zeros_like(delta)
    dprior[...] = jnp.zeros_like(dprior)
    dkv[...] = jnp.zeros_like(dkv)
    dwk[...] = jnp.zeros_like(dwk)
    dwv[...] = jnp.zeros_like(dwv)
    dq[...] = jnp.zeros_like(dq)
    copies[4].wait()
    for i in range(listed.shape[0]):
        listed[i] = 0
    targets = [edges[0, e] for e in range(count)]
    sizes = [sum((target == a).astype(jnp.int32) for target in targets) for a in range(dests)]
    starts = [jnp.int32(0)]
    for a in range(dests):
        starts.append(starts[a] + (sizes[a] + GROUP - 1) // GROUP * GROUP)
    heads = list(starts[:dests])
    for e, target in enumerate(targets):
        at = jnp.int32(places)
        for a in range(dests):
            at = jnp.where(target == a, heads[a], at)
            heads[a] = heads[a] + (target == a).astype(jnp.int32)
        listed[at] = 256 + 16 * edges[1, e] + edges[2, e]
    used = starts[dests] // GROUP

    copies[1].wait()
    copies[2].wait()
    none = jnp.zeros((TILE, WIDE), BF16)
    for a in range(dests):
        q = q_ref[a * TILE : (a + 1) * TILE, :].astype(F32) * 0.125
        g = g_ref[a * TILE : (a + 1) * TILE, :].astype(F32)
        for h in range(2):
            mine = first if h == 0 else jnp.logical_not(first)
            qg[a, h * TILE : (h + 1) * TILE, :WIDE] = jnp.where(mine, q, 0.0).astype(BF16)
            qg[a, h * TILE : (h + 1) * TILE, WIDE:] = none
            qg[a, (2 + h) * TILE : (3 + h) * TILE, :WIDE] = none
            qg[a, (2 + h) * TILE : (3 + h) * TILE, WIDE:] = jnp.where(mine, g, 0.0).astype(BF16)
    copies[3].wait()
    for b in range(own_tiles):
        keep[b] = jnp.ones((TILE, WIDE), F32)
    period = lax.broadcasted_iota(jnp.int32, (16, 8, WIDE), 2) % 8
    slot = lax.broadcasted_iota(jnp.int32, (16, 8, WIDE), 1)
    for j in range(halo_tiles // 2):
        ids = column(rows_ref[j : j + 1, :].astype(F32))
        ok = (ids < float(own)).astype(F32)
        keep[own_tiles + 2 * j] = ok[:TILE]
        keep[own_tiles + 2 * j + 1] = ok[TILE:]
        tiled = jnp.sum(jnp.where(period == slot, ids.reshape(16, 8, WIDE), 0.0), axis=1)
        ids_ref[16 * j : 16 * j + 16, :] = tiled
    copies[5].wait()
    one_lane = lax.broadcasted_iota(jnp.int32, (1, WIDE), 1)
    for r in range(RELS):
        prior[r : r + 1, :] = jnp.where(one_lane < TILE, prior_in[0, r], prior_in[1, r])
    copies[0].wait()
    for r in range(RELS):
        for w in range(2):
            for h in range(2):
                at = (2 * w + h) * TILE
                wbd[r, at : at + TILE, at : at + TILE] = rel_ref[w, r, h]
    for copy in copies[6:]:
        copy.wait()

    def entry(i):
        code = listed[i]
        return (code >> 4) & 15, code & 15, (code >= 256).astype(F32)

    def rows(b):
        return pl.ds(pl.multiple_of(b * TILE, TILE), TILE)

    def tile_of(group):
        at = group * GROUP
        return sum((at >= starts[a]).astype(jnp.int32) for a in range(1, dests))

    def scores(group):
        i = group * GROUP
        a = tile_of(group)
        parts = []
        for u in range(GROUP):
            b, r, live = entry(i + u)
            pair = jnp.concatenate([k_ref[rows(b), :], v_ref[rows(b), :]], axis=1)
            parts.append(mul(pair, wbd[r], NN).astype(BF16))
        mixed = jnp.concatenate(parts, axis=0)
        kvm[pl.ds(i, GROUP)] = mixed[:, :WIDE].reshape(GROUP, TILE, WIDE)
        both = mul(mixed, qg[a], NT)
        logs[pl.ds(i, GROUP)] = both[:, :WIDE].reshape(GROUP, TILE, WIDE)
        grads[pl.ds(i, GROUP)] = both[:, WIDE:].reshape(GROUP, TILE, WIDE)
        total = None
        for u in range(GROUP):
            b, r, live = entry(i + u)
            ex = jnp.exp(prior[pl.ds(r, 1), :] * both[u * TILE : (u + 1) * TILE, :WIDE])
            ex = jnp.where(keep[b] * live > 0.0, ex, 0.0)
            exps[i + u] = ex
            total = ex if total is None else total + ex
        denom[a] += jnp.sum(total, axis=0, keepdims=True)

    def normalise(group):
        i = group * GROUP
        a = tile_of(group)
        total = None
        for u in range(GROUP):
            soft = exps[i + u] * shrink[a] * denom[a]
            exps[i + u] = soft
            prob = soft.astype(BF16)
            probs[i + u] = prob
            term = prob.astype(F32) * grads[i + u]
            total = term if total is None else total + term
        delta[a] += jnp.sum(total, axis=0, keepdims=True)

    def backward(group):
        i = group * GROUP
        a = tile_of(group)
        parts = []
        for u in range(GROUP):
            b, r, live = entry(i + u)
            score_grad = exps[i + u] * (grads[i + u] - delta[a])
            dprior[pl.ds(r, 1), :] += jnp.sum(score_grad * logs[i + u], axis=0, keepdims=True)
            parts.append((score_grad * prior[pl.ds(r, 1), :]).astype(BF16))
        lgrad = jnp.concatenate(parts, axis=0)
        pair = jnp.concatenate([lgrad, probs[pl.ds(i, GROUP)].reshape(GROUP * TILE, WIDE)], axis=1)
        mixed_grad = mul(pair, qg[a], NN).astype(BF16)
        dq[a] += mul(lgrad, kvm[pl.ds(i, GROUP)].reshape(GROUP * TILE, WIDE), TN)
        for u in range(GROUP):
            b, r, live = entry(i + u)
            part = mixed_grad[u * TILE : (u + 1) * TILE]
            dkv[b] += mul(part, wbd[r], NT)
            dwk[r] += mul(k_ref[rows(b), :], part[:, :WIDE], TN)
            dwv[r] += mul(v_ref[rows(b), :], part[:, WIDE:], TN)

    def sweep(work):
        def some(step, carry):
            for u in range(UNROLL):
                work(step * UNROLL + u)
            return carry

        lax.fori_loop(0, (used + UNROLL - 1) // UNROLL, some, 0)

    sweep(scores)
    shrink[...] = jnp.where(denom[...] > 1e18, 2.0**-64, 1.0)
    denom[...] = 1.0 / (denom[...] * shrink[...])
    sweep(normalise)
    sweep(backward)

    at_own = 2 * (dests * REL_BLOCK)
    for a in range(dests):
        grad = jnp.where(first, dq[a, :TILE, :], dq[a, TILE:, :]) * 0.125
        at = at_own + a * TILE
        pack_out[at : at + TILE, :] = grad.astype(BF16)
    for b in range(own_tiles):
        for w in range(2):
            at = at_own + (1 + w) * own + b * TILE
            pack_out[at : at + TILE, :] = dkv[b, :, w * WIDE : (w + 1) * WIDE].astype(BF16)
    for w, ref in enumerate((dwk, dwv)):
        for r in range(RELS):
            at = (w * RELS + r) * TILE
            drel[at : at + TILE, :] = jnp.where(first, ref[r, :TILE, :], ref[r, TILE:, :])
    sums = dprior[...]
    spot = lax.broadcasted_iota(jnp.int32, sums.shape, 1)
    row = lax.broadcasted_iota(jnp.int32, sums.shape, 0)
    one = jnp.sum(jnp.where(spot < TILE, sums, 0.0), axis=1, keepdims=True)
    two = jnp.sum(jnp.where(spot < TILE, 0.0, sums), axis=1, keepdims=True)
    chosen = jnp.where((spot // 16) % 2 == 0, one, two)
    line = jnp.sum(jnp.where(spot % 16 == row, chosen, 0.0), axis=0, keepdims=True)
    high = line.astype(BF16).astype(F32)
    line = jnp.where(one_lane < 32, high, line - high)
    tail = jnp.where(lax.broadcasted_iota(jnp.int32, (16, WIDE), 0) == 0, line, 0.0).astype(BF16)
    for w in range(2):
        for y in range(dests):
            at = (w * dests + y) * REL_ROWS
            to = (w * dests + y) * REL_BLOCK
            pack_out[to : to + REL_ROWS, :] = drel[at : at + REL_ROWS, :].astype(BF16)
            pack_out[to + REL_ROWS : to + REL_BLOCK, :] = tail
    pack_copy = pltpu.make_async_copy(pack_out, pack_hbm, out_sems.at[0])
    pack_copy.start()
    for b in range(halo_tiles):
        back = dkv[own_tiles + b]
        block = jnp.concatenate(
            [
                back[:, :WIDE].reshape(8, 8, WIDE),
                back[:, WIDE:].reshape(8, 8, WIDE),
                jnp.broadcast_to(ids_ref[8 * b : 8 * b + 8, :].reshape(8, 1, WIDE), (8, 8, WIDE)),
            ],
            axis=1,
        )
        send_out[8 * b : 8 * b + 8] = block.astype(BF16)
    send_copy = pltpu.make_async_copy(send_out, send_hbm, out_sems.at[1])
    send_copy.start()
    pack_copy.wait()
    send_copy.wait()


def attend(edges, rel_prior, queries, grad_output, key_rows, value_rows, halo_keys, halo_values, rel_weight, halo_rows):
    rows = queries.shape[0]
    halo = halo_keys.shape[0]
    dests = rows // TILE
    sources = (rows + halo) // TILE
    count = edges.shape[1]
    groups = -(-(count // GROUP + dests - 1) // UNROLL) * UNROLL
    places = groups * GROUP
    slabs = 64
    return pl.pallas_call(
        attend_kernel,
        out_shape=(
            jax.ShapeDtypeStruct((2 * dests * REL_BLOCK + 3 * rows, WIDE), BF16),
            jax.ShapeDtypeStruct((slabs, BLOCK, WIDE), BF16),
        ),
        in_specs=[HBM] * 10,
        out_specs=(HBM,) * 2,
        scratch_shapes=[
            pltpu.VMEM((2 * dests * REL_BLOCK + 3 * rows, WIDE), BF16),
            pltpu.VMEM((slabs, BLOCK, WIDE), BF16),
            pltpu.SemaphoreType.DMA((2,)),
            pltpu.SMEM(edges.shape, jnp.int32),
            pltpu.SMEM((places + 1,), jnp.int32),
            pltpu.SMEM(rel_prior.shape, F32),
            pltpu.VMEM(queries.shape, BF16),
            pltpu.VMEM(grad_output.shape, BF16),
            pltpu.VMEM(rel_weight.shape, BF16),
            pltpu.VMEM(halo_rows.shape, jnp.int32),
            pltpu.VMEM((rows + halo, WIDE), BF16),
            pltpu.VMEM((rows + halo, WIDE), BF16),
            pltpu.SemaphoreType.DMA((10,)),
            pltpu.VMEM((RELS, 2 * WIDE, 2 * WIDE), BF16),
            pltpu.VMEM((dests, 2 * WIDE, 2 * WIDE), BF16),
            pltpu.VMEM((sources, TILE, WIDE), F32),
            pltpu.VMEM((16, WIDE), F32),
            pltpu.VMEM((places, TILE, WIDE), BF16),
            pltpu.VMEM((places, TILE, WIDE), BF16),
            pltpu.VMEM((places, TILE, WIDE), F32),
            pltpu.VMEM((places, TILE, WIDE), F32),
            pltpu.VMEM((places, TILE, WIDE), F32),
            pltpu.VMEM((dests, 1, WIDE), F32),
            pltpu.VMEM((dests, 1, WIDE), F32),
            pltpu.VMEM((dests, 1, WIDE), F32),
            pltpu.VMEM((16, WIDE), F32),
            pltpu.VMEM((sources, TILE, 2 * WIDE), F32),
            pltpu.VMEM((RELS, WIDE, WIDE), F32),
            pltpu.VMEM((RELS, WIDE, WIDE), F32),
            pltpu.VMEM((dests, WIDE, WIDE), F32),
            pltpu.VMEM((2 * RELS * TILE, WIDE), F32),
            pltpu.VMEM((slabs, WIDE), F32),
        ],
        compiler_params=pltpu.CompilerParams(vmem_limit_bytes=MOST),
        cost_estimate=pl.CostEstimate(flops=3 * 10**9, bytes_accessed=4 * 10**6, transcendentals=400000),
        name="attend",
    )(edges, rel_prior, queries, grad_output, key_rows, value_rows, halo_keys, halo_values, rel_weight, halo_rows)


def bundle_kernel(place, pack_ref, nf_ref, types_ref, mine_out, send_out, own_out, keep_out, rel_out):
    half = rel_out.shape[0]
    for out, core in ((rel_out, 1 - place[0]), (keep_out, place[0])):
        out[...] = pack_ref[pl.ds(pl.multiple_of(core * half, half), half), :]
    rows, feats = nf_ref.shape
    turned = jnp.transpose(nf_ref[...], (1, 0)).astype(F32).reshape(feats // 16, 2, 8, rows)
    low = turned[:, 0].reshape(feats // 2, rows)
    high = turned[:, 1].reshape(feats // 2, rows)
    even = place[0] == 0
    mine_out[...] = jnp.where(even, low, high).astype(BF16)
    send_out[:, :rows] = jnp.where(even, high, low).astype(BF16)
    for j in range(rows // WIDE):
        kinds = column(types_ref[j : j + 1, :].astype(F32)).astype(BF16)
        send_out[j * WIDE : (j + 1) * WIDE, rows + WIDE :] = kinds
    send_out[:, rows : rows + WIDE] = pack_ref[2 * half : 2 * half + rows, :]
    for w in range(2):
        at = 2 * half + (1 + w) * rows
        own_out[:, w * WIDE : (w + 1) * WIDE] = pack_ref[at : at + rows, :]


def bundle(place, pack, node_feats, node_types):
    rows, feats = node_feats.shape
    half = (pack.shape[0] - 3 * rows) // 2
    return pl.pallas_call(
        bundle_kernel,
        out_shape=(
            jax.ShapeDtypeStruct((feats // 2, rows), BF16),
            jax.ShapeDtypeStruct((feats // 2, rows + 2 * WIDE), BF16),
            jax.ShapeDtypeStruct((rows, 2 * WIDE), BF16),
            jax.ShapeDtypeStruct((half, WIDE), BF16),
            jax.ShapeDtypeStruct((half, WIDE), BF16),
        ),
        in_specs=[SMEM] + [VMEM] * 3,
        out_specs=(VMEM,) * 5,
        compiler_params=pltpu.CompilerParams(vmem_limit_bytes=LIMIT),
        cost_estimate=pl.CostEstimate(flops=10**6, bytes_accessed=2 * 10**6, transcendentals=0),
        name="bundle",
    )(place, pack, node_feats, node_types)


def spread(place, products, outs):
    size = outs[0].shape[0]
    for d in range(len(outs)):
        block = lax.rem(place[1] + d, len(outs))
        outs[d][:, : products.shape[1]] = products[pl.ds(pl.multiple_of(block * size, size), size), :]


def project_queries_kernel(place, mine_ref, sent_ref, got_ref, rel_ref, rel_got_ref, pair_out, *refs):
    outs, products = refs[:-1], refs[-1]
    rows = mine_ref.shape[1]
    pair_out[:, :rows] = mine_ref[...]
    pair_out[:, rows:] = got_ref[:, :rows]
    query = jnp.concatenate([ref[:, rows : rows + WIDE] for ref in (sent_ref, got_ref)], axis=0).astype(F32)
    kinds = jnp.concatenate([ref[:, rows + WIDE :] for ref in (sent_ref, got_ref)], axis=0).astype(F32)
    for t in range(EARLY):
        masked = jnp.where(kinds == float(t), query, 0.0).astype(BF16)
        products[:, t * WIDE : (t + 1) * WIDE] = mul(pair_out[...], masked, NN).astype(BF16)
    spread(place, products, outs)
    for d in range(len(outs)):
        block = lax.rem(place[1] + d, len(outs))
        here = pl.ds(pl.multiple_of(block * REL_BLOCK, REL_BLOCK), REL_BLOCK)
        both = with_line(rel_ref[here, :].astype(F32) + rel_got_ref[here, :].astype(F32)).astype(BF16)
        for k in range(REL_BLOCK // TILE):
            at = (EARLY + k) * WIDE
            outs[d][:, at : at + WIDE] = both[k * TILE : (k + 1) * TILE, :]


def project_queries(place, mine, sent, got, rel, rel_got, count):
    feats, rows = mine.shape
    wide = EARLY * WIDE
    more = REL_BLOCK // TILE * WIDE
    return pl.pallas_call(
        project_queries_kernel,
        out_shape=(jax.ShapeDtypeStruct((feats, 2 * rows), BF16),)
        + (jax.ShapeDtypeStruct((feats // count, wide + more), BF16),) * count,
        in_specs=[SMEM] + [VMEM] * 5,
        out_specs=(VMEM,) * (1 + count),
        scratch_shapes=[pltpu.VMEM((feats, wide), BF16)],
        compiler_params=pltpu.CompilerParams(vmem_limit_bytes=LIMIT),
        cost_estimate=pl.CostEstimate(flops=10**9, bytes_accessed=2 * 10**6, transcendentals=0),
        name="project_queries",
    )(place, mine, sent, got, rel, rel_got)


def collect_kernel(own_ref, inc_ref, kv_out):
    rows = own_ref.shape[0]
    slabs = inc_ref.shape[0]
    row = lax.broadcasted_iota(jnp.int32, (16, WIDE), 0)
    block = lax.broadcasted_iota(jnp.int32, (16, WIDE), 1) // 8
    node = lax.broadcasted_iota(jnp.int32, (rows, WIDE), 0).astype(F32)
    back = own_ref[...].astype(F32)
    for c in range(slabs // 16):
        grads = inc_ref[16 * c : 16 * c + 16].astype(F32)
        ids = grads[:, 16, :]
        line = jnp.sum(jnp.where(row == block, ids, 0.0), axis=0, keepdims=True)
        pick = (node == line).astype(F32).astype(BF16)
        both = jnp.concatenate(
            [grads[:, :8].reshape(WIDE, WIDE), grads[:, 8:16].reshape(WIDE, WIDE)], axis=1
        )
        back = back + mul(pick, both.astype(BF16), NN)
    kv_out[...] = back.astype(BF16)


def collect(own, incoming):
    rows = own.shape[0]
    return pl.pallas_call(
        collect_kernel,
        out_shape=jax.ShapeDtypeStruct((rows, 2 * WIDE), BF16),
        in_specs=[VMEM, VMEM],
        out_specs=VMEM,
        compiler_params=pltpu.CompilerParams(vmem_limit_bytes=LIMIT),
        cost_estimate=pl.CostEstimate(flops=10**8, bytes_accessed=10**6, transcendentals=0),
        name="collect",
    )(own, incoming)


def relation_places_kernel(*refs):
    out = refs[-1]
    parts = []
    for k in range(REL_BLOCK // TILE):
        at = (EARLY + k) * WIDE
        total = refs[0][:, at : at + WIDE].astype(F32)
        for ref in refs[1:-1]:
            total = total + ref[:, at : at + WIDE].astype(F32)
        parts.append(total)
    total = with_line(jnp.concatenate(parts, axis=0)).astype(BF16)
    for z in range(out.shape[0]):
        out[z] = total


def relation_places(arrived, count):
    return pl.pallas_call(
        relation_places_kernel,
        out_shape=jax.ShapeDtypeStruct((count, REL_BLOCK, WIDE), BF16),
        in_specs=[VMEM] * len(arrived),
        out_specs=VMEM,
        compiler_params=pltpu.CompilerParams(vmem_limit_bytes=LIMIT),
        cost_estimate=pl.CostEstimate(flops=10**6, bytes_accessed=10**6, transcendentals=0),
        name="relation_places",
    )(*arrived)


def relation_sum_kernel(inc_ref, rel_out, prior_out):
    total = inc_ref[0].astype(F32)
    for s in range(1, inc_ref.shape[0]):
        total = total + inc_ref[s].astype(F32)
    rel_out[...] = total.astype(BF16)
    line = total[REL_ROWS : REL_ROWS + 1, :]
    line = line + pltpu.roll(line, WIDE - 32, 1)
    prior_out[0:1, :] = line[:, :RELS]
    prior_out[1:2, :] = pltpu.roll(line, WIDE - 16, 1)[:, :RELS]


def relation_sum(incoming):
    return pl.pallas_call(
        relation_sum_kernel,
        out_shape=(
            jax.ShapeDtypeStruct(incoming.shape[1:], BF16),
            jax.ShapeDtypeStruct((2, RELS), F32),
        ),
        in_specs=[VMEM],
        out_specs=(VMEM,) * 2,
        compiler_params=pltpu.CompilerParams(vmem_limit_bytes=LIMIT),
        cost_estimate=pl.CostEstimate(flops=10**6, bytes_accessed=10**6, transcendentals=0),
        name="relation_sum",
    )(incoming)


def project_kernel(place, pair_ref, kv_ref, got_kv_ref, sent_ref, got_ref, *refs):
    outs, products = refs[:-1], refs[-1]
    rows = kv_ref.shape[0]
    kinds = jnp.concatenate([ref[:, rows + WIDE :] for ref in (sent_ref, got_ref)], axis=0).astype(F32)
    for p in range(3):
        pair = (sent_ref, got_ref) if p == 0 else (kv_ref, got_kv_ref)
        column_at = rows if p == 0 else (p - 1) * WIDE
        part = jnp.concatenate([ref[:, column_at : column_at + WIDE] for ref in pair], axis=0).astype(F32)
        for t in range(EARLY if p == 0 else 0, TYPES):
            at = (p * TYPES + t - EARLY) * WIDE
            masked = jnp.where(kinds == float(t), part, 0.0).astype(BF16)
            products[:, at : at + WIDE] = mul(pair_ref[...], masked, NN).astype(BF16)
    spread(place, products, outs)


def project(place, pair, kv, got_kv, sent, got, count):
    feats = pair.shape[0]
    wide = (PROJ - EARLY) * WIDE
    return pl.pallas_call(
        project_kernel,
        out_shape=(jax.ShapeDtypeStruct((feats // count, wide), BF16),) * count,
        in_specs=[SMEM] + [VMEM] * 5,
        out_specs=(VMEM,) * count,
        scratch_shapes=[pltpu.VMEM((feats, wide), BF16)],
        compiler_params=pltpu.CompilerParams(vmem_limit_bytes=LIMIT),
        cost_estimate=pl.CostEstimate(flops=10**9, bytes_accessed=4 * 10**6, transcendentals=0),
        name="project",
    )(place, pair, kv, got_kv, sent, got)


def features_kernel(place, sent_ref, kv_ref, w_ref, *refs):
    outs, total = refs[:-1], refs[-1]
    rows = kv_ref.shape[0]
    kinds = sent_ref[:, rows + WIDE :].astype(F32)
    acc = None
    for p in range(3):
        part = sent_ref[:, rows : rows + WIDE] if p == 0 else kv_ref[:, (p - 1) * WIDE : p * WIDE]
        part = part.astype(F32)
        for t in range(TYPES):
            masked = jnp.where(kinds == float(t), part, 0.0).astype(BF16)
            term = mul(masked, w_ref[p * TYPES + t], NT)
            acc = term if acc is None else acc + term
    for h in range(len(outs)):
        total[h] = acc[:, h * WIDE : (h + 1) * WIDE]
    me = place[2]
    first = me + 1 - 2 * lax.rem(me, 2)
    for out, owner in zip(outs, (me, 3 - me, first, 3 - first)):
        out[...] = total[owner].astype(BF16)


def features(place, sent, kv, weights):
    rows = kv.shape[0]
    count = weights.shape[1] // WIDE
    return pl.pallas_call(
        features_kernel,
        out_shape=(jax.ShapeDtypeStruct((rows, WIDE), BF16),) * count,
        in_specs=[SMEM, VMEM, VMEM, VMEM],
        out_specs=(VMEM,) * count,
        scratch_shapes=[pltpu.VMEM((count, rows, WIDE), F32)],
        compiler_params=pltpu.CompilerParams(vmem_limit_bytes=LIMIT),
        cost_estimate=pl.CostEstimate(flops=10**9, bytes_accessed=3 * 10**6, transcendentals=0),
        name="features",
    )(place, sent, kv, weights)


def relation_kernel(place, near_ref, far_ref, c_near_ref, c_far_ref, out_ref, flat):
    y = place[1]
    far = 3 - y
    owners = (y, y + 1 - 2 * lax.rem(y, 2), far, far + 1 - 2 * lax.rem(far, 2))
    for core, refs in ((place[0], (near_ref, far_ref)), (1 - place[0], (c_near_ref, c_far_ref))):
        for n, owner in enumerate(owners):
            at = pl.multiple_of((core * len(owners) + owner) * REL_ROWS, 16)
            flat[pl.ds(at, REL_ROWS), :] = refs[n // 2][n % 2, :REL_ROWS, :].astype(F32)
    for w in range(2):
        for r in range(RELS):
            at = (w * RELS + r) * TILE
            for h in range(2):
                out_ref[w, r, h] = flat[at : at + TILE, h * TILE : (h + 1) * TILE]


def relations(place, *blocks):
    return pl.pallas_call(
        relation_kernel,
        out_shape=jax.ShapeDtypeStruct((2, RELS, 2, TILE, TILE), F32),
        in_specs=[SMEM] + [VMEM] * 4,
        out_specs=VMEM,
        scratch_shapes=[pltpu.VMEM((2 * RELS * TILE, WIDE), F32)],
        compiler_params=pltpu.CompilerParams(vmem_limit_bytes=LIMIT),
        cost_estimate=pl.CostEstimate(flops=10**6, bytes_accessed=3 * 10**6, transcendentals=0),
        name="relations",
    )(place, *blocks)


def place_sum_kernel(*refs):
    out = refs[-1]
    half = (len(refs) - 1) // 2
    narrow = EARLY * WIDE
    for at, group in ((0, refs[:half]), (narrow, refs[half:-1])):
        width = narrow if at == 0 else group[0].shape[1]
        total = group[0][:, :width].astype(F32)
        for ref in group[1:]:
            total = total + ref[:, :width].astype(F32)
        out[:, at : at + width] = total.astype(BF16)


def place_sum(query, rest):
    rows = query[0].shape[0]
    return pl.pallas_call(
        place_sum_kernel,
        out_shape=jax.ShapeDtypeStruct((rows, PROJ * WIDE), BF16),
        in_specs=[VMEM] * (len(query) + len(rest)),
        out_specs=VMEM,
        compiler_params=pltpu.CompilerParams(vmem_limit_bytes=LIMIT),
        cost_estimate=pl.CostEstimate(flops=10**6, bytes_accessed=10**6, transcendentals=0),
        name="place_sum",
    )(*query, *rest)


def shifted(blocks, axis):
    count = len(blocks)
    return [blocks[0]] + [
        lax.ppermute(blocks[d], axis, [(i, (i + d) % count) for i in range(count)])
        for d in range(1, count)
    ]


def per_device(
    node_feats,
    node_types,
    queries,
    key_rows,
    value_rows,
    halo_keys,
    halo_values,
    halo_rows,
    edge_tiles,
    grad_output,
    proj_weight,
    rel_weight,
    rel_prior,
):
    y_count = lax.axis_size("y")
    z_count = lax.axis_size("z")
    place = jnp.stack(
        [lax.axis_index("core"), lax.axis_index("y"), lax.axis_index("heads")]
    ).astype(jnp.int32)
    swap = [(0, 1), (1, 0)]
    pack, send = attend(
        edge_tiles.T,
        rel_prior.T,
        queries,
        grad_output,
        key_rows,
        value_rows,
        halo_keys,
        halo_values,
        rel_weight,
        halo_rows.reshape(-1, WIDE),
    )
    incoming = lax.all_to_all(send, ("y", "z", "core"), 0, 0, tiled=True)
    feats_t, sent, own, rel, rel_theirs = bundle(place, pack, node_feats, node_types.reshape(-1, WIDE))
    got = lax.ppermute(sent, "core", swap)
    rel_got = lax.ppermute(rel_theirs, "core", swap)
    pair, *q_blocks = project_queries(place, feats_t, sent, got, rel, rel_got, y_count)
    q_arrived = shifted(q_blocks, "y")
    own, *q_blocks = lax.optimization_barrier((own, *q_blocks))
    kv = collect(own, incoming)
    got_kv = lax.ppermute(kv, "core", swap)
    got_kv, *q_arrived = lax.optimization_barrier((got_kv, *q_arrived))
    rel_z = lax.all_to_all(relation_places(q_arrived, z_count), "z", 0, 0, tiled=True)
    arrived = shifted(project(place, pair, kv, got_kv, sent, got, y_count), "y")
    feat_blocks = features(place, sent, kv, proj_weight.reshape(PROJ, -1, WIDE))
    mine, partners, *away = feat_blocks
    away = [lax.ppermute(block, "heads", [(0, 1), (1, 0), (2, 3), (3, 2)]) for block in away]
    arrived[0], got_mine, got_partners = lax.optimization_barrier((arrived[0], *away))
    partners = partners.astype(F32) + got_partners.astype(F32)
    last = lax.ppermute(partners.astype(BF16), "heads", [(0, 3), (3, 0), (1, 2), (2, 1)])
    grad_feats = (mine.astype(F32) + got_mine.astype(F32) + last.astype(F32)).astype(BF16)
    by_y = place_sum(q_arrived, arrived)
    next_y = [(0, 1), (1, 0), (2, 3), (3, 2)]
    last_y = [(0, 3), (3, 0), (1, 2), (2, 1)]
    rel_z, by_y = lax.optimization_barrier((rel_z, by_y))
    by_z = lax.all_to_all(by_y.reshape(z_count, -1, PROJ * WIDE), "z", 0, 0, tiled=True)
    rel_mine, prior = relation_sum(rel_z)
    rel_first = lax.ppermute(rel_mine, "y", next_y)
    rel_near = jnp.stack([rel_mine, rel_first])
    rel_far = lax.ppermute(rel_near, "y", last_y)
    blocks = (rel_near, rel_far)
    grad_rel = relations(place, *blocks, *(lax.ppermute(block, "core", swap) for block in blocks))
    by_z, grad_rel, grad_feats = lax.optimization_barrier((by_z, grad_rel, grad_feats))
    grad_proj = jnp.sum(by_z.astype(F32), axis=0).reshape(-1, 3, TYPES, WIDE)
    grad_prior = prior.T
    return (grad_feats, grad_proj, grad_rel, grad_prior)


def solution(mesh):
    heads = mesh.devices.shape[1]
    split = Mesh(mesh.devices.reshape(4, 8, 2, heads), ("y", "z", "core", "heads"))
    nodes = ("y", "z", "core")
    return jax.shard_map(
        per_device,
        mesh=split,
        in_specs=(
            P(nodes, None),
            P(nodes),
            P(nodes, "heads"),
            P(nodes, "heads"),
            P(nodes, "heads"),
            P(nodes, "heads"),
            P(nodes, "heads"),
            P(nodes),
            P(nodes, None),
            P(nodes, "heads"),
            P(None, None, None, "heads"),
            P(None, None, "heads", None, None),
            P(None, "heads"),
        ),
        out_specs=(
            P(nodes, "heads"),
            P(nodes, None, None, "heads"),
            P(None, None, "heads", None, None),
            P(None, "heads"),
        ),
        check_vma=False,
    )
```
